256 devices in a mesh: dst: 32 (over y, x, core), src: 8 (over z).
Axes of the slice: x: 4, y: 4, z: 8, core: 2. Of those that a mesh axis runs over, the one named last changes fastest.
Arguments:
- inputs: float32 [32768, 256], P(('dst', 'src')), may hold values from -64 to 64
- projection: float32 [256, 512], replicated, may hold values from -0.375 to 0.375
- att_src: float32 [8, 64], replicated, may hold values from -0.75 to 0.75
- att_dst: float32 [8, 64], replicated, may hold values from -0.75 to 0.75
- blocks: int32 [32, 8, 32, 2], P('dst', 'src'), may hold values from 0 to 31, as said below
- counts: int32 [32, 8], P('dst', 'src'), may hold values from 16 to 32, as said below
- tile_masks: int32 [32, 8, 32, 128, 128], P('dst', 'src'), may hold values 0 or 1
- cotangent: float32 [32768, 512], P(('dst', 'src')), may hold values from -6 to 6
Outputs:
- output: float32 [32768, 512], P(('dst', 'src'))
- in_grad: float32 [32768, 256], P(('dst', 'src'))
- proj_grad: float32 [256, 512], replicated
- att_src_grad: float32 [8, 64], replicated
- att_dst_grad: float32 [8, 64], replicated
The draws below stay inside these ranges and needn't reach their ends.
Inputs may be any that keep to these rules, and one draw needn't show every extreme that they name: blocks[i, j, k] = (b, c) with b below 8 and c below 32; the slots of one device name distinct blocks. Only the first counts[i, j] slots of device (i, j) hold edges; some device uses all 32.
All inputs are finite; a program needn't handle non-finite values. No bound on the sum of `tile_masks` on one device may be relied on, other than what follows from the above.
Results may differ from the reference program's by a relative error of at most 0.0029.
Values sent between devices are 32-bit elements; how exact they have to be, the bound alone decides.
A program may use at most 128 MiB of HBM per device.

```python
import jax
import jax.numpy as jnp
from jax import lax

FEAT = 256
HEADS = 8
HEAD_DIM = 64
TILE = 128
ROWS_DEV = 128
SLOTS = 32
OUT_WIDTH = 512
NODES = 32768
DST_ROWS = 1024
SRC_ROWS = 4096
DST_BLOCKS = 8
SRC_BLOCKS = 32
N_DST = 32
N_SRC = 8


def draw_inputs(key, part):
    key = jax.random.fold_in(key, 7)
    base = jax.random.normal(jax.random.fold_in(key, 1), (NODES, FEAT), jnp.float32)
    return jnp.clip(base, -6.0, 6.0)


def draw_blocks(key, part):
    key = jax.random.fold_in(key, 11)
    keys = jax.random.split(key, N_DST * N_SRC)
    chosen = jax.vmap(lambda one_key: jax.random.permutation(one_key, DST_BLOCKS * SRC_BLOCKS)[:SLOTS])(keys)
    coords = jnp.stack([chosen // SRC_BLOCKS, chosen % SRC_BLOCKS], axis=-1)
    return coords.reshape(N_DST, N_SRC, SLOTS, 2).astype(jnp.int32)


def draw_counts(key, part):
    key = jax.random.fold_in(key, 12)
    values = jax.random.randint(jax.random.fold_in(key, 1), (N_DST * N_SRC,), max(1, SLOTS // 2), SLOTS + 1)
    fullest = jax.random.randint(jax.random.fold_in(key, 2), (), 0, N_DST * N_SRC)
    values = values.at[fullest].set(SLOTS)
    return values.reshape(N_DST, N_SRC).astype(jnp.int32)


def touch_ends(values, own_key, low, high):
    extent = values.shape
    spot = [jax.random.randint(jax.random.fold_in(own_key, axis), (), 0, extent[axis]) for axis in range(len(extent))]
    values = values.at[tuple(spot)].set(low)
    longest = extent.index(max(extent))
    spot[longest] = (spot[longest] + 1) % extent[longest]
    return values.at[tuple(spot)].set(high)


def block_levels(rng, dims, cuts, smallest, largest):
    factor_of, own = 1.0, jax.random.fold_in(rng, 6)
    for position, shards_of in cuts:
        steps = jnp.exp(jax.random.uniform(jax.random.fold_in(own, position), (shards_of,), jnp.float32, smallest / len(cuts), largest / len(cuts)))
        factor_of = factor_of * jnp.repeat(steps, dims[position] // shards_of).reshape([-1 if axis == position else 1 for axis in range(len(dims))])
    return factor_of


def scatter_about(rng, shape, spread, reach, shards=(), kind=jnp.bfloat16):
    result = spread * jax.random.normal(rng, shape, jnp.float32)
    if shards:
        result = result * block_levels(rng, shape, shards, -0.22, 0.18)
    return jnp.clip(result, -reach, reach).astype(kind)


def setup_inputs(seed: int = 0) -> dict:
    streams_of = jax.random.split(jax.random.key(seed), 9)
    inputs = draw_inputs(jax.random.fold_in(streams_of[8], 71), 0)
    projection = scatter_about(streams_of[1], (FEAT, OUT_WIDTH), FEAT ** -0.5, 0.375, (), jnp.float32)
    att_src = scatter_about(streams_of[2], (HEADS, HEAD_DIM), HEAD_DIM ** -0.5, 0.75, (), jnp.float32)
    att_dst = scatter_about(streams_of[3], (HEADS, HEAD_DIM), HEAD_DIM ** -0.5, 0.75, (), jnp.float32)
    blocks = draw_blocks(jax.random.fold_in(streams_of[8], 71), 0)
    counts = draw_counts(jax.random.fold_in(streams_of[8], 71), 0)
    tile_masks = touch_ends((jax.random.randint(streams_of[6], (N_DST, N_SRC, SLOTS, TILE, TILE), 0, 4) < 1).astype(jnp.int32), jax.random.fold_in(streams_of[6], 1), 0, 1)
    cotangent = scatter_about(streams_of[7], (NODES, OUT_WIDTH), 1.0, 6.0, ((0, 256),), jnp.float32)
    return dict(inputs=inputs, projection=projection, att_src=att_src, att_dst=att_dst, blocks=blocks, counts=counts, tile_masks=tile_masks, cotangent=cotangent)


NEG_FILL = -1e+30

def leaky_relu(raw):
    return jnp.where(raw > 0, raw, 0.2 * raw)

def reference(inputs, projection, att_src, att_dst, blocks, counts, tile_masks, cotangent):
    highest = lax.Precision.HIGHEST
    col_ids = jnp.repeat(jnp.arange(N_SRC, dtype=jnp.int32), SLOTS)
    slot_ids = jnp.tile(jnp.arange(SLOTS, dtype=jnp.int32), N_SRC)

    def forward(inputs, projection, att_src, att_dst):
        features = jnp.dot(inputs, projection, precision=highest)
        feat3 = features.reshape(NODES, HEADS, HEAD_DIM)
        dst_score = jnp.einsum('nhc,hc->nh', feat3, att_dst, precision=highest)
        src_score = jnp.einsum('nhc,hc->nh', feat3, att_src, precision=highest)
        panels = features.reshape(N_DST, N_SRC, ROWS_DEV, OUT_WIDTH).transpose(1, 0, 2, 3).reshape(N_SRC, SRC_ROWS, OUT_WIDTH)
        src_panels = src_score.reshape(N_DST, N_SRC, ROWS_DEV, HEADS).transpose(1, 0, 2, 3).reshape(N_SRC, SRC_ROWS, HEADS)
        feat_rows = features.reshape(N_DST, DST_ROWS, OUT_WIDTH)
        dst_rows = dst_score.reshape(N_DST, DST_ROWS, HEADS)
        self_rows = src_score.reshape(N_DST, DST_ROWS, HEADS)

        @jax.checkpoint
        def one_group(group):
            feat_group, dst_group, self_group, block_group, count_group, mask_group = group
            start_carry = (leaky_relu(dst_group + self_group), jnp.ones((DST_ROWS, HEADS), jnp.float32), feat_group)

            @jax.checkpoint
            def step(carry, item):
                row_max, row_sum, row_acc = carry
                column, slot, coord, mask = item
                live = slot < lax.dynamic_index_in_dim(count_group, column, 0, keepdims=False)
                keep = jnp.logical_and(mask > 0, live)[None]
                dst_start = (coord[0] * TILE).astype(jnp.int32)
                src_start = (coord[1] * TILE).astype(jnp.int32)
                panel = lax.dynamic_index_in_dim(panels, column, 0, keepdims=False)
                src_panel = lax.dynamic_index_in_dim(src_panels, column, 0, keepdims=False)
                dst_tile = lax.dynamic_slice_in_dim(dst_group, dst_start, TILE, 0)
                src_tile = lax.dynamic_slice_in_dim(src_panel, src_start, TILE, 0)
                logits = leaky_relu(dst_tile.T[:, :, None] + src_tile.T[:, None, :])
                tile_max = lax.optimization_barrier(jnp.max(jnp.where(keep, logits, NEG_FILL), axis=2)).T
                old_max = lax.dynamic_slice_in_dim(row_max, dst_start, TILE, 0)
                new_max = jnp.maximum(old_max, tile_max)
                weights = jnp.exp(jnp.where(keep, logits - new_max.T[:, :, None], NEG_FILL))
                factor = jnp.exp(old_max - new_max)
                new_sum = lax.dynamic_slice_in_dim(row_sum, dst_start, TILE, 0) * factor + lax.optimization_barrier(jnp.sum(weights, axis=2)).T
                h_src = lax.dynamic_slice_in_dim(panel, src_start, TILE, 0).reshape(TILE, HEADS, HEAD_DIM)
                old_acc = lax.dynamic_slice_in_dim(row_acc, dst_start, TILE, 0).reshape(TILE, HEADS, HEAD_DIM)
                new_acc = old_acc * factor[:, :, None] + jnp.einsum('hds,shc->dhc', weights, h_src, precision=highest)
                row_max = lax.dynamic_update_slice_in_dim(row_max, new_max, dst_start, 0)
                row_sum = lax.dynamic_update_slice_in_dim(row_sum, new_sum, dst_start, 0)
                row_acc = lax.dynamic_update_slice_in_dim(row_acc, new_acc.reshape(TILE, OUT_WIDTH), dst_start, 0)
                return ((row_max, row_sum, row_acc), None)
            items = (col_ids, slot_ids, block_group.reshape(N_SRC * SLOTS, 2), mask_group.reshape(N_SRC * SLOTS, TILE, TILE))
            final, unused = lax.scan(step, start_carry, items)
            row_max, row_sum, row_acc = final
            agg = (row_acc.reshape(DST_ROWS, HEADS, HEAD_DIM) / row_sum[:, :, None]).reshape(DST_ROWS, OUT_WIDTH)
            return jax.nn.elu(agg)
        outs = lax.map(one_group, (feat_rows, dst_rows, self_rows, blocks, counts, tile_masks))
        return outs.reshape(NODES, OUT_WIDTH)
    output, pull = jax.vjp(forward, inputs, projection, att_src, att_dst)
    grads = pull(cotangent)
    return (output, grads[0], grads[1], grads[2], grads[3])
```

```python
import functools

import jax
import jax.numpy as jnp
from jax import lax
from jax.experimental import pallas as pl
from jax.experimental.pallas import tpu as pltpu
from jax.sharding import PartitionSpec as P

HIGHEST = lax.Precision.HIGHEST
F32 = jnp.float32
BF16 = jnp.bfloat16
LOG2E = 1.4426950408889634
NEG = -1e30
MESH = pl.DeviceIdType.MESH
VMEM = pl.BlockSpec(memory_space=pltpu.VMEM)
SMEM = pl.BlockSpec(memory_space=pltpu.SMEM)
ANY = pl.BlockSpec(memory_space=pl.ANY)
NN = (((1,), (0,)), ((), ()))
NT = (((1,), (1,)), ((), ()))
BIG_VMEM = 60 * 1024 * 1024


def dot(a, b, dims=NN, precision=None):
    return lax.dot_general(a, b, dims, precision=precision, preferred_element_type=F32)


def split(value):
    high = value.astype(BF16)
    return high, (value - high.astype(F32)).astype(BF16)


def leaky(raw):
    return jnp.maximum(raw, 0.2 * raw)


def per_head_rows(att):
    wide = jnp.concatenate([att] * 8, axis=1)
    head = lax.broadcasted_iota(jnp.int32, wide.shape, 0)
    column = lax.broadcasted_iota(jnp.int32, wide.shape, 1)
    return jnp.where(column // 64 == head, wide, 0.0)


def score_rows(att, proj):
    return dot(per_head_rows(att), proj, NT, HIGHEST)


def lanes(shape):
    return lax.broadcasted_iota(jnp.int32, shape, len(shape) - 1)


def place():
    d = lax.axis_index("dst")
    z = lax.axis_index("src")
    return d, d // 8, lax.rem(d // 2, 4), lax.rem(d, 2), z


def node(y, x, k):
    return lax.rem(y + 8, 4) * 8 + lax.rem(x + 8, 4) * 2 + k


class Links:
    def __init__(self, send, recv):
        self.send, self.recv, self.used, self.open = send, recv, 0, []

    def push(self, source, landing, **target):
        copy = pltpu.make_async_remote_copy(
            src_ref=source,
            dst_ref=landing,
            send_sem=self.send.at[self.used],
            recv_sem=self.recv.at[self.used],
            device_id=target,
            device_id_type=MESH,
        )
        self.used += 1
        copy.start()
        self.open.append(copy)
        return copy

    def drain(self):
        for copy in self.open:
            copy.wait_send()


def greet(dsts, srcs):
    barrier = pltpu.get_barrier_semaphore()
    for other in dsts:
        pl.semaphore_signal(barrier, inc=1, device_id={"dst": other}, device_id_type=MESH)
    for other in srcs:
        pl.semaphore_signal(barrier, inc=1, device_id={"src": other}, device_id_type=MESH)
    return lambda: pl.semaphore_wait(barrier, len(dsts) + len(srcs))


def run_chains(chains):
    chains = list(chains)
    while chains:
        for chain in list(chains):
            try:
                next(chain)
            except StopIteration:
                chains.remove(chain)


def gather_body(x_ref, p_ref, att_ref, panel_ref, a_ref, send, recv, own_sem):
    d, y, x, k, z = place()
    sibling = node(y, x, 1 - k)
    wait_all = greet(
        [sibling, node(y + 1, x, k), node(y - 1, x, k), node(y, x + 1, k), node(y, x - 1, k)],
        [lax.rem(z + s, 8) for s in range(1, 8)],
    )
    own_copy = pltpu.make_async_copy(x_ref, panel_ref.at[d], own_sem)
    own_copy.start()
    rows = score_rows(att_ref[...], p_ref[...]) * LOG2E
    a_ref[z] = dot(rows, x_ref[...], NT, HIGHEST)
    wait_all()
    links = Links(send, recv)

    def chain(half):
        def at(u, v):
            return node(y + v, x + u, k) if half == 0 else node(y + u, x + v, k)

        def region(u, v, quarter=None):
            if quarter is None:
                return panel_ref.at[at(u, v), pl.ds(64 * half, 64)]
            return panel_ref.at[at(u, v), pl.ds(64 * half + 32 * quarter, 32)]

        def to(part, du, dv, src=None):
            return links.push(part if src is None else src, part, dst=at(du, dv))

        def twin(u, v, src=None):
            part = region(u, v)
            return links.push(part if src is None else src, part, dst=sibling)

        own = x_ref.at[pl.ds(64 * half, 64)]
        first = [to(region(0, 0), 1, 0, own), to(region(0, 0), -1, 0, own)]
        second = {0: [to(region(0, 0), 0, 1, own), to(region(0, 0), 0, -1, own)]}
        twins = [twin(0, 0, own)]
        last = {}

        def spread(u):
            second[u] = [to(region(u, 0), 0, 1), to(region(u, 0), 0, -1)]
            twins.append(twin(u, 0))

        def relay(u):
            pair = []
            for index, v in ((0, -1), (1, 1)):
                yield
                second[u][index].wait_recv()
                pair.append(to(region(u, v, index), 0, -v))
                twins.append(twin(u, v))
            last[u] = pair

        def finish(u):
            yield
            for copy in last[u]:
                copy.wait_recv()
            twins.append(twin(u, 2))

        far = []
        for index, u in ((0, -1), (1, 1)):
            yield
            first[index].wait_recv()
            far.append(to(region(u, 0, index), -u, 0))
            spread(u)
        yield from relay(0)
        yield
        for copy in far:
            copy.wait_recv()
        spread(2)
        yield from relay(-1)
        yield from relay(1)
        yield from finish(0)
        yield from relay(2)
        yield from finish(-1)
        yield from finish(1)
        yield from finish(2)
        yield
        for copy in twins:
            copy.wait_recv()

    scores = [
        links.push(a_ref.at[z], a_ref.at[z], src=lax.rem(z + s, 8)) for s in range(1, 8)
    ]
    run_chains([chain(0), chain(1)])
    for copy in scores:
        copy.wait_recv()
    own_copy.wait()
    links.drain()


def gather_inputs(x, proj, att_dst):
    count = 72 + 7
    return pl.pallas_call(
        gather_body,
        out_shape=(
            jax.ShapeDtypeStruct((32, 128, 256), F32),
            jax.ShapeDtypeStruct((8, 8, 128), F32),
        ),
        in_specs=[VMEM] * 3,
        out_specs=(ANY, VMEM),
        scratch_shapes=[
            pltpu.SemaphoreType.DMA((count,)),
            pltpu.SemaphoreType.DMA((count,)),
            pltpu.SemaphoreType.DMA,
        ],
        compiler_params=pltpu.CompilerParams(collective_id=0, has_side_effects=True),
    )(x, proj, att_dst)


def prepare_features(x_ref, p_ref, p_cat, hb, extra):
    high, low = split(p_ref[...])
    p_cat[0:256] = high
    p_cat[256:512] = low
    p_cat[512:768] = high
    even = (lanes((1, 128)) < 64).astype(BF16)
    odd = (lanes((1, 128)) >= 64).astype(BF16)

    def step(c, carry):
        xc = x_ref[c]
        x_high, x_low = split(xc)
        h = dot(jnp.concatenate([x_high, x_high, x_low], axis=1), p_cat[...])
        h_high, h_low = split(h)
        for pair in range(4):
            cols = slice(128 * pair, 128 * pair + 128)
            hb[c, pair, 0:128] = h_high[:, cols] * even
            hb[c, pair, 128:256] = h_high[:, cols] * odd
            hb[c, pair, 256:384] = h_low[:, cols] * even
            hb[c, pair, 384:512] = h_low[:, cols] * odd
        extra(c, xc)
        return carry

    lax.fori_loop(0, 32, step, 0)


def columns_of(rows):
    pad = jnp.zeros((128 - rows.shape[0], 128), F32)
    return jnp.concatenate([rows, pad], axis=0).T


def forward_body(
    blocks, counts, x_ref, p_ref, att_ref, a_ref, mask_ref, acc_out, b_out, p_cat, hb, top, abc, sums, acc
):
    rows = score_rows(att_ref[...], p_ref[...]) * LOG2E

    def extra(c, xc):
        b_out[c] = dot(rows, xc, NT, HIGHEST)

    prepare_features(x_ref, p_ref, p_cat, hb, extra)
    top[...] = jnp.full(top.shape, NEG, F32)
    sums[...] = jnp.zeros(sums.shape, F32)
    acc[...] = jnp.zeros(acc.shape, F32)
    live = counts[0]

    def find_top(k, carry):
        b, c = blocks[k, 0], blocks[k, 1]
        keep = mask_ref[k] > 0
        scores = b_out[c]
        for h in range(8):
            top[b * 8 + h] = jnp.maximum(top[b * 8 + h], jnp.where(keep, scores[h : h + 1], NEG))
        return carry

    lax.fori_loop(0, live, find_top, 0)

    def spread_top(b, carry):
        a_cols = columns_of(a_ref[b])
        for h in range(8):
            a_col = a_cols[:, h : h + 1]
            best = jnp.max(top[b * 8 + h], axis=1, keepdims=True)
            top[b * 8 + h] = jnp.broadcast_to(leaky(a_col + best), (128, 128))
            abc[b * 8 + h] = jnp.broadcast_to(a_col, (128, 128))
        return carry

    lax.fori_loop(0, 8, spread_top, 0)

    def accumulate(k, carry):
        b, c = blocks[k, 0], blocks[k, 1]
        keep = mask_ref[k] > 0
        scores = b_out[c]
        for pair in range(4):
            highs, lows = [], []
            for h in (2 * pair, 2 * pair + 1):
                raw = abc[b * 8 + h] + jnp.where(keep, scores[h : h + 1], NEG)
                w = jnp.exp2(leaky(raw) - top[b * 8 + h])
                sums[b * 8 + h] += w
                high, low = split(w)
                highs.append(high)
                lows.append(low)
            left = jnp.concatenate(highs + highs + lows, axis=1)
            right = jnp.concatenate([hb[c, pair], hb[c, pair, 0:256]], axis=0)
            acc[b * 4 + pair] += dot(left, right)
        return carry

    lax.fori_loop(0, live, accumulate, 0)

    def pack(b, carry):
        lane = lanes((128, 128))
        stats = [jnp.zeros((128, 128), F32)] * 2
        for h in range(8):
            way, h4 = h // 4, h % 4
            total = jnp.sum(sums[b * 8 + h], axis=1, keepdims=True)
            stats[way] = jnp.where(lane == h4, top[b * 8 + h], stats[way])
            stats[way] = jnp.where(lane == h4 + 4, total, stats[way])
        for way in range(2):
            packed = stats[way].T[0:8]
            for sub in range(2):
                span = slice(64 * sub, 64 * sub + 64)
                acc_out[b, way, sub, 0:64, 0:128] = acc[b * 4 + 2 * way][span]
                acc_out[b, way, sub, 0:64, 128:256] = acc[b * 4 + 2 * way + 1][span]
                acc_out[b, way, sub, 64:72, 0:128] = packed
                acc_out[b, way, sub, 64:72, 128:256] = jnp.zeros((8, 128), F32)
        return carry

    lax.fori_loop(0, 8, pack, 0)


def forward_local(blocks, counts, panel, proj, att_src, a, masks):
    return pl.pallas_call(
        forward_body,
        out_shape=(
            jax.ShapeDtypeStruct((8, 2, 2, 72, 256), F32),
            jax.ShapeDtypeStruct((32, 8, 128), F32),
        ),
        in_specs=[SMEM, SMEM] + [VMEM] * 5,
        out_specs=(VMEM, VMEM),
        scratch_shapes=[
            pltpu.VMEM((768, 512), BF16),
            pltpu.VMEM((32, 4, 512, 128), BF16),
            pltpu.VMEM((64, 128, 128), F32),
            pltpu.VMEM((64, 128, 128), F32),
            pltpu.VMEM((64, 128, 128), F32),
            pltpu.VMEM((32, 128, 128), F32),
        ],
        compiler_params=pltpu.CompilerParams(vmem_limit_bytes=BIG_VMEM),
    )(blocks, counts, panel, proj, att_src, a, masks)


def merge(arrived, mine, sub):
    one, two = arrived[64:72, 0:128], mine[64:72, 0:128]
    best = jnp.maximum(one[0:4], two[0:4])
    f_one, f_two = jnp.exp2(one[0:4] - best), jnp.exp2(two[0:4] - best)
    total = one[4:8] * f_one + two[4:8] * f_two
    cols = columns_of(jnp.concatenate([f_one, f_two], axis=0))[64 * sub : 64 * sub + 64]
    lane = lanes((64, 128))
    tiles = []
    for pair in range(2):
        span = slice(128 * pair, 128 * pair + 128)
        factor = [
            jnp.where(lane < 64, cols[:, s + 2 * pair : s + 2 * pair + 1], cols[:, s + 2 * pair + 1 : s + 2 * pair + 2])
            for s in (0, 4)
        ]
        tiles.append(arrived[0:64, span] * factor[0] + mine[0:64, span] * factor[1])
    return jnp.concatenate(tiles, axis=1), jnp.concatenate([best, total], axis=0)


def sum_body(acc_ref, out_ref, slots, send, recv):
    z = lax.axis_index("src")
    right, left = lax.rem(z + 1, 8), lax.rem(z + 7, 8)
    greet([], [right, left])()

    def copy(step, way, sub):
        if isinstance(step, int) and step == 0:
            src = acc_ref.at[left if way == 0 else right, way, sub]
        else:
            src = slots.at[step - 1, way, sub]
        return pltpu.make_async_remote_copy(
            src_ref=src,
            dst_ref=slots.at[step, way, sub],
            send_sem=send.at[step, way, sub],
            recv_sem=recv.at[step, way, sub],
            device_id={"src": right if way == 0 else left},
            device_id_type=MESH,
        )

    order = [(way, sub) for sub in range(2) for way in range(2)]
    for way, sub in order:
        copy(0, way, sub).start()

    def block_of(step, way):
        return lax.rem(z + 15 - step, 8) if way == 0 else lax.rem(z + 1 + step, 8)

    def hop(step, carry):
        for way, sub in order:
            pltpu.make_async_remote_copy(
                src_ref=slots.at[step - 1, way, sub],
                dst_ref=slots.at[step - 1, way, sub],
                send_sem=send.at[step - 1, way, sub],
                recv_sem=recv.at[step - 1, way, sub],
                device_id={"src": right if way == 0 else left},
                device_id_type=MESH,
            ).wait_recv()
            values, stats = merge(slots[step - 1, way, sub], acc_ref[block_of(step, way), way, sub], sub)
            slots[step - 1, way, sub, 0:64] = values
            slots[step - 1, way, sub, 64:72, 0:128] = stats
            copy(step, way, sub).start()
        return carry

    lax.fori_loop(1, 7, hop, 0)
    for way, sub in order:
        last = copy(6, way, sub)
        last.wait_recv()
        values, stats = merge(slots[6, way, sub], acc_ref[z, way, sub], sub)
        out_ref[way, sub, 0:64] = values
        out_ref[way, sub, 64:72, 0:128] = stats
        out_ref[way, sub, 64:72, 128:256] = jnp.zeros((8, 128), F32)
    for step in range(7):
        for way, sub in order:
            copy(step, way, sub).wait_send()


def sum_over_src(acc):
    return pl.pallas_call(
        sum_body,
        out_shape=jax.ShapeDtypeStruct((2, 2, 72, 256), F32),
        in_specs=[VMEM],
        out_specs=VMEM,
        scratch_shapes=[
            pltpu.VMEM((7, 2, 2, 72, 256), F32),
            pltpu.SemaphoreType.DMA((7, 2, 2)),
            pltpu.SemaphoreType.DMA((7, 2, 2)),
        ],
        compiler_params=pltpu.CompilerParams(collective_id=1, has_side_effects=True),
    )(acc)


def minus_one(power):
    series = power * (1 + power * (1 / 2 + power * (1 / 6 + power * (1 / 24 + power * (1 / 120)))))
    return jnp.where(power > -0.1, series, jnp.exp(power) - 1)


def owner_body(total_ref, x_ref, p_ref, att_ref, a_ref, cot_ref, out_ref, pay_ref, self_ref, dself_ref):
    proj = p_ref[...]
    h_own = dot(x_ref[...], proj, NN, HIGHEST)
    rows = score_rows(att_ref[...], proj) * LOG2E
    raw = a_ref[...] + dot(rows, x_ref[...], NT, HIGHEST)
    own = leaky(raw)
    parts = [total_ref[way, 0, 64:72, 0:128] for way in range(2)]
    tops = jnp.concatenate([part[0:4] for part in parts], axis=0)
    sums = jnp.concatenate([part[4:8] for part in parts], axis=0)
    best = jnp.maximum(tops, own)
    f_tot, f_own = jnp.exp2(tops - best), jnp.exp2(own - best)
    inverse = 1.0 / (sums * f_tot + f_own)
    slope = jnp.where(raw > 0, 1.0, 0.2)
    cols = columns_of(jnp.concatenate([f_tot * inverse, f_own * inverse, inverse, slope], axis=0))
    lane = lanes((128, 128))
    stats = jnp.zeros((128, 128), F32)
    for pair in range(4):
        way, inner = pair // 2, pair % 2
        span = slice(128 * pair, 128 * pair + 128)
        local = slice(128 * inner, 128 * inner + 128)
        acc = jnp.concatenate([total_ref[way, sub, 0:64, local] for sub in range(2)], axis=0)

        def wide(kind):
            s = 8 * kind + 2 * pair
            return jnp.where(lane < 64, cols[:, s : s + 1], cols[:, s + 1 : s + 2])

        alpha, h_pair = wide(1), h_own[:, span]
        agg = acc * wide(0) + h_pair * alpha
        low = jnp.minimum(agg, 0.0)
        out_ref[:, span] = jnp.where(agg > 0, agg, minus_one(low))
        grad = cot_ref[:, span] * jnp.where(agg > 0, 1.0, jnp.exp(low))
        pay_ref[0:128, span] = grad * wide(2)
        self_ref[span] = (grad * alpha).T
        for odd in range(2):
            h = 2 * pair + odd
            mine = lane >= 64 if odd else lane < 64
            row_dot = jnp.sum(jnp.where(mine, grad * agg, 0.0), axis=1, keepdims=True)
            d_alpha = jnp.sum(jnp.where(mine, grad * h_pair, 0.0), axis=1, keepdims=True)
            d_self = cols[:, 8 + h : 9 + h] * (d_alpha - row_dot) * cols[:, 24 + h : 25 + h]
            stats = jnp.where(lane == h, row_dot * cols[:, 16 + h : 17 + h], stats)
            stats = jnp.where(lane == 8 + h, d_self, stats)
    turned = stats.T
    pay_ref[128:136, 0:128] = best
    pay_ref[128:136, 128:256] = turned[0:8]
    pay_ref[128:136, 256:512] = jnp.zeros((8, 256), F32)
    dself_ref[...] = turned[8:16]


def owner_rows(total, x, proj, att_src, a_own, cotangent):
    return pl.pallas_call(
        owner_body,
        out_shape=(
            jax.ShapeDtypeStruct((128, 512), F32),
            jax.ShapeDtypeStruct((136, 512), F32),
            jax.ShapeDtypeStruct((512, 128), F32),
            jax.ShapeDtypeStruct((8, 128), F32),
        ),
        in_specs=[VMEM] * 6,
        out_specs=(VMEM,) * 4,
    )(total, x, proj, att_src, a_own, cotangent)


def grads_body(pay_ref, all_ref, send, recv, own_sem):
    z = lax.axis_index("src")
    right, left = lax.rem(z + 1, 8), lax.rem(z + 7, 8)
    wait_all = greet([], [right, left])
    own_copy = pltpu.make_async_copy(pay_ref, all_ref.at[z], own_sem)
    own_copy.start()
    wait_all()
    links = Links(send, recv)
    spans = (pl.ds(0, 64), pl.ds(64, 72))

    def push(step, way, sub):
        block = lax.rem(z + 8 - step, 8) if way == 0 else lax.rem(z + step, 8)
        part = all_ref.at[block, spans[sub]]
        src = pay_ref.at[spans[sub]] if step == 0 else part
        return links.push(src, part, src=right if way == 0 else left)

    order = [(way, sub) for sub in range(2) for way in range(2)]
    coming = {item: push(0, *item) for item in order}
    for step in range(1, 4):
        for item in order:
            coming[item].wait_recv()
            if step < 3 or item[0] == item[1]:
                coming[item] = push(step, *item)
            else:
                del coming[item]
    for copy in coming.values():
        copy.wait_recv()
    own_copy.wait()
    links.drain()


def gather_grads(pay):
    return pl.pallas_call(
        grads_body,
        out_shape=jax.ShapeDtypeStruct((8, 136, 512), F32),
        in_specs=[VMEM],
        out_specs=ANY,
        scratch_shapes=[
            pltpu.SemaphoreType.DMA((14,)),
            pltpu.SemaphoreType.DMA((14,)),
            pltpu.SemaphoreType.DMA,
        ],
        compiler_params=pltpu.CompilerParams(collective_id=2, has_side_effects=True),
    )(pay)


def backward_body(
    blocks, counts, spot, x_ref, p_ref, a_ref, b_ref, mask_ref, pay_ref, self_ref, dself_ref,
    dh_out, dsrc_out, ddst_out, p_cat, hb, gn, gt, top, abc, dots, ddst, dsrc,
):
    prepare_features(x_ref, p_ref, p_cat, hb, lambda c, xc: None)
    even = (lax.broadcasted_iota(jnp.int32, (128, 1), 0) < 64).astype(F32)
    odd = 1.0 - even

    def setup(b, carry):
        cols = columns_of(
            jnp.concatenate([a_ref[b], pay_ref[b, 128:136, 0:128], pay_ref[b, 128:136, 128:256]], axis=0)
        )
        dots[b] = cols
        for h in range(8):
            abc[b * 8 + h] = jnp.broadcast_to(cols[:, h : h + 1], (128, 128))
            top[b * 8 + h] = jnp.broadcast_to(cols[:, 8 + h : 9 + h], (128, 128))
        for pair in range(4):
            grad = pay_ref[b, 0:128, 128 * pair : 128 * pair + 128]
            high, low = split(grad)
            gn[b, pair, :, 0:128] = high
            gn[b, pair, :, 128:256] = low
            turned = grad.T
            e_high, e_low = split(turned * even)
            o_high, o_low = split(turned * odd)
            gt[b, pair, :, 0:128] = e_high
            gt[b, pair, :, 128:256] = o_high
            gt[b, pair, :, 256:384] = e_low
            gt[b, pair, :, 384:512] = o_low
        return carry

    lax.fori_loop(0, 8, setup, 0)
    ddst[...] = jnp.zeros(ddst.shape, F32)
    dsrc[...] = jnp.zeros(dsrc.shape, F32)
    dh_out[...] = jnp.zeros(dh_out.shape, F32)
    dh_out[spot[0]] = self_ref[...]

    def step(k, carry):
        b, c = blocks[k, 0], blocks[k, 1]
        keep = mask_ref[k] > 0
        scores = b_ref[c]
        cols = dots[b]
        for pair in range(4):
            g_high, g_low = gn[b, pair, :, 0:128], gn[b, pair, :, 128:256]
            h_high, h_low = hb[c, pair, 0:256], hb[c, pair, 256:512]
            d_alpha = dot(
                jnp.concatenate([g_high, g_high, g_low], axis=1),
                jnp.concatenate([h_high, h_low, h_high], axis=1),
                NT,
            )
            highs, lows = [], []
            for side in range(2):
                h = 2 * pair + side
                raw = abc[b * 8 + h] + jnp.where(keep, scores[h : h + 1], NEG)
                w = jnp.exp2(leaky(raw) - top[b * 8 + h])
                d_raw = w * (d_alpha[:, 128 * side : 128 * side + 128] - cols[:, 16 + h : 17 + h])
                d_raw = jnp.where(raw > 0, d_raw, 0.2 * d_raw)
                ddst[b * 8 + h] += d_raw
                dsrc[c * 8 + h] += jnp.sum(d_raw.reshape(16, 8, 128), axis=0)
                high, low = split(w)
                highs.append(high)
                lows.append(low)
            left = jnp.concatenate([gt[b, pair], gt[b, pair, :, 0:256]], axis=1)
            right = jnp.concatenate(highs + highs + lows, axis=0)
            dh_out[c, 128 * pair : 128 * pair + 128] += dot(left, right)
        return carry

    lax.fori_loop(0, counts[0], step, 0)

    def pack_dst(b, carry):
        lane = lanes((128, 128))
        packed = jnp.zeros((128, 128), F32)
        for h in range(8):
            packed = jnp.where(lane == h, jnp.sum(ddst[b * 8 + h], axis=1, keepdims=True), packed)
        ddst_out[b] = packed.T[0:8]
        return carry

    lax.fori_loop(0, 8, pack_dst, 0)
    ddst_out[spot[1]] += dself_ref[...]

    def pack_src(c, carry):
        dsrc_out[c] = jnp.concatenate(
            [jnp.sum(dsrc[c * 8 + h], axis=0, keepdims=True) for h in range(8)], axis=0
        )
        return carry

    lax.fori_loop(0, 32, pack_src, 0)
    dsrc_out[spot[0]] += dself_ref[...]


def backward_local(blocks, counts, spot, panel, proj, a, b, masks, pays, dh_self, d_self):
    return pl.pallas_call(
        backward_body,
        out_shape=(
            jax.ShapeDtypeStruct((32, 512, 128), F32),
            jax.ShapeDtypeStruct((32, 8, 128), F32),
            jax.ShapeDtypeStruct((8, 8, 128), F32),
        ),
        in_specs=[SMEM] * 3 + [VMEM] * 8,
        out_specs=(VMEM,) * 3,
        scratch_shapes=[
            pltpu.VMEM((768, 512), BF16),
            pltpu.VMEM((32, 4, 512, 128), BF16),
            pltpu.VMEM((8, 4, 128, 256), BF16),
            pltpu.VMEM((8, 4, 128, 512), BF16),
            pltpu.VMEM((64, 128, 128), F32),
            pltpu.VMEM((64, 128, 128), F32),
            pltpu.VMEM((8, 128, 128), F32),
            pltpu.VMEM((64, 128, 128), F32),
            pltpu.VMEM((256, 8, 128), F32),
        ],
        compiler_params=pltpu.CompilerParams(vmem_limit_bytes=BIG_VMEM),
    )(blocks, counts, spot, panel, proj, a, b, masks, pays, dh_self, d_self)


def project_body(dh_ref, dsrc_ref, x_ref, p_ref, att_ref, dx_ref, dp_ref, v_ref, p_cat, rows_t):
    @pl.when(pl.program_id(0) == 0)
    def _():
        proj = p_ref[...]
        high, low = split(proj)
        p_cat[:, 0:512] = high
        p_cat[:, 512:1024] = low
        p_cat[:, 1024:1536] = high
        rows = jnp.concatenate([score_rows(att_ref[...], proj), jnp.zeros((120, 256), F32)], axis=0)
        rows_t[...] = rows.T
        dp_ref[...] = jnp.zeros(dp_ref.shape, F32)
        v_ref[...] = jnp.zeros(v_ref.shape, F32)

    for s in range(dh_ref.shape[0]):
        x, d_src = x_ref[s], dsrc_ref[s]
        dh_high, dh_low = split(dh_ref[s])
        x_high, x_low = split(x)
        wide_src = jnp.concatenate([d_src, jnp.zeros((120, 128), F32)], axis=0)
        dx_ref[s] = dot(p_cat[...], jnp.concatenate([dh_high, dh_high, dh_low], axis=0)) + dot(
            rows_t[...], wide_src, NN, HIGHEST
        )
        dp_ref[...] += dot(
            jnp.concatenate([dh_high, dh_high, dh_low], axis=1), jnp.concatenate([x_high, x_low, x_high], axis=0)
        )
        v_ref[...] += dot(d_src, x, NN, HIGHEST)


def project_grads(dh, dsrc, panel, proj, att_src):
    n = 4
    return pl.pallas_call(
        project_body,
        grid=(32 // n,),
        out_shape=(
            jax.ShapeDtypeStruct((32, 256, 128), F32),
            jax.ShapeDtypeStruct((512, 256), F32),
            jax.ShapeDtypeStruct((8, 256), F32),
        ),
        in_specs=[
            pl.BlockSpec((n, 512, 128), lambda i: (i, 0, 0)),
            pl.BlockSpec((n, 8, 128), lambda i: (i, 0, 0)),
            pl.BlockSpec((n, 128, 256), lambda i: (i, 0, 0)),
            VMEM,
            VMEM,
        ],
        out_specs=(
            pl.BlockSpec((n, 256, 128), lambda i: (i, 0, 0)),
            pl.BlockSpec((512, 256), lambda i: (0, 0)),
            pl.BlockSpec((8, 256), lambda i: (0, 0)),
        ),
        scratch_shapes=[pltpu.VMEM((256, 1536), BF16), pltpu.VMEM((256, 128), F32)],
        compiler_params=pltpu.CompilerParams(vmem_limit_bytes=BIG_VMEM),
    )(dh, dsrc, panel, proj, att_src)


def reduce_body(
    dx_ref, dp_ref, v_ref, ddst_ref, x_ref, dx_out, dp_out, dst_out,
    send, recv, twin_dx, total, far, near, far2, near2, dst_all, pay, twin_pay, merged, plane, joined, tower,
):
    d, y, x, k, z = place()
    sibling = node(y, x, 1 - k)
    chip = y * 4 + x
    offsets = [(dy, dx) for dy in range(4) for dx in range(4) if (dy, dx) != (0, 0)]
    others = [lax.rem(z + s, 8) for s in range(1, 8)]
    wait_all = greet([sibling] + [node(y + dy, x + dx, k) for dy, dx in offsets], others)
    links = Links(send, recv)
    wait_all()

    dst_copies = [links.push(ddst_ref.at[t], dst_all.at[z], src=t) for t in others]

    def rank(offset):
        return 0 if 2 in offset else (2 if offset == (0, 0) else 1)

    cells = sorted([(0, 0)] + offsets, key=rank)
    twin_copies = {}
    for dy, dx in cells:
        yy, xx = lax.rem(y + dy, 4), lax.rem(x + dx, 4)
        twin_copies[dy, dx] = links.push(dx_ref.at[yy, xx, 1 - k], twin_dx.at[yy, xx], dst=sibling)

    def ring(region, plus, minus, far_buf, near_buf):
        c0 = links.push(region(2, 0), far_buf.at[0], dst=plus)
        c1 = links.push(region(2, 1), far_buf.at[1], dst=minus)
        c2 = links.push(region(1, 1), near_buf.at[0], dst=plus)
        c3 = links.push(region(-1, 0), near_buf.at[1], dst=minus)
        yield
        c0.wait_recv()
        part = region(1, 0)
        part[...] += far_buf[0]
        c4 = links.push(part, near_buf.at[2], dst=plus)
        yield
        c1.wait_recv()
        part = region(-1, 1)
        part[...] += far_buf[1]
        c5 = links.push(part, near_buf.at[3], dst=minus)
        for copy, index, piece in ((c2, 0, 1), (c3, 1, 0), (c4, 2, 0), (c5, 3, 1)):
            yield
            copy.wait_recv()
            part = region(0, piece)
            part[...] += near_buf[index]

    def grads(half):
        rows = pl.ds(128 * half, 128)

        def wide(v, piece):
            if half == 0:
                return total.at[lax.rem(y + v + 4, 4), pl.ds(2 * piece, 2), rows]
            return total.at[pl.ds(2 * piece, 2), lax.rem(x + v + 4, 4), rows]

        def narrow(u, piece):
            span = pl.ds(128 * half + 64 * piece, 64)
            if half == 0:
                return total.at[y, lax.rem(x + u + 4, 4), span]
            return total.at[lax.rem(y + u + 4, 4), x, span]

        along_y = (node(y + 1, x, k), node(y - 1, x, k))
        along_x = (node(y, x + 1, k), node(y, x - 1, k))
        first, then = (along_y, along_x) if half == 0 else (along_x, along_y)
        yield from ring(wide, *first, far.at[half], near.at[half])
        yield from ring(narrow, *then, far2.at[half], near2.at[half])

    def weights():
        for i in range(32):
            pay[i // 2, i % 2, 0:16] = dp_ref[16 * i : 16 * i + 16, 0:128]
            pay[i // 2, i % 2, 16:32] = dp_ref[16 * i : 16 * i + 16, 128:256]
            pay[i // 2, i % 2, 32:40] = jnp.zeros((8, 128), F32)
        for h in range(8):
            for side in range(2):
                i = 8 + h + 16 * side
                pay[i // 2, i % 2, 32:33] = v_ref[h : h + 1, 128 * side : 128 * side + 128]
        yield
        for copy in dst_copies:
            copy.wait_recv()
        dst_all[z] = ddst_ref[z]
        dst_total = dst_all[0]
        for t in range(1, 8):
            dst_total = dst_total + dst_all[t]
        dst_out[...] = dst_total
        u = dot(dst_total, x_ref[...], NN, HIGHEST)
        for h in range(8):
            for side in range(2):
                i = h + 16 * side
                pay[i // 2, i % 2, 32:33] = u[h : h + 1, 128 * side : 128 * side + 128]
        over = links.push(pay.at[:, 1 - k], twin_pay, dst=sibling)
        yield
        over.wait_recv()
        merged[...] = pay[:, k] + twin_pay[...]
        coming = []
        for dy, dx in offsets:
            target = lax.rem(y + dy, 4) * 4 + lax.rem(x + dx, 4)
            coming.append(links.push(merged.at[target], plane.at[chip], dst=node(y + dy, x + dx, k)))
        plane[chip] = merged[chip]
        yield
        for copy in coming:
            copy.wait_recv()
        value = plane[0]
        for i in range(1, 16):
            value = value + plane[i]
        joined[...] = value
        tower[z] = value
        coming = [links.push(joined, tower.at[z], src=t) for t in others]
        yield
        for copy in coming:
            copy.wait_recv()
        value = tower[0]
        for i in range(1, 8):
            value = value + tower[i]
        dp_out[chip, k] = value
        coming = [
            links.push(dp_out.at[chip, k], dp_out.at[chip, k], dst=node(y + dy, x + dx, k)) for dy, dx in offsets
        ]
        yield
        for copy in coming:
            copy.wait_recv()
        over = links.push(dp_out.at[:, k], dp_out.at[:, k], dst=sibling)
        yield
        over.wait_recv()

    small = weights()
    next(small)
    for dy, dx in cells:
        yy, xx = lax.rem(y + dy, 4), lax.rem(x + dx, 4)
        twin_copies[dy, dx].wait_recv()
        total[yy, xx] = dx_ref[yy, xx, k] + twin_dx[yy, xx]
    run_chains([grads(0), grads(1), small])
    dx_out[...] = total[y, x]
    links.drain()


def reduce_grads(dx, dp, v, ddst, x):
    count = 7 + 16 + 24 + 1 + 15 + 7 + 15 + 1
    return pl.pallas_call(
        reduce_body,
        out_shape=(
            jax.ShapeDtypeStruct((256, 128), F32),
            jax.ShapeDtypeStruct((16, 2, 40, 128), F32),
            jax.ShapeDtypeStruct((8, 128), F32),
        ),
        in_specs=[VMEM] * 5,
        out_specs=(VMEM,) * 3,
        scratch_shapes=[
            pltpu.SemaphoreType.DMA((count,)),
            pltpu.SemaphoreType.DMA((count,)),
            pltpu.VMEM((4, 4, 256, 128), F32),
            pltpu.VMEM((4, 4, 256, 128), F32),
            pltpu.VMEM((2, 2, 2, 128, 128), F32),
            pltpu.VMEM((2, 4, 2, 128, 128), F32),
            pltpu.VMEM((2, 2, 64, 128), F32),
            pltpu.VMEM((2, 4, 64, 128), F32),
            pltpu.VMEM((8, 8, 128), F32),
            pltpu.VMEM((16, 2, 40, 128), F32),
            pltpu.VMEM((16, 40, 128), F32),
            pltpu.VMEM((16, 40, 128), F32),
            pltpu.VMEM((16, 40, 128), F32),
            pltpu.VMEM((40, 128), F32),
            pltpu.VMEM((8, 40, 128), F32),
        ],
        compiler_params=pltpu.CompilerParams(
            collective_id=3, has_side_effects=True, vmem_limit_bytes=BIG_VMEM
        ),
    )(dx.reshape(4, 4, 2, 256, 128), dp, v, ddst, x)


def finish_body(dx_ref, w_ref, dst_ref, p_ref, src_att_ref, dst_att_ref, in_ref, proj_ref, src_ref, dst_out):
    proj = p_ref[...]
    a_rows = per_head_rows(dst_att_ref[...])
    s_rows = per_head_rows(src_att_ref[...])
    score = dot(a_rows, proj, NT, HIGHEST)
    pad = jnp.zeros((120, 256), F32)
    score_t = jnp.concatenate([score, pad], axis=0).T
    dst_wide = jnp.concatenate([dst_ref[...], jnp.zeros((120, 128), F32)], axis=0)
    in_ref[...] = (dx_ref[...] + dot(score_t, dst_wide, NN, HIGHEST)).T

    def row(i):
        return jnp.concatenate([w_ref[i, 32:33], w_ref[i + 16, 32:33]], axis=1)

    u = jnp.concatenate([row(h) for h in range(8)], axis=0)
    v = jnp.concatenate([row(8 + h) for h in range(8)], axis=0)
    uv = jnp.concatenate([u, v, jnp.zeros((112, 256), F32)], axis=0)
    att = jnp.concatenate([a_rows, s_rows, jnp.zeros((112, 512), F32)], axis=0)
    grad_t = jnp.concatenate(
        [jnp.concatenate([w_ref[i, 0:16], w_ref[i, 16:32]], axis=1) for i in range(32)], axis=0
    )
    proj_ref[...] = (grad_t + dot(att.T, uv, NN, HIGHEST)).T
    both = dot(jnp.concatenate([u, v], axis=0), proj, NN, HIGHEST)
    dst_out[...] = jnp.concatenate([both[h : h + 1, 64 * h : 64 * h + 64] for h in range(8)], axis=0)
    src_ref[...] = jnp.concatenate([both[8 + h : 9 + h, 64 * h : 64 * h + 64] for h in range(8)], axis=0)


def finish(dx, weights, dst_total, proj, att_src, att_dst):
    return pl.pallas_call(
        finish_body,
        out_shape=(
            jax.ShapeDtypeStruct((128, 256), F32),
            jax.ShapeDtypeStruct((256, 512), F32),
            jax.ShapeDtypeStruct((8, 64), F32),
            jax.ShapeDtypeStruct((8, 64), F32),
        ),
        in_specs=[VMEM] * 6,
        out_specs=(VMEM,) * 4,
    )(dx, weights.reshape(32, 40, 128), dst_total, proj, att_src, att_dst)


def shards(inputs, projection, att_src, att_dst, blocks, counts, tile_masks, cotangent):
    coords = blocks[0, 0]
    live = counts.reshape(1)
    masks = tile_masks[0, 0]
    z = lax.axis_index("src")
    spot = jnp.stack([lax.axis_index("dst"), z]).astype(jnp.int32)
    panel, a = gather_inputs(inputs, projection, att_dst)
    acc, b = forward_local(coords, live, panel, projection, att_src, a, masks)
    total = sum_over_src(acc)
    a_own = lax.dynamic_index_in_dim(a, z, 0, keepdims=False)
    output, pay, dh_self, d_self = owner_rows(total, inputs, projection, att_src, a_own, cotangent)
    pays = gather_grads(pay)
    dh, dsrc, ddst = backward_local(
        coords, live, spot, panel, projection, a, b, masks, pays, dh_self, d_self
    )
    dx, dp, v = project_grads(dh, dsrc, panel, projection, att_src)
    dx_own, weights, dst_total = reduce_grads(dx, dp, v, ddst, inputs)
    in_grad, proj_grad, src_grad, dst_grad = finish(
        dx_own, weights, dst_total, projection, att_src, att_dst
    )
    return (output, in_grad, proj_grad, src_grad, dst_grad)


def solution(mesh):
    in_specs = (
        P(("dst", "src"), None),
        P(),
        P(),
        P(),
        P("dst", "src", None, None),
        P("dst", "src"),
        P("dst", "src", None, None, None),
        P(("dst", "src"), None),
    )
    out_specs = (P(("dst", "src"), None), P(("dst", "src"), None), P(), P(), P())
    return jax.shard_map(shards, mesh=mesh, in_specs=in_specs, out_specs=out_specs, check_vma=False)
```

```python
import functools

import jax
import jax.numpy as jnp
from jax import lax
from jax.experimental import pallas as pl
from jax.experimental.pallas import tpu as pltpu
from jax.sharding import PartitionSpec as P

HIGHEST = lax.Precision.HIGHEST
F32 = jnp.float32
BF16 = jnp.bfloat16
LOG2E = 1.4426950408889634
NEG = -1e30
MESH = pl.DeviceIdType.MESH
VMEM = pl.BlockSpec(memory_space=pltpu.VMEM)
SMEM = pl.BlockSpec(memory_space=pltpu.SMEM)
ANY = pl.BlockSpec(memory_space=pl.ANY)
NN = (((1,), (0,)), ((), ()))
NT = (((1,), (1,)), ((), ()))
BIG_VMEM = 60 * 1024 * 1024


def dot(a, b, dims=NN, precision=None):
    return lax.dot_general(a, b, dims, precision=precision, preferred_element_type=F32)


def split(value):
    high = value.astype(BF16)
    return high, (value - high.astype(F32)).astype(BF16)


def leaky(raw):
    return jnp.maximum(raw, 0.2 * raw)


def per_head_rows(att):
    wide = jnp.concatenate([att] * 8, axis=1)
    head = lax.broadcasted_iota(jnp.int32, wide.shape, 0)
    column = lax.broadcasted_iota(jnp.int32, wide.shape, 1)
    return jnp.where(column // 64 == head, wide, 0.0)


def score_rows(att, proj):
    return dot(per_head_rows(att), proj, NT, HIGHEST)


def lanes(shape):
    return lax.broadcasted_iota(jnp.int32, shape, len(shape) - 1)


def place():
    d = lax.axis_index("dst")
    z = lax.axis_index("src")
    return d, d // 8, lax.rem(d // 2, 4), lax.rem(d, 2), z


def node(y, x, k):
    return lax.rem(y + 8, 4) * 8 + lax.rem(x + 8, 4) * 2 + k


class Links:
    def __init__(self, send, recv):
        self.send, self.recv, self.used, self.open = send, recv, 0, []

    def push(self, source, landing, **target):
        copy = pltpu.make_async_remote_copy(
            src_ref=source,
            dst_ref=landing,
            send_sem=self.send.at[self.used],
            recv_sem=self.recv.at[self.used],
            device_id=target,
            device_id_type=MESH,
        )
        self.used += 1
        copy.start()
        self.open.append(copy)
        return copy

    def drain(self):
        for copy in self.open:
            copy.wait_send()


def greet(dsts, srcs):
    barrier = pltpu.get_barrier_semaphore()
    for other in dsts:
        pl.semaphore_signal(barrier, inc=1, device_id={"dst": other}, device_id_type=MESH)
    for other in srcs:
        pl.semaphore_signal(barrier, inc=1, device_id={"src": other}, device_id_type=MESH)
    return lambda: pl.semaphore_wait(barrier, len(dsts) + len(srcs))


def run_chains(chains):
    chains = list(chains)
    while chains:
        for chain in list(chains):
            try:
                next(chain)
            except StopIteration:
                chains.remove(chain)


def gather_body(x_ref, p_ref, src_ref, dst_ref, panel_ref, a_ref, pay, send, recv, own_sem):
    d, y, x, k, z = place()
    sibling = node(y, x, 1 - k)
    wait_all = greet(
        [sibling, node(y + 1, x, k), node(y - 1, x, k), node(y, x + 1, k), node(y, x - 1, k)],
        [lax.rem(z + s, 8) for s in range(1, 8)],
    )
    rows = jnp.concatenate([score_rows(r[...], p_ref[...]) for r in (src_ref, dst_ref)], axis=0) * LOG2E
    scores = dot(rows, x_ref[...], NT, HIGHEST)
    pay[0:128] = x_ref[...]
    pay[128:136, 0:128] = scores[0:8]
    pay[128:136, 128:256] = scores[8:16]
    a_ref[z] = scores[8:16]
    own_copy = pltpu.make_async_copy(pay, panel_ref.at[d], own_sem)
    own_copy.start()
    wait_all()
    links = Links(send, recv)

    def chain(half):
        def at(u, v):
            return node(y + v, x + u, k) if half == 0 else node(y + u, x + v, k)

        def region(u, v, quarter=None):
            start, size = 64 * half, 64 + 8 * half
            if quarter is not None:
                start, size = start + 32 * quarter, 32 + 8 * half * quarter
            return panel_ref.at[at(u, v), pl.ds(start, size)]

        def to(part, du, dv, src=None):
            return links.push(part if src is None else src, part, dst=at(du, dv))

        def twin(u, v, src=None):
            part = region(u, v)
            return links.push(part if src is None else src, part, dst=sibling)

        own = pay.at[pl.ds(64 * half, 64 + 8 * half)]
        first = [to(region(0, 0), 1, 0, own), to(region(0, 0), -1, 0, own)]
        second = {0: [to(region(0, 0), 0, 1, own), to(region(0, 0), 0, -1, own)]}
        twins = [twin(0, 0, own)]
        last = {}

        def spread(u):
            second[u] = [to(region(u, 0), 0, 1), to(region(u, 0), 0, -1)]
            twins.append(twin(u, 0))

        def relay(u):
            pair = []
            for index, v in ((0, -1), (1, 1)):
                yield
                second[u][index].wait_recv()
                pair.append(to(region(u, v, index), 0, -v))
                twins.append(twin(u, v))
            last[u] = pair

        def finish(u):
            yield
            for copy in last[u]:
                copy.wait_recv()
            twins.append(twin(u, 2))

        far = []
        for index, u in ((0, -1), (1, 1)):
            yield
            first[index].wait_recv()
            far.append(to(region(u, 0, index), -u, 0))
            spread(u)
        yield from relay(0)
        yield
        for copy in far:
            copy.wait_recv()
        spread(2)
        yield from relay(-1)
        yield from relay(1)
        yield from finish(0)
        yield from relay(2)
        yield from finish(-1)
        yield from finish(1)
        yield from finish(2)
        yield
        for copy in twins:
            copy.wait_recv()

    scores = [
        links.push(a_ref.at[z], a_ref.at[z], src=lax.rem(z + s, 8)) for s in range(1, 8)
    ]
    run_chains([chain(0), chain(1)])
    for copy in scores:
        copy.wait_recv()
    own_copy.wait()
    links.drain()


def gather_inputs(x, proj, att_src, att_dst):
    count = 72 + 7
    return pl.pallas_call(
        gather_body,
        out_shape=(
            jax.ShapeDtypeStruct((32, 136, 256), F32),
            jax.ShapeDtypeStruct((8, 8, 128), F32),
        ),
        in_specs=[VMEM] * 4,
        out_specs=(ANY, VMEM),
        scratch_shapes=[
            pltpu.VMEM((136, 256), F32),
            pltpu.SemaphoreType.DMA((count,)),
            pltpu.SemaphoreType.DMA((count,)),
            pltpu.SemaphoreType.DMA,
        ],
        compiler_params=pltpu.CompilerParams(collective_id=0, has_side_effects=True),
    )(x, proj, att_src, att_dst)


def split_weights(p_ref, p_cat):
    high, low = split(p_ref[...])
    p_cat[0:256] = high
    p_cat[256:512] = low
    p_cat[512:768] = high


def stream_in(panel, x_ref, masks, mask_ref, sems):
    def part(group):
        span = pl.ds(4 * group, 4)
        return pltpu.make_async_copy(panel.at[span], x_ref.at[span], sems.at[group])

    for group in range(8):
        part(group).start()
    pltpu.make_async_copy(masks, mask_ref, sems.at[8]).start()
    return part


def prepare_features(x_ref, p_cat, hb, arrive):
    even = (lanes((1, 128)) < 64).astype(BF16)
    odd = (lanes((1, 128)) >= 64).astype(BF16)
    n = 4

    def step(group, carry):
        arrive(group).wait()
        x_high, x_low = split(jnp.concatenate([x_ref[group * n + s, 0:128] for s in range(n)], axis=0))
        left = jnp.concatenate([x_high, x_high, x_low], axis=1)
        for wide in range(2):
            h_high, h_low = split(dot(left, p_cat[:, 256 * wide : 256 * wide + 256]))
            for s in range(n):
                for side in range(2):
                    part = (slice(128 * s, 128 * s + 128), slice(128 * side, 128 * side + 128))
                    pair = 2 * wide + side
                    hb[group * n + s, pair, 0:128] = h_high[part] * even
                    hb[group * n + s, pair, 128:256] = h_high[part] * odd
                    hb[group * n + s, pair, 256:384] = h_low[part] * even
                    hb[group * n + s, pair, 384:512] = h_low[part] * odd
        return carry

    lax.fori_loop(0, 32 // n, step, 0)


def columns_of(rows):
    pad = jnp.zeros((128 - rows.shape[0], 128), F32)
    return jnp.concatenate([rows, pad], axis=0).T


def spread_rows(rows_of, put):
    parts = []
    for b in range(8):
        kinds = rows_of(b)
        pieces = []
        for rows in kinds:
            high = rows.astype(BF16).astype(F32)
            middle = (rows - high).astype(BF16).astype(F32)
            pieces += [high, middle, rows - high - middle]
        parts.append(columns_of(jnp.concatenate(pieces, axis=0)).astype(BF16))
    left = jnp.concatenate(parts, axis=0)
    count = len(kinds)
    row = lax.broadcasted_iota(jnp.int32, (128, 128 * count), 0)
    kind = lax.broadcasted_iota(jnp.int32, (128, 128 * count), 1) // 128
    for h in range(8):
        pick = jnp.logical_and(row // 24 == kind, lax.rem(row, 8) == h)
        out = dot(left, jnp.where(pick, 1.0, 0.0).astype(BF16))
        for k in range(count):
            for b in range(8):
                put(k, b, h, out[128 * b : 128 * b + 128, 128 * k : 128 * k + 128])


def forward_body(
    blocks, counts, panel, p_ref, a_ref, masks, acc_out, p_cat, hb, top, abc, sums, acc, top_rows, x_ref, mask_ref, sems
):
    arrive = stream_in(panel, x_ref, masks, mask_ref, sems)
    split_weights(p_ref, p_cat)
    prepare_features(x_ref, p_cat, hb, arrive)
    pltpu.make_async_copy(masks, mask_ref, sems.at[8]).wait()
    top[...] = jnp.full(top.shape, NEG, F32)
    sums[...] = jnp.zeros(sums.shape, F32)
    acc[...] = jnp.zeros(acc.shape, F32)
    live = counts[0]

    def find_top(k, carry):
        b, c = blocks[k, 0], blocks[k, 1]
        keep = mask_ref[k] > 0
        scores = x_ref[c, 128:136, 0:128]
        for h in range(8):
            top[b * 8 + h] = jnp.maximum(top[b * 8 + h], jnp.where(keep, scores[h : h + 1], NEG))
        return carry

    lax.fori_loop(0, live, find_top, 0)

    def find_rows(b, carry):
        best = jnp.concatenate([jnp.max(top[b * 8 + h].T, axis=0, keepdims=True) for h in range(8)], axis=0)
        top_rows[b] = leaky(a_ref[b] + best)
        return carry

    lax.fori_loop(0, 8, find_rows, 0)

    def put(kind, b, h, tile):
        (abc, top)[kind][b * 8 + h] = tile

    spread_rows(lambda b: [a_ref[b], top_rows[b]], put)

    def accumulate(k, carry):
        b, c = blocks[k, 0], blocks[k, 1]
        keep = mask_ref[k] > 0
        scores = x_ref[c, 128:136, 0:128]
        for pair in range(4):
            highs, lows = [], []
            for h in (2 * pair, 2 * pair + 1):
                raw = abc[b * 8 + h] + jnp.where(keep, scores[h : h + 1], NEG)
                w = jnp.exp2(leaky(raw) - top[b * 8 + h])
                sums[b * 8 + h] += w
                high, low = split(w)
                highs.append(high)
                lows.append(low)
            left = jnp.concatenate(highs + highs + lows, axis=1)
            right = jnp.concatenate([hb[c, pair], hb[c, pair, 0:256]], axis=0)
            acc[b * 4 + pair] += dot(left, right)
        return carry

    lax.fori_loop(0, live, accumulate, 0)

    def pack(b, carry):
        totals = [jnp.sum(sums[b * 8 + h].T, axis=0, keepdims=True) for h in range(8)]
        for way in range(2):
            packed = jnp.concatenate([top_rows[b, 4 * way : 4 * way + 4]] + totals[4 * way : 4 * way + 4], axis=0)
            for sub in range(2):
                span = slice(64 * sub, 64 * sub + 64)
                acc_out[b, way, sub, 0:64, 0:128] = acc[b * 4 + 2 * way][span]
                acc_out[b, way, sub, 0:64, 128:256] = acc[b * 4 + 2 * way + 1][span]
                acc_out[b, way, sub, 64:72, 0:128] = packed
                acc_out[b, way, sub, 64:72, 128:256] = jnp.zeros((8, 128), F32)
        return carry

    lax.fori_loop(0, 8, pack, 0)


def forward_local(blocks, counts, panel, proj, a, masks):
    return pl.pallas_call(
        forward_body,
        out_shape=jax.ShapeDtypeStruct((8, 2, 2, 72, 256), F32),
        in_specs=[SMEM, SMEM, ANY, VMEM, VMEM, ANY],
        out_specs=VMEM,
        scratch_shapes=[
            pltpu.VMEM((768, 512), BF16),
            pltpu.VMEM((32, 4, 512, 128), BF16),
            pltpu.VMEM((64, 128, 128), F32),
            pltpu.VMEM((64, 128, 128), F32),
            pltpu.VMEM((64, 128, 128), F32),
            pltpu.VMEM((32, 128, 128), F32),
            pltpu.VMEM((8, 8, 128), F32),
            pltpu.VMEM((32, 136, 256), F32),
            pltpu.VMEM((32, 128, 128), jnp.int32),
            pltpu.SemaphoreType.DMA((9,)),
        ],
        compiler_params=pltpu.CompilerParams(vmem_limit_bytes=BIG_VMEM),
    )(blocks, counts, panel, proj, a, masks)


def merge(arrived, mine, sub):
    one, two = arrived[64:72, 0:128], mine[64:72, 0:128]
    best = jnp.maximum(one[0:4], two[0:4])
    f_one, f_two = jnp.exp2(one[0:4] - best), jnp.exp2(two[0:4] - best)
    total = one[4:8] * f_one + two[4:8] * f_two
    cols = columns_of(jnp.concatenate([f_one, f_two], axis=0))[64 * sub : 64 * sub + 64]
    lane = lanes((64, 128))
    tiles = []
    for pair in range(2):
        span = slice(128 * pair, 128 * pair + 128)
        factor = [
            jnp.where(lane < 64, cols[:, s + 2 * pair : s + 2 * pair + 1], cols[:, s + 2 * pair + 1 : s + 2 * pair + 2])
            for s in (0, 4)
        ]
        tiles.append(arrived[0:64, span] * factor[0] + mine[0:64, span] * factor[1])
    return jnp.concatenate(tiles, axis=1), jnp.concatenate([best, total], axis=0)


def sum_body(acc_ref, out_ref, slots, send, recv):
    z = lax.axis_index("src")
    right, left = lax.rem(z + 1, 8), lax.rem(z + 7, 8)
    greet([], [right, left])()

    def copy(step, way, sub):
        if isinstance(step, int) and step == 0:
            src = acc_ref.at[left if way == 0 else right, way, sub]
        else:
            src = slots.at[step - 1, way, sub]
        return pltpu.make_async_remote_copy(
            src_ref=src,
            dst_ref=slots.at[step, way, sub],
            send_sem=send.at[step, way, sub],
            recv_sem=recv.at[step, way, sub],
            device_id={"src": right if way == 0 else left},
            device_id_type=MESH,
        )

    order = [(way, sub) for sub in range(2) for way in range(2)]
    for way, sub in order:
        copy(0, way, sub).start()

    def block_of(step, way):
        return lax.rem(z + 15 - step, 8) if way == 0 else lax.rem(z + 1 + step, 8)

    def hop(step, carry):
        for way, sub in order:
            pltpu.make_async_remote_copy(
                src_ref=slots.at[step - 1, way, sub],
                dst_ref=slots.at[step - 1, way, sub],
                send_sem=send.at[step - 1, way, sub],
                recv_sem=recv.at[step - 1, way, sub],
                device_id={"src": right if way == 0 else left},
                device_id_type=MESH,
            ).wait_recv()
            values, stats = merge(slots[step - 1, way, sub], acc_ref[block_of(step, way), way, sub], sub)
            slots[step - 1, way, sub, 0:64] = values
            slots[step - 1, way, sub, 64:72, 0:128] = stats
            copy(step, way, sub).start()
        return carry

    lax.fori_loop(1, 7, hop, 0)
    for way, sub in order:
        last = copy(6, way, sub)
        last.wait_recv()
        values, stats = merge(slots[6, way, sub], acc_ref[z, way, sub], sub)
        out_ref[way, sub, 0:64] = values
        out_ref[way, sub, 64:72, 0:128] = stats
        out_ref[way, sub, 64:72, 128:256] = jnp.zeros((8, 128), F32)
    for step in range(7):
        for way, sub in order:
            copy(step, way, sub).wait_send()


def sum_over_src(acc):
    return pl.pallas_call(
        sum_body,
        out_shape=jax.ShapeDtypeStruct((2, 2, 72, 256), F32),
        in_specs=[VMEM],
        out_specs=VMEM,
        scratch_shapes=[
            pltpu.VMEM((7, 2, 2, 72, 256), F32),
            pltpu.SemaphoreType.DMA((7, 2, 2)),
            pltpu.SemaphoreType.DMA((7, 2, 2)),
        ],
        compiler_params=pltpu.CompilerParams(collective_id=1, has_side_effects=True),
    )(acc)


def minus_one(power):
    series = power * (1 + power * (1 / 2 + power * (1 / 6 + power * (1 / 24 + power * (1 / 120)))))
    return jnp.where(power > -0.1, series, jnp.exp(power) - 1)


def owner_body(total_ref, x_ref, p_ref, att_ref, a_ref, cot_ref, out_ref, pay_ref, self_ref, dself_ref):
    proj = p_ref[...]
    h_own = dot(x_ref[...], proj, NN, HIGHEST)
    rows = score_rows(att_ref[...], proj) * LOG2E
    raw = a_ref[...] + dot(rows, x_ref[...], NT, HIGHEST)
    own = leaky(raw)
    parts = [total_ref[way, 0, 64:72, 0:128] for way in range(2)]
    tops = jnp.concatenate([part[0:4] for part in parts], axis=0)
    sums = jnp.concatenate([part[4:8] for part in parts], axis=0)
    best = jnp.maximum(tops, own)
    f_tot, f_own = jnp.exp2(tops - best), jnp.exp2(own - best)
    inverse = 1.0 / (sums * f_tot + f_own)
    slope = jnp.where(raw > 0, 1.0, 0.2)
    cols = columns_of(jnp.concatenate([f_tot * inverse, f_own * inverse, inverse, slope], axis=0))
    lane = lanes((128, 128))
    stats = jnp.zeros((128, 128), F32)
    for pair in range(4):
        way, inner = pair // 2, pair % 2
        span = slice(128 * pair, 128 * pair + 128)
        local = slice(128 * inner, 128 * inner + 128)
        acc = jnp.concatenate([total_ref[way, sub, 0:64, local] for sub in range(2)], axis=0)

        def wide(kind):
            s = 8 * kind + 2 * pair
            return jnp.where(lane < 64, cols[:, s : s + 1], cols[:, s + 1 : s + 2])

        alpha, h_pair = wide(1), h_own[:, span]
        agg = acc * wide(0) + h_pair * alpha
        low = jnp.minimum(agg, 0.0)
        out_ref[:, span] = jnp.where(agg > 0, agg, minus_one(low))
        grad = cot_ref[:, span] * jnp.where(agg > 0, 1.0, jnp.exp(low))
        pay_ref[0:128, span] = grad * wide(2)
        self_ref[span] = (grad * alpha).T
        for odd in range(2):
            h = 2 * pair + odd
            mine = lane >= 64 if odd else lane < 64
            row_dot = jnp.sum(jnp.where(mine, grad * agg, 0.0), axis=1, keepdims=True)
            d_alpha = jnp.sum(jnp.where(mine, grad * h_pair, 0.0), axis=1, keepdims=True)
            d_self = cols[:, 8 + h : 9 + h] * (d_alpha - row_dot) * cols[:, 24 + h : 25 + h]
            stats = jnp.where(lane == h, row_dot * cols[:, 16 + h : 17 + h], stats)
            stats = jnp.where(lane == 8 + h, d_self, stats)
    turned = stats.T
    pay_ref[128:136, 0:128] = best
    pay_ref[128:136, 128:256] = turned[0:8]
    pay_ref[128:136, 256:512] = jnp.zeros((8, 256), F32)
    dself_ref[...] = turned[8:16]


def owner_rows(total, x, proj, att_src, a_own, cotangent):
    return pl.pallas_call(
        owner_body,
        out_shape=(
            jax.ShapeDtypeStruct((128, 512), F32),
            jax.ShapeDtypeStruct((136, 512), F32),
            jax.ShapeDtypeStruct((512, 128), F32),
            jax.ShapeDtypeStruct((8, 128), F32),
        ),
        in_specs=[VMEM] * 6,
        out_specs=(VMEM,) * 4,
    )(total, x, proj, att_src, a_own, cotangent)


def grads_body(pay_ref, all_ref, send, recv, own_sem):
    z = lax.axis_index("src")
    right, left = lax.rem(z + 1, 8), lax.rem(z + 7, 8)
    wait_all = greet([], [right, left])
    own_copy = pltpu.make_async_copy(pay_ref, all_ref.at[z], own_sem)
    own_copy.start()
    wait_all()
    links = Links(send, recv)
    spans = (pl.ds(0, 64), pl.ds(64, 72))

    def push(step, way, sub):
        block = lax.rem(z + 8 - step, 8) if way == 0 else lax.rem(z + step, 8)
        part = all_ref.at[block, spans[sub]]
        src = pay_ref.at[spans[sub]] if step == 0 else part
        return links.push(src, part, src=right if way == 0 else left)

    order = [(way, sub) for sub in range(2) for way in range(2)]
    coming = {item: push(0, *item) for item in order}
    for step in range(1, 4):
        for item in order:
            coming[item].wait_recv()
            if step < 3 or item[0] == item[1]:
                coming[item] = push(step, *item)
            else:
                del coming[item]
    for copy in coming.values():
        copy.wait_recv()
    own_copy.wait()
    links.drain()


def gather_grads(pay):
    return pl.pallas_call(
        grads_body,
        out_shape=jax.ShapeDtypeStruct((8, 136, 512), F32),
        in_specs=[VMEM],
        out_specs=ANY,
        scratch_shapes=[
            pltpu.SemaphoreType.DMA((14,)),
            pltpu.SemaphoreType.DMA((14,)),
            pltpu.SemaphoreType.DMA,
        ],
        compiler_params=pltpu.CompilerParams(collective_id=2, has_side_effects=True),
    )(pay)


def backward_body(
    blocks, counts, spot, panel, p_ref, att_ref, a_ref, masks, pay_ref, self_ref, dself_ref,
    dx_out, dp_out, ddst_out, p_cat, hb, gn, gt, top, abc, dots, ddst, dsrc, dh, p_wide, att_wide,
    dx_slots, dx_sems, x_ref, mask_ref, sems,
):
    arrive = stream_in(panel, x_ref, masks, mask_ref, sems)
    split_weights(p_ref, p_cat)
    prepare_features(x_ref, p_cat, hb, arrive)
    pltpu.make_async_copy(masks, mask_ref, sems.at[8]).wait()
    even = (lax.broadcasted_iota(jnp.int32, (128, 1), 0) < 64).astype(F32)
    odd = 1.0 - even

    def setup(b, carry):
        dots[b] = columns_of(pay_ref[b, 128:136, 128:256])
        for pair in range(4):
            grad = pay_ref[b, 0:128, 128 * pair : 128 * pair + 128]
            high, low = split(grad)
            gn[b, pair, :, 0:128] = high
            gn[b, pair, :, 128:256] = low
            turned = grad.T
            e_high, e_low = split(turned * even)
            o_high, o_low = split(turned * odd)
            gt[b, pair, :, 0:128] = e_high
            gt[b, pair, :, 128:256] = o_high
            gt[b, pair, :, 256:384] = e_low
            gt[b, pair, :, 384:512] = o_low
        return carry

    lax.fori_loop(0, 8, setup, 0)

    def put(kind, b, h, tile):
        (abc, top)[kind][b * 8 + h] = tile

    spread_rows(lambda b: [a_ref[b], pay_ref[b, 128:136, 0:128]], put)
    ddst[...] = jnp.zeros(ddst.shape, F32)
    dsrc[...] = jnp.zeros(dsrc.shape, F32)
    dh[...] = jnp.zeros(dh.shape, F32)
    dh[spot[0]] = self_ref[...]

    def step(k, carry):
        b, c = blocks[k, 0], blocks[k, 1]
        keep = mask_ref[k] > 0
        scores = x_ref[c, 128:136, 0:128]
        cols = dots[b]
        for pair in range(4):
            g_high, g_low = gn[b, pair, :, 0:128], gn[b, pair, :, 128:256]
            h_high, h_low = hb[c, pair, 0:256], hb[c, pair, 256:512]
            d_alpha = dot(
                jnp.concatenate([g_high, g_high, g_low], axis=1),
                jnp.concatenate([h_high, h_low, h_high], axis=1),
                NT,
            )
            highs, lows = [], []
            for side in range(2):
                h = 2 * pair + side
                raw = abc[b * 8 + h] + jnp.where(keep, scores[h : h + 1], NEG)
                w = jnp.exp2(leaky(raw) - top[b * 8 + h])
                d_raw = w * (d_alpha[:, 128 * side : 128 * side + 128] - cols[:, h : h + 1])
                d_raw = jnp.where(raw > 0, d_raw, 0.2 * d_raw)
                ddst[b * 8 + h] += d_raw
                dsrc[c * 8 + h] += jnp.sum(d_raw.reshape(16, 8, 128), axis=0)
                high, low = split(w)
                highs.append(high)
                lows.append(low)
            left = jnp.concatenate([gt[b, pair], gt[b, pair, :, 0:256]], axis=1)
            right = jnp.concatenate(highs + highs + lows, axis=0)
            dh[c, 128 * pair : 128 * pair + 128] += dot(left, right)
        return carry

    lax.fori_loop(0, counts[0], step, 0)

    def pack_dst(b, carry):
        ddst_out[b] = jnp.concatenate(
            [jnp.sum(ddst[b * 8 + h].T, axis=0, keepdims=True) for h in range(8)], axis=0
        )
        return carry

    lax.fori_loop(0, 8, pack_dst, 0)
    ddst_out[spot[1]] += dself_ref[...]

    high, low = split(p_ref[...])
    p_wide[:, 0:512] = high
    p_wide[:, 512:1024] = low
    p_wide[:, 1024:1536] = high
    att_cols = columns_of(jnp.concatenate([att_ref[...], jnp.zeros((8, 64), F32)], axis=1))
    for h in range(8):
        att_wide[64 * h : 64 * h + 64] = jnp.broadcast_to(att_cols[0:64, h : h + 1], (64, 128))
    dp_out[...] = jnp.zeros(dp_out.shape, F32)
    own = spot[0]

    def leave(four, slot):
        return pltpu.make_async_copy(dx_slots.at[slot], dx_out.at[pl.ds(4 * four, 4)], dx_sems.at[slot])

    def project(four, carry):
        wide_dh, wide_src = [], []
        for s in range(4):
            c = 4 * four + s
            d_src = jnp.concatenate(
                [jnp.sum(dsrc[c * 8 + h], axis=0, keepdims=True) for h in range(8)], axis=0
            )
            d_src = d_src + jnp.where(c == own, dself_ref[...], 0.0)
            spread = jnp.concatenate(
                [att_wide[64 * h : 64 * h + 64] * d_src[h : h + 1] for h in range(8)], axis=0
            )
            wide_dh.append(dh[c] + spread)
            wide_src.append(jnp.concatenate([d_src, jnp.zeros((8, 128), F32)], axis=0))
        high, low = split(jnp.concatenate(wide_dh, axis=1))
        s_high, s_low = split(jnp.concatenate(wide_src, axis=1))
        x_high, x_low = split(jnp.concatenate([x_ref[4 * four + s, 0:128] for s in range(4)], axis=0))
        dx = dot(p_wide[...], jnp.concatenate([high, high, low], axis=0))
        slot = lax.rem(four, 2)

        @pl.when(four >= 2)
        def _():
            leave(four - 2, slot).wait()

        for s in range(4):
            dx_slots[slot, s] = dx[:, 128 * s : 128 * s + 128]
        leave(four, slot).start()
        tall_high = jnp.concatenate([high, s_high], axis=0)
        tall_low = jnp.concatenate([low, s_low], axis=0)
        dp_out[...] += dot(
            jnp.concatenate([tall_high, tall_high, tall_low], axis=1),
            jnp.concatenate([x_high, x_low, x_high], axis=0),
        )
        return carry

    lax.fori_loop(0, 8, project, 0)
    leave(6, 0).wait()
    leave(7, 1).wait()


def backward_local(blocks, counts, spot, panel, proj, att_src, a, masks, pays, dh_self, d_self):
    return pl.pallas_call(
        backward_body,
        out_shape=(
            jax.ShapeDtypeStruct((32, 256, 128), F32),
            jax.ShapeDtypeStruct((528, 256), F32),
            jax.ShapeDtypeStruct((8, 8, 128), F32),
        ),
        in_specs=[SMEM] * 3 + [ANY, VMEM, VMEM, VMEM, ANY, VMEM, VMEM, VMEM],
        out_specs=(ANY, VMEM, VMEM),
        scratch_shapes=[
            pltpu.VMEM((768, 512), BF16),
            pltpu.VMEM((32, 4, 512, 128), BF16),
            pltpu.VMEM((8, 4, 128, 256), BF16),
            pltpu.VMEM((8, 4, 128, 512), BF16),
            pltpu.VMEM((64, 128, 128), F32),
            pltpu.VMEM((64, 128, 128), F32),
            pltpu.VMEM((8, 128, 128), F32),
            pltpu.VMEM((64, 128, 128), F32),
            pltpu.VMEM((256, 8, 128), F32),
            pltpu.VMEM((32, 512, 128), F32),
            pltpu.VMEM((256, 1536), BF16),
            pltpu.VMEM((512, 128), F32),
            pltpu.VMEM((2, 4, 256, 128), F32),
            pltpu.SemaphoreType.DMA((2,)),
            pltpu.VMEM((32, 136, 256), F32),
            pltpu.VMEM((32, 128, 128), jnp.int32),
            pltpu.SemaphoreType.DMA((9,)),
        ],
        compiler_params=pltpu.CompilerParams(vmem_limit_bytes=BIG_VMEM),
    )(blocks, counts, spot, panel, proj, att_src, a, masks, pays, dh_self, d_self)


def reduce_body(
    dx_ref, dp_ref, ddst_ref, x_ref, dx_out, dp_out, dst_out,
    send, recv, twin_dx, total, far, near, far2, near2, dst_all, pay, twin_pay, merged, plane, joined, tower,
):
    d, y, x, k, z = place()
    sibling = node(y, x, 1 - k)
    chip = y * 4 + x
    offsets = [(dy, dx) for dy in range(4) for dx in range(4) if (dy, dx) != (0, 0)]
    others = [lax.rem(z + s, 8) for s in range(1, 8)]
    wait_all = greet([sibling] + [node(y + dy, x + dx, k) for dy, dx in offsets], others)
    links = Links(send, recv)
    wait_all()

    dst_copies = [links.push(ddst_ref.at[t], dst_all.at[z], src=t) for t in others]

    def rank(offset):
        return 0 if 2 in offset else (2 if offset == (0, 0) else 1)

    cells = sorted([(0, 0)] + offsets, key=rank)
    twin_copies = {}
    for dy, dx in cells:
        yy, xx = lax.rem(y + dy, 4), lax.rem(x + dx, 4)
        twin_copies[dy, dx] = links.push(dx_ref.at[yy, xx, 1 - k], twin_dx.at[yy, xx], dst=sibling)

    def ring(region, plus, minus, far_buf, near_buf):
        c0 = links.push(region(2, 0), far_buf.at[0], dst=plus)
        c1 = links.push(region(2, 1), far_buf.at[1], dst=minus)
        c2 = links.push(region(1, 1), near_buf.at[0], dst=plus)
        c3 = links.push(region(-1, 0), near_buf.at[1], dst=minus)
        yield
        c0.wait_recv()
        part = region(1, 0)
        part[...] += far_buf[0]
        c4 = links.push(part, near_buf.at[2], dst=plus)
        yield
        c1.wait_recv()
        part = region(-1, 1)
        part[...] += far_buf[1]
        c5 = links.push(part, near_buf.at[3], dst=minus)
        for copy, index, piece in ((c2, 0, 1), (c3, 1, 0), (c4, 2, 0), (c5, 3, 1)):
            yield
            copy.wait_recv()
            part = region(0, piece)
            part[...] += near_buf[index]

    def grads(half):
        rows = pl.ds(128 * half, 128)

        def wide(v, piece):
            if half == 0:
                return total.at[lax.rem(y + v + 4, 4), pl.ds(2 * piece, 2), rows]
            return total.at[pl.ds(2 * piece, 2), lax.rem(x + v + 4, 4), rows]

        def narrow(u, piece):
            span = pl.ds(128 * half + 64 * piece, 64)
            if half == 0:
                return total.at[y, lax.rem(x + u + 4, 4), span]
            return total.at[lax.rem(y + u + 4, 4), x, span]

        along_y = (node(y + 1, x, k), node(y - 1, x, k))
        along_x = (node(y, x + 1, k), node(y, x - 1, k))
        first, then = (along_y, along_x) if half == 0 else (along_x, along_y)
        yield from ring(wide, *first, far.at[half], near.at[half])
        yield from ring(narrow, *then, far2.at[half], near2.at[half])

    def weights():
        for i in range(32):
            pay[i // 2, i % 2, 0:16] = dp_ref[16 * i : 16 * i + 16, 0:128]
            pay[i // 2, i % 2, 16:32] = dp_ref[16 * i : 16 * i + 16, 128:256]
            pay[i // 2, i % 2, 32:40] = jnp.zeros((8, 128), F32)
        for h in range(8):
            for side in range(2):
                i = 8 + h + 16 * side
                pay[i // 2, i % 2, 32:33] = dp_ref[512 + h : 513 + h, 128 * side : 128 * side + 128]
        yield
        for copy in dst_copies:
            copy.wait_recv()
        dst_all[z] = ddst_ref[z]
        dst_total = dst_all[0]
        for t in range(1, 8):
            dst_total = dst_total + dst_all[t]
        dst_out[...] = dst_total
        u = dot(dst_total, x_ref[...], NN, HIGHEST)
        for h in range(8):
            for side in range(2):
                i = h + 16 * side
                pay[i // 2, i % 2, 32:33] = u[h : h + 1, 128 * side : 128 * side + 128]
        over = links.push(pay.at[:, 1 - k], twin_pay, dst=sibling)
        yield
        over.wait_recv()
        merged[...] = pay[:, k] + twin_pay[...]
        coming = []
        for dy, dx in offsets:
            target = lax.rem(y + dy, 4) * 4 + lax.rem(x + dx, 4)
            coming.append(links.push(merged.at[target], plane.at[chip], dst=node(y + dy, x + dx, k)))
        plane[chip] = merged[chip]
        yield
        for copy in coming:
            copy.wait_recv()
        value = plane[0]
        for i in range(1, 16):
            value = value + plane[i]
        joined[...] = value
        tower[z] = value
        coming = [links.push(joined, tower.at[z], src=t) for t in others]
        yield
        for copy in coming:
            copy.wait_recv()
        value = tower[0]
        for i in range(1, 8):
            value = value + tower[i]
        dp_out[chip, k] = value
        coming = [
            links.push(dp_out.at[chip, k], dp_out.at[chip, k], dst=node(y + dy, x + dx, k)) for dy, dx in offsets
        ]
        yield
        for copy in coming:
            copy.wait_recv()
        over = links.push(dp_out.at[:, k], dp_out.at[:, k], dst=sibling)
        yield
        over.wait_recv()

    small = weights()
    next(small)
    for dy, dx in cells:
        yy, xx = lax.rem(y + dy, 4), lax.rem(x + dx, 4)
        twin_copies[dy, dx].wait_recv()
        total[yy, xx] = dx_ref[yy, xx, k] + twin_dx[yy, xx]
    run_chains([grads(0), grads(1), small])
    dx_out[...] = total[y, x]
    links.drain()


def reduce_grads(dx, dp, ddst, x):
    count = 7 + 16 + 24 + 1 + 15 + 7 + 15 + 1
    return pl.pallas_call(
        reduce_body,
        out_shape=(
            jax.ShapeDtypeStruct((256, 128), F32),
            jax.ShapeDtypeStruct((16, 2, 40, 128), F32),
            jax.ShapeDtypeStruct((8, 128), F32),
        ),
        in_specs=[VMEM] * 4,
        out_specs=(VMEM,) * 3,
        scratch_shapes=[
            pltpu.SemaphoreType.DMA((count,)),
            pltpu.SemaphoreType.DMA((count,)),
            pltpu.VMEM((4, 4, 256, 128), F32),
            pltpu.VMEM((4, 4, 256, 128), F32),
            pltpu.VMEM((2, 2, 2, 128, 128), F32),
            pltpu.VMEM((2, 4, 2, 128, 128), F32),
            pltpu.VMEM((2, 2, 64, 128), F32),
            pltpu.VMEM((2, 4, 64, 128), F32),
            pltpu.VMEM((8, 8, 128), F32),
            pltpu.VMEM((16, 2, 40, 128), F32),
            pltpu.VMEM((16, 40, 128), F32),
            pltpu.VMEM((16, 40, 128), F32),
            pltpu.VMEM((16, 40, 128), F32),
            pltpu.VMEM((40, 128), F32),
            pltpu.VMEM((8, 40, 128), F32),
        ],
        compiler_params=pltpu.CompilerParams(
            collective_id=3, has_side_effects=True, vmem_limit_bytes=BIG_VMEM
        ),
    )(dx.reshape(4, 4, 2, 256, 128), dp, ddst, x)


def finish_body(dx_ref, w_ref, dst_ref, p_ref, dst_att_ref, in_ref, proj_ref, src_ref, dst_out):
    proj = p_ref[...]
    a_rows = per_head_rows(dst_att_ref[...])
    score = dot(a_rows, proj, NT, HIGHEST)
    pad = jnp.zeros((120, 256), F32)
    score_t = jnp.concatenate([score, pad], axis=0).T
    dst_wide = jnp.concatenate([dst_ref[...], jnp.zeros((120, 128), F32)], axis=0)
    in_ref[...] = (dx_ref[...] + dot(score_t, dst_wide, NN, HIGHEST)).T

    def row(i):
        return jnp.concatenate([w_ref[i, 32:33], w_ref[i + 16, 32:33]], axis=1)

    u = jnp.concatenate([row(h) for h in range(8)], axis=0)
    v = jnp.concatenate([row(8 + h) for h in range(8)], axis=0)
    wide_u = jnp.concatenate([u, jnp.zeros((120, 256), F32)], axis=0)
    att = jnp.concatenate([a_rows, jnp.zeros((120, 512), F32)], axis=0)
    grad_t = jnp.concatenate(
        [jnp.concatenate([w_ref[i, 0:16], w_ref[i, 16:32]], axis=1) for i in range(32)], axis=0
    )
    proj_ref[...] = (grad_t + dot(att.T, wide_u, NN, HIGHEST)).T
    both = dot(jnp.concatenate([u, v], axis=0), proj, NN, HIGHEST)
    dst_out[...] = jnp.concatenate([both[h : h + 1, 64 * h : 64 * h + 64] for h in range(8)], axis=0)
    src_ref[...] = jnp.concatenate([both[8 + h : 9 + h, 64 * h : 64 * h + 64] for h in range(8)], axis=0)


def finish(dx, weights, dst_total, proj, att_dst):
    return pl.pallas_call(
        finish_body,
        out_shape=(
            jax.ShapeDtypeStruct((128, 256), F32),
            jax.ShapeDtypeStruct((256, 512), F32),
            jax.ShapeDtypeStruct((8, 64), F32),
            jax.ShapeDtypeStruct((8, 64), F32),
        ),
        in_specs=[VMEM] * 5,
        out_specs=(VMEM,) * 4,
    )(dx, weights.reshape(32, 40, 128), dst_total, proj, att_dst)


def shards(inputs, projection, att_src, att_dst, blocks, counts, tile_masks, cotangent):
    coords = blocks[0, 0]
    live = counts.reshape(1)
    masks = tile_masks[0, 0]
    z = lax.axis_index("src")
    spot = jnp.stack([lax.axis_index("dst"), z]).astype(jnp.int32)
    panel, a = gather_inputs(inputs, projection, att_src, att_dst)
    acc = forward_local(coords, live, panel, projection, a, masks)
    total = sum_over_src(acc)
    a_own = lax.dynamic_index_in_dim(a, z, 0, keepdims=False)
    output, pay, dh_self, d_self = owner_rows(total, inputs, projection, att_src, a_own, cotangent)
    pays = gather_grads(pay)
    dx, dp, ddst = backward_local(
        coords, live, spot, panel, projection, att_src, a, masks, pays, dh_self, d_self
    )
    dx_own, weights, dst_total = reduce_grads(dx, dp, ddst, inputs)
    in_grad, proj_grad, src_grad, dst_grad = finish(dx_own, weights, dst_total, projection, att_dst)
    return (output, in_grad, proj_grad, src_grad, dst_grad)


def solution(mesh):
    in_specs = (
        P(("dst", "src"), None),
        P(),
        P(),
        P(),
        P("dst", "src", None, None),
        P("dst", "src"),
        P("dst", "src", None, None, None),
        P(("dst", "src"), None),
    )
    out_specs = (P(("dst", "src"), None), P(("dst", "src"), None), P(), P(), P())
    return jax.shard_map(shards, mesh=mesh, in_specs=in_specs, out_specs=out_specs, check_vma=False)
```

```python
import functools

import jax
import jax.numpy as jnp
from jax import lax
from jax.experimental import pallas as pl
from jax.experimental.pallas import tpu as pltpu
from jax.sharding import PartitionSpec as P

HIGHEST = lax.Precision.HIGHEST
F32 = jnp.float32
BF16 = jnp.bfloat16
LOG2E = 1.4426950408889634
NEG = -1e30
MESH = pl.DeviceIdType.MESH
VMEM = pl.BlockSpec(memory_space=pltpu.VMEM)
SMEM = pl.BlockSpec(memory_space=pltpu.SMEM)
ANY = pl.BlockSpec(memory_space=pl.ANY)
NN = (((1,), (0,)), ((), ()))
NT = (((1,), (1,)), ((), ()))
BIG_VMEM = 60 * 1024 * 1024


def dot(a, b, dims=NN, precision=None):
    return lax.dot_general(a, b, dims, precision=precision, preferred_element_type=F32)


def split(value):
    high = value.astype(BF16)
    return high, (value - high.astype(F32)).astype(BF16)


def leaky(raw):
    return jnp.maximum(raw, 0.2 * raw)


def per_head_rows(att):
    wide = jnp.concatenate([att] * 8, axis=1)
    head = lax.broadcasted_iota(jnp.int32, wide.shape, 0)
    column = lax.broadcasted_iota(jnp.int32, wide.shape, 1)
    return jnp.where(column // 64 == head, wide, 0.0)


def score_rows(att, proj):
    return dot(per_head_rows(att), proj, NT, HIGHEST)


def lanes(shape):
    return lax.broadcasted_iota(jnp.int32, shape, len(shape) - 1)


def place():
    d = lax.axis_index("dst")
    z = lax.axis_index("src")
    return d, d // 8, lax.rem(d // 2, 4), lax.rem(d, 2), z


def node(y, x, k):
    return lax.rem(y + 8, 4) * 8 + lax.rem(x + 8, 4) * 2 + k


class Links:
    def __init__(self, send, recv):
        self.send, self.recv, self.used, self.open = send, recv, 0, []

    def push(self, source, landing, **target):
        copy = pltpu.make_async_remote_copy(
            src_ref=source,
            dst_ref=landing,
            send_sem=self.send.at[self.used],
            recv_sem=self.recv.at[self.used],
            device_id=target,
            device_id_type=MESH,
        )
        self.used += 1
        copy.start()
        self.open.append(copy)
        return copy

    def drain(self):
        for copy in self.open:
            copy.wait_send()


def greet(dsts, srcs):
    barrier = pltpu.get_barrier_semaphore()
    for other in dsts:
        pl.semaphore_signal(barrier, inc=1, device_id={"dst": other}, device_id_type=MESH)
    for other in srcs:
        pl.semaphore_signal(barrier, inc=1, device_id={"src": other}, device_id_type=MESH)
    return lambda: pl.semaphore_wait(barrier, len(dsts) + len(srcs))


def run_chains(chains):
    chains = list(chains)
    while chains:
        for chain in list(chains):
            try:
                next(chain)
            except StopIteration:
                chains.remove(chain)


def around(links, own_ref, all_ref, z):
    spans = (pl.ds(0, 64), pl.ds(64, 72))
    right, left = lax.rem(z + 1, 8), lax.rem(z + 7, 8)

    def push(step, way, sub):
        block = lax.rem(z + 8 - step, 8) if way == 0 else lax.rem(z + step, 8)
        part = all_ref.at[block, spans[sub]]
        source = own_ref.at[spans[sub]] if step == 0 else part
        return links.push(source, part, src=right if way == 0 else left)

    order = [(way, sub) for sub in range(2) for way in range(2)]
    coming = {item: push(0, *item) for item in order}
    for step in range(1, 4):
        for item in order:
            yield
            coming[item].wait_recv()
            if step < 3 or item[0] == item[1]:
                coming[item] = push(step, *item)
            else:
                del coming[item]
    for copy in list(coming.values()):
        yield
        copy.wait_recv()


def gather_body(x_ref, p_ref, src_ref, dst_ref, panel_ref, group_ref, own_ref, pay, send, recv, own_sem):
    d, y, x, k, z = place()
    sibling = node(y, x, 1 - k)
    wait_all = greet(
        [sibling, node(y + 1, x, k), node(y - 1, x, k), node(y, x + 1, k), node(y, x - 1, k)],
        [lax.rem(z + 1, 8), lax.rem(z + 7, 8)],
    )
    rows = jnp.concatenate([score_rows(r[...], p_ref[...]) for r in (src_ref, dst_ref)], axis=0) * LOG2E
    scores = dot(rows, x_ref[...], NT, HIGHEST)
    pay[0:128] = x_ref[...]
    pay[128:136, 0:128] = scores[0:8]
    pay[128:136, 128:256] = scores[8:16]
    own_ref[...] = scores
    own_copies = [
        pltpu.make_async_copy(pay, panel_ref.at[d], own_sem.at[0]),
        pltpu.make_async_copy(pay, group_ref.at[z], own_sem.at[1]),
    ]
    for copy in own_copies:
        copy.start()
    wait_all()
    links = Links(send, recv)

    def chain(half):
        def at(u, v):
            return node(y + v, x + u, k) if half == 0 else node(y + u, x + v, k)

        def region(u, v, quarter=None):
            start, size = 64 * half, 64 + 8 * half
            if quarter is not None:
                start, size = start + 32 * quarter, 32 + 8 * half * quarter
            return panel_ref.at[at(u, v), pl.ds(start, size)]

        def to(part, du, dv, src=None):
            return links.push(part if src is None else src, part, dst=at(du, dv))

        def twin(u, v, src=None):
            part = region(u, v)
            return links.push(part if src is None else src, part, dst=sibling)

        own = pay.at[pl.ds(64 * half, 64 + 8 * half)]
        first = [to(region(0, 0), 1, 0, own), to(region(0, 0), -1, 0, own)]
        second = {0: [to(region(0, 0), 0, 1, own), to(region(0, 0), 0, -1, own)]}
        twins = [twin(0, 0, own)]
        last = {}

        def spread(u):
            second[u] = [to(region(u, 0), 0, 1), to(region(u, 0), 0, -1)]
            twins.append(twin(u, 0))

        def relay(u):
            pair = []
            for index, v in ((0, -1), (1, 1)):
                yield
                second[u][index].wait_recv()
                pair.append(to(region(u, v, index), 0, -v))
                twins.append(twin(u, v))
            last[u] = pair

        def finish(u):
            yield
            for copy in last[u]:
                copy.wait_recv()
            twins.append(twin(u, 2))

        far = []
        for index, u in ((0, -1), (1, 1)):
            yield
            first[index].wait_recv()
            far.append(to(region(u, 0, index), -u, 0))
            spread(u)
        yield from relay(0)
        yield
        for copy in far:
            copy.wait_recv()
        spread(2)
        yield from relay(-1)
        yield from relay(1)
        yield from finish(0)
        yield from relay(2)
        yield from finish(-1)
        yield from finish(1)
        yield from finish(2)
        yield
        for copy in twins:
            copy.wait_recv()

    run_chains([chain(0), chain(1), around(links, pay, group_ref, z)])
    for copy in own_copies:
        copy.wait()
    links.drain()


def gather_inputs(x, proj, att_src, att_dst):
    count = 72 + 14
    return pl.pallas_call(
        gather_body,
        out_shape=(
            jax.ShapeDtypeStruct((32, 136, 256), F32),
            jax.ShapeDtypeStruct((8, 136, 256), F32),
            jax.ShapeDtypeStruct((16, 128), F32),
        ),
        in_specs=[VMEM] * 4,
        out_specs=(ANY, ANY, VMEM),
        scratch_shapes=[
            pltpu.VMEM((136, 256), F32),
            pltpu.SemaphoreType.DMA((count,)),
            pltpu.SemaphoreType.DMA((count,)),
            pltpu.SemaphoreType.DMA((2,)),
        ],
        compiler_params=pltpu.CompilerParams(collective_id=0, has_side_effects=True),
    )(x, proj, att_src, att_dst)


def split_weights(p_ref, p_cat):
    high, low = split(p_ref[...])
    p_cat[0:256] = high
    p_cat[256:512] = low
    p_cat[512:768] = high


def stream_in(panel, x_ref, masks, mask_ref, group, a_ref, sems):
    def part(i):
        span = pl.ds(4 * i, 4)
        return pltpu.make_async_copy(panel.at[span], x_ref.at[span], sems.at[i])

    for i in range(8):
        part(i).start()
    pltpu.make_async_copy(masks, mask_ref, sems.at[8]).start()
    pltpu.make_async_copy(group.at[:, pl.ds(128, 8), pl.ds(128, 128)], a_ref, sems.at[9]).start()
    return part


def prepare_features(x_ref, p_cat, hb, arrive):
    even = (lanes((1, 128)) < 64).astype(BF16)
    odd = (lanes((1, 128)) >= 64).astype(BF16)
    n = 4

    def step(group, carry):
        arrive(group).wait()
        x_high, x_low = split(jnp.concatenate([x_ref[group * n + s, 0:128] for s in range(n)], axis=0))
        left = jnp.concatenate([x_high, x_high, x_low], axis=1)
        for wide in range(2):
            h_high, h_low = split(dot(left, p_cat[:, 256 * wide : 256 * wide + 256]))
            for s in range(n):
                for side in range(2):
                    part = (slice(128 * s, 128 * s + 128), slice(128 * side, 128 * side + 128))
                    pair = 2 * wide + side
                    hb[group * n + s, pair, 0:128] = h_high[part] * even
                    hb[group * n + s, pair, 128:256] = h_high[part] * odd
                    hb[group * n + s, pair, 256:384] = h_low[part] * even
                    hb[group * n + s, pair, 384:512] = h_low[part] * odd
        return carry

    lax.fori_loop(0, 32 // n, step, 0)


def columns_of(rows):
    pad = jnp.zeros((128 - rows.shape[0], 128), F32)
    return jnp.concatenate([rows, pad], axis=0).T


def spread_rows(rows_of, put):
    parts = []
    for b in range(8):
        kinds = rows_of(b)
        pieces = []
        for rows in kinds:
            high = rows.astype(BF16).astype(F32)
            middle = (rows - high).astype(BF16).astype(F32)
            pieces += [high, middle, rows - high - middle]
        parts.append(columns_of(jnp.concatenate(pieces, axis=0)).astype(BF16))
    left = jnp.concatenate(parts, axis=0)
    count = len(kinds)
    row = lax.broadcasted_iota(jnp.int32, (128, 128 * count), 0)
    kind = lax.broadcasted_iota(jnp.int32, (128, 128 * count), 1) // 128
    for h in range(8):
        pick = jnp.logical_and(row // 24 == kind, lax.rem(row, 8) == h)
        out = dot(left, jnp.where(pick, 1.0, 0.0).astype(BF16))
        for k in range(count):
            for b in range(8):
                put(k, b, h, out[128 * b : 128 * b + 128, 128 * k : 128 * k + 128])


def forward_body(
    blocks, counts, panel, p_ref, group, masks, acc_out, p_cat, hb, top, abc, sums, acc, top_rows, a_ref, x_ref, mask_ref, sems
):
    arrive = stream_in(panel, x_ref, masks, mask_ref, group, a_ref, sems)
    split_weights(p_ref, p_cat)
    prepare_features(x_ref, p_cat, hb, arrive)
    pltpu.make_async_copy(masks, mask_ref, sems.at[8]).wait()
    pltpu.make_async_copy(group.at[:, pl.ds(128, 8), pl.ds(128, 128)], a_ref, sems.at[9]).wait()
    top[...] = jnp.full(top.shape, NEG, F32)
    sums[...] = jnp.zeros(sums.shape, F32)
    acc[...] = jnp.zeros(acc.shape, F32)
    live = counts[0]

    def find_top(k, carry):
        b, c = blocks[2 * k], blocks[2 * k + 1]
        keep = mask_ref[k] > 0
        scores = x_ref[c, 128:136, 0:128]
        for h in range(8):
            top[b * 8 + h] = jnp.maximum(top[b * 8 + h], jnp.where(keep, scores[h : h + 1], NEG))
        return carry

    lax.fori_loop(0, live, find_top, 0)

    def find_rows(b, carry):
        best = jnp.concatenate([jnp.max(top[b * 8 + h].T, axis=0, keepdims=True) for h in range(8)], axis=0)
        top_rows[b] = leaky(a_ref[b] + best)
        return carry

    lax.fori_loop(0, 8, find_rows, 0)

    def put(kind, b, h, tile):
        (abc, top)[kind][b * 8 + h] = tile

    spread_rows(lambda b: [a_ref[b], top_rows[b]], put)

    def accumulate(k, carry):
        b, c = blocks[2 * k], blocks[2 * k + 1]
        keep = mask_ref[k] > 0
        scores = x_ref[c, 128:136, 0:128]
        for pair in range(4):
            highs, lows = [], []
            for h in (2 * pair, 2 * pair + 1):
                raw = abc[b * 8 + h] + jnp.where(keep, scores[h : h + 1], NEG)
                w = jnp.exp2(leaky(raw) - top[b * 8 + h])
                sums[b * 8 + h] += w
                high, low = split(w)
                highs.append(high)
                lows.append(low)
            left = jnp.concatenate(highs + highs + lows, axis=1)
            right = jnp.concatenate([hb[c, pair], hb[c, pair, 0:256]], axis=0)
            acc[b * 4 + pair] += dot(left, right)
        return carry

    lax.fori_loop(0, live, accumulate, 0)

    def pack(b, carry):
        totals = [jnp.sum(sums[b * 8 + h].T, axis=0, keepdims=True) for h in range(8)]
        for way in range(2):
            for inner in range(2):
                h = 4 * way + 2 * inner
                packed = jnp.concatenate(
                    [top_rows[b, h : h + 2]] + totals[h : h + 2] + [jnp.zeros((4, 128), F32)], axis=0
                )
                for half in range(2):
                    sub = 2 * inner + half
                    acc_out[b, way, sub, 0:64] = acc[b * 4 + 2 * way + inner][64 * half : 64 * half + 64]
                    acc_out[b, way, sub, 64:72] = packed
        return carry

    lax.fori_loop(0, 8, pack, 0)


def forward_local(blocks, counts, panel, proj, group, masks):
    return pl.pallas_call(
        forward_body,
        out_shape=jax.ShapeDtypeStruct((8, 2, 4, 72, 128), F32),
        in_specs=[SMEM, SMEM, ANY, VMEM, ANY, ANY],
        out_specs=VMEM,
        scratch_shapes=[
            pltpu.VMEM((768, 512), BF16),
            pltpu.VMEM((32, 4, 512, 128), BF16),
            pltpu.VMEM((64, 128, 128), F32),
            pltpu.VMEM((64, 128, 128), F32),
            pltpu.VMEM((64, 128, 128), F32),
            pltpu.VMEM((32, 128, 128), F32),
            pltpu.VMEM((8, 8, 128), F32),
            pltpu.VMEM((8, 8, 128), F32),
            pltpu.VMEM((32, 136, 256), F32),
            pltpu.VMEM((32, 128, 128), jnp.int32),
            pltpu.SemaphoreType.DMA((10,)),
        ],
        compiler_params=pltpu.CompilerParams(vmem_limit_bytes=BIG_VMEM),
    )(blocks, counts, panel, proj, group, masks)


def merge(arrived, mine, half):
    one, two = arrived[64:72], mine[64:72]
    best = jnp.maximum(one[0:2], two[0:2])
    f_one, f_two = jnp.exp2(one[0:2] - best), jnp.exp2(two[0:2] - best)
    total = one[2:4] * f_one + two[2:4] * f_two
    cols = columns_of(jnp.concatenate([f_one, f_two, best, total], axis=0))[64 * half : 64 * half + 64]
    lane = lanes((64, 128))
    factor = [jnp.where(lane < 64, cols[:, s : s + 1], cols[:, s + 1 : s + 2]) for s in (0, 2)]
    values = arrived[0:64] * factor[0] + mine[0:64] * factor[1]
    return values, jnp.concatenate([best, total, one[4:8]], axis=0)


def exchange_body(
    acc_ref, x_ref, p_ref, own_ref, cot_ref, out_ref, all_ref, self_ref, dself_ref,
    slots, total, pay, h_own, send, recv, grad_send, grad_recv, own_sem,
):
    z = lax.axis_index("src")
    right, left = lax.rem(z + 1, 8), lax.rem(z + 7, 8)
    wait_all = greet([], [right, left])
    wait_all()

    def copy(step, way, sub):
        if isinstance(step, int) and step == 0:
            src = acc_ref.at[left if way == 0 else right, way, sub]
        else:
            src = slots.at[step - 1, way, sub]
        return pltpu.make_async_remote_copy(
            src_ref=src,
            dst_ref=slots.at[step, way, sub],
            send_sem=send.at[step, way, sub],
            recv_sem=recv.at[step, way, sub],
            device_id={"src": right if way == 0 else left},
            device_id_type=MESH,
        )

    order = [(way, sub) for sub in range(4) for way in range(2)]
    for way, sub in order:
        copy(0, way, sub).start()
    h_own[...] = dot(x_ref[...], p_ref[...], NN, HIGHEST)

    def block_of(step, way):
        return lax.rem(z + 15 - step, 8) if way == 0 else lax.rem(z + 1 + step, 8)

    def hop(step, carry):
        for way, sub in order:
            pltpu.make_async_remote_copy(
                src_ref=slots.at[step - 1, way, sub],
                dst_ref=slots.at[step - 1, way, sub],
                send_sem=send.at[step - 1, way, sub],
                recv_sem=recv.at[step - 1, way, sub],
                device_id={"src": right if way == 0 else left},
                device_id_type=MESH,
            ).wait_recv()
            values, stats = merge(slots[step - 1, way, sub], acc_ref[block_of(step, way), way, sub], sub % 2)
            slots[step - 1, way, sub, 0:64] = values
            slots[step - 1, way, sub, 64:72] = stats
            copy(step, way, sub).start()
        return carry

    lax.fori_loop(1, 7, hop, 0)
    for way, sub in order:
        last = copy(6, way, sub)
        last.wait_recv()
        values, stats = merge(slots[6, way, sub], acc_ref[z, way, sub], sub % 2)
        total[way, sub, 0:64] = values
        total[way, sub, 64:72] = stats
    owner_rows(total, own_ref, h_own, cot_ref, out_ref, pay, self_ref, dself_ref)
    own_copy = pltpu.make_async_copy(pay, all_ref.at[z], own_sem)
    own_copy.start()
    links = Links(grad_send, grad_recv)
    run_chains([around(links, pay, all_ref, z)])
    for step in range(7):
        for way, sub in order:
            copy(step, way, sub).wait_send()
    own_copy.wait()
    links.drain()


def exchange(acc, x, proj, own, cotangent):
    return pl.pallas_call(
        exchange_body,
        out_shape=(
            jax.ShapeDtypeStruct((128, 512), F32),
            jax.ShapeDtypeStruct((8, 136, 512), F32),
            jax.ShapeDtypeStruct((512, 128), F32),
            jax.ShapeDtypeStruct((8, 128), F32),
        ),
        in_specs=[VMEM] * 5,
        out_specs=(VMEM, ANY, VMEM, VMEM),
        scratch_shapes=[
            pltpu.VMEM((7, 2, 4, 72, 128), F32),
            pltpu.VMEM((2, 4, 72, 128), F32),
            pltpu.VMEM((136, 512), F32),
            pltpu.VMEM((128, 512), F32),
            pltpu.SemaphoreType.DMA((7, 2, 4)),
            pltpu.SemaphoreType.DMA((7, 2, 4)),
            pltpu.SemaphoreType.DMA((14,)),
            pltpu.SemaphoreType.DMA((14,)),
            pltpu.SemaphoreType.DMA,
        ],
        compiler_params=pltpu.CompilerParams(collective_id=1, has_side_effects=True),
    )(acc, x, proj, own, cotangent)


def minus_one(power):
    series = power * (1 + power * (1 / 2 + power * (1 / 6 + power * (1 / 24 + power * (1 / 120)))))
    return jnp.where(power > -0.1, series, jnp.exp(power) - 1)


def owner_rows(total_ref, own_ref, h_own, cot_ref, out_ref, pay_ref, self_ref, dself_ref):
    raw = own_ref[0:8] + own_ref[8:16]
    own = leaky(raw)
    parts = [total_ref[pair // 2, 2 * (pair % 2), 64:72] for pair in range(4)]
    tops = jnp.concatenate([part[0:2] for part in parts], axis=0)
    sums = jnp.concatenate([part[2:4] for part in parts], axis=0)
    best = jnp.maximum(tops, own)
    f_tot, f_own = jnp.exp2(tops - best), jnp.exp2(own - best)
    inverse = 1.0 / (sums * f_tot + f_own)
    slope = jnp.where(raw > 0, 1.0, 0.2)
    cols = columns_of(jnp.concatenate([f_tot * inverse, f_own * inverse, inverse, slope], axis=0))
    lane = lanes((128, 128))
    stats = jnp.zeros((128, 128), F32)
    for pair in range(4):
        way, inner = pair // 2, pair % 2
        span = slice(128 * pair, 128 * pair + 128)
        acc = jnp.concatenate([total_ref[way, 2 * inner + half, 0:64] for half in range(2)], axis=0)

        def wide(kind):
            s = 8 * kind + 2 * pair
            return jnp.where(lane < 64, cols[:, s : s + 1], cols[:, s + 1 : s + 2])

        alpha, h_pair = wide(1), h_own[:, span]
        agg = acc * wide(0) + h_pair * alpha
        low = jnp.minimum(agg, 0.0)
        out_ref[:, span] = jnp.where(agg > 0, agg, minus_one(low))
        grad = cot_ref[:, span] * jnp.where(agg > 0, 1.0, jnp.exp(low))
        pay_ref[0:128, span] = grad * wide(2)
        self_ref[span] = (grad * alpha).T
        for odd in range(2):
            h = 2 * pair + odd
            mine = lane >= 64 if odd else lane < 64
            row_dot = jnp.sum(jnp.where(mine, grad * agg, 0.0), axis=1, keepdims=True)
            d_alpha = jnp.sum(jnp.where(mine, grad * h_pair, 0.0), axis=1, keepdims=True)
            d_self = cols[:, 8 + h : 9 + h] * (d_alpha - row_dot) * cols[:, 24 + h : 25 + h]
            stats = jnp.where(lane == h, row_dot * cols[:, 16 + h : 17 + h], stats)
            stats = jnp.where(lane == 8 + h, d_self, stats)
    turned = stats.T
    pay_ref[128:136, 0:128] = best
    pay_ref[128:136, 128:256] = turned[0:8]
    pay_ref[128:136, 256:512] = jnp.zeros((8, 256), F32)
    dself_ref[...] = turned[8:16]


def backward_body(
    blocks, counts, spot, panel, p_ref, att_ref, group, masks, pay_ref, self_ref, dself_ref,
    dx_out, w_out, ddst_out, p_cat, hb, gn, gt, top, abc, dots, ddst, dsrc, dh, p_wide, att_wide,
    dx_slots, dx_sems, dp_out, group_sems, a_ref, x_ref, mask_ref, sems,
):
    arrive = stream_in(panel, x_ref, masks, mask_ref, group, a_ref, sems)
    split_weights(p_ref, p_cat)
    prepare_features(x_ref, p_cat, hb, arrive)
    pltpu.make_async_copy(masks, mask_ref, sems.at[8]).wait()
    pltpu.make_async_copy(group.at[:, pl.ds(128, 8), pl.ds(128, 128)], a_ref, sems.at[9]).wait()
    even = (lax.broadcasted_iota(jnp.int32, (128, 1), 0) < 64).astype(F32)
    odd = 1.0 - even

    def setup(b, carry):
        dots[b] = columns_of(pay_ref[b, 128:136, 128:256])
        for pair in range(4):
            grad = pay_ref[b, 0:128, 128 * pair : 128 * pair + 128]
            high, low = split(grad)
            gn[b, pair, :, 0:128] = high
            gn[b, pair, :, 128:256] = low
            turned = grad.T
            e_high, e_low = split(turned * even)
            o_high, o_low = split(turned * odd)
            gt[b, pair, :, 0:128] = e_high
            gt[b, pair, :, 128:256] = o_high
            gt[b, pair, :, 256:384] = e_low
            gt[b, pair, :, 384:512] = o_low
        return carry

    lax.fori_loop(0, 8, setup, 0)

    def put(kind, b, h, tile):
        (abc, top)[kind][b * 8 + h] = tile

    spread_rows(lambda b: [a_ref[b], pay_ref[b, 128:136, 0:128]], put)
    ddst[...] = jnp.zeros(ddst.shape, F32)
    dsrc[...] = jnp.zeros(dsrc.shape, F32)
    dh[...] = jnp.zeros(dh.shape, F32)
    dh[spot[0]] = self_ref[...]

    def step(k, carry):
        b, c = blocks[2 * k], blocks[2 * k + 1]
        keep = mask_ref[k] > 0
        scores = x_ref[c, 128:136, 0:128]
        cols = dots[b]
        for pair in range(4):
            g_high, g_low = gn[b, pair, :, 0:128], gn[b, pair, :, 128:256]
            h_high, h_low = hb[c, pair, 0:256], hb[c, pair, 256:512]
            d_alpha = dot(
                jnp.concatenate([g_high, g_high, g_low], axis=1),
                jnp.concatenate([h_high, h_low, h_high], axis=1),
                NT,
            )
            highs, lows = [], []
            for side in range(2):
                h = 2 * pair + side
                raw = abc[b * 8 + h] + jnp.where(keep, scores[h : h + 1], NEG)
                w = jnp.exp2(leaky(raw) - top[b * 8 + h])
                d_raw = w * (d_alpha[:, 128 * side : 128 * side + 128] - cols[:, h : h + 1])
                d_raw = jnp.where(raw > 0, d_raw, 0.2 * d_raw)
                ddst[b * 8 + h] += d_raw
                dsrc[c * 8 + h] += jnp.sum(d_raw.reshape(16, 8, 128), axis=0)
                high, low = split(w)
                highs.append(high)
                lows.append(low)
            left = jnp.concatenate([gt[b, pair], gt[b, pair, :, 0:256]], axis=1)
            right = jnp.concatenate(highs + highs + lows, axis=0)
            dh[c, 128 * pair : 128 * pair + 128] += dot(left, right)
        return carry

    lax.fori_loop(0, counts[0], step, 0)

    def group_half(b, side):
        part = group.at[b, pl.ds(0, 128), pl.ds(128 * side, 128)]
        return pltpu.make_async_copy(part, abc.at[2 * b + side], group_sems.at[2 * b + side])

    for b in range(8):
        for side in range(2):
            group_half(b, side).start()

    def pack_dst(b, carry):
        ddst_out[b] = jnp.concatenate(
            [jnp.sum(ddst[b * 8 + h].T, axis=0, keepdims=True) for h in range(8)], axis=0
        )
        return carry

    lax.fori_loop(0, 8, pack_dst, 0)
    ddst_out[spot[1]] += dself_ref[...]

    high, low = split(p_ref[...])
    p_wide[:, 0:512] = high
    p_wide[:, 512:1024] = low
    p_wide[:, 1024:1536] = high
    att_cols = columns_of(jnp.concatenate([att_ref[...], jnp.zeros((8, 64), F32)], axis=1))
    for h in range(8):
        att_wide[64 * h : 64 * h + 64] = jnp.broadcast_to(att_cols[0:64, h : h + 1], (64, 128))
    dp_out[...] = jnp.zeros(dp_out.shape, F32)
    own = spot[0]

    def leave(four, slot):
        return pltpu.make_async_copy(dx_slots.at[slot], dx_out.at[pl.ds(4 * four, 4)], dx_sems.at[slot])

    def project(four, carry):
        wide_dh, wide_src = [], []
        for s in range(4):
            c = 4 * four + s
            d_src = jnp.concatenate(
                [jnp.sum(dsrc[c * 8 + h], axis=0, keepdims=True) for h in range(8)], axis=0
            )
            d_src = d_src + jnp.where(c == own, dself_ref[...], 0.0)
            spread = jnp.concatenate(
                [att_wide[64 * h : 64 * h + 64] * d_src[h : h + 1] for h in range(8)], axis=0
            )
            wide_dh.append(dh[c] + spread)
            wide_src.append(jnp.concatenate([d_src, jnp.zeros((8, 128), F32)], axis=0))
        high, low = split(jnp.concatenate(wide_dh, axis=1))
        s_high, s_low = split(jnp.concatenate(wide_src, axis=1))
        x_high, x_low = split(jnp.concatenate([x_ref[4 * four + s, 0:128] for s in range(4)], axis=0))
        dx = dot(p_wide[...], jnp.concatenate([high, high, low], axis=0))
        slot = lax.rem(four, 2)

        @pl.when(four >= 2)
        def _():
            leave(four - 2, slot).wait()

        for s in range(4):
            dx_slots[slot, s] = dx[:, 128 * s : 128 * s + 128]
        leave(four, slot).start()
        tall_high = jnp.concatenate([high, s_high], axis=0)
        tall_low = jnp.concatenate([low, s_low], axis=0)
        dp_out[...] += dot(
            jnp.concatenate([tall_high, tall_high, tall_low], axis=1),
            jnp.concatenate([x_high, x_low, x_high], axis=0),
        )
        return carry

    lax.fori_loop(0, 8, project, 0)
    u = jnp.zeros((8, 256), F32)
    for b in range(8):
        for side in range(2):
            group_half(b, side).wait()
        u += dot(ddst_out[b], jnp.concatenate([abc[2 * b], abc[2 * b + 1]], axis=1), NN, HIGHEST)
    for i in range(32):
        w_out[i, 0:16] = dp_out[16 * i : 16 * i + 16, 0:128]
        w_out[i, 16:32] = dp_out[16 * i : 16 * i + 16, 128:256]
        w_out[i, 32:48] = jnp.zeros((16, 128), F32)
    for h in range(8):
        for side in range(2):
            span = slice(128 * side, 128 * side + 128)
            w_out[h + 16 * side, 32:33] = u[h : h + 1, span]
            w_out[8 + h + 16 * side, 32:33] = dp_out[512 + h : 513 + h, span]
    leave(6, 0).wait()
    leave(7, 1).wait()


def backward_local(blocks, counts, spot, panel, proj, att_src, group, masks, pays, dh_self, d_self):
    return pl.pallas_call(
        backward_body,
        out_shape=(
            jax.ShapeDtypeStruct((32, 256, 128), F32),
            jax.ShapeDtypeStruct((32, 48, 128), F32),
            jax.ShapeDtypeStruct((8, 8, 128), F32),
        ),
        in_specs=[SMEM] * 3 + [ANY, VMEM, VMEM, ANY, ANY, VMEM, VMEM, VMEM],
        out_specs=(ANY, VMEM, VMEM),
        scratch_shapes=[
            pltpu.VMEM((768, 512), BF16),
            pltpu.VMEM((32, 4, 512, 128), BF16),
            pltpu.VMEM((8, 4, 128, 256), BF16),
            pltpu.VMEM((8, 4, 128, 512), BF16),
            pltpu.VMEM((64, 128, 128), F32),
            pltpu.VMEM((64, 128, 128), F32),
            pltpu.VMEM((8, 128, 128), F32),
            pltpu.VMEM((64, 128, 128), F32),
            pltpu.VMEM((256, 8, 128), F32),
            pltpu.VMEM((32, 512, 128), F32),
            pltpu.VMEM((256, 1536), BF16),
            pltpu.VMEM((512, 128), F32),
            pltpu.VMEM((2, 4, 256, 128), F32),
            pltpu.SemaphoreType.DMA((2,)),
            pltpu.VMEM((528, 256), F32),
            pltpu.SemaphoreType.DMA((16,)),
            pltpu.VMEM((8, 8, 128), F32),
            pltpu.VMEM((32, 136, 256), F32),
            pltpu.VMEM((32, 128, 128), jnp.int32),
            pltpu.SemaphoreType.DMA((10,)),
        ],
        compiler_params=pltpu.CompilerParams(vmem_limit_bytes=BIG_VMEM),
    )(blocks, counts, spot, panel, proj, att_src, group, masks, pays, dh_self, d_self)


def reduce_body(
    dx_ref, w_ref, ddst_ref, dx_out, dp_out, dst_out,
    send, recv, twin_dx, twin_w, total, far, near, far2, near2, dst_all, joined, tower,
):
    d, y, x, k, z = place()
    sibling = node(y, x, 1 - k)
    chip = y * 4 + x
    offsets = [(dy, dx) for dy in range(4) for dx in range(4) if (dy, dx) != (0, 0)]
    others = [lax.rem(z + s, 8) for s in range(1, 8)]
    wait_all = greet([sibling] + [node(y + dy, x + dx, k) for dy, dx in offsets], others)
    links = Links(send, recv)
    wait_all()

    def rank(offset):
        return 0 if 2 in offset else (2 if offset == (0, 0) else 1)

    cells = sorted([(0, 0)] + offsets, key=rank)
    twin_weights = links.push(w_ref.at[:, :, 1 - k], twin_w, dst=sibling)
    twin_copies = {}
    for dy, dx in cells:
        yy, xx = lax.rem(y + dy, 4), lax.rem(x + dx, 4)
        twin_copies[dy, dx] = links.push(dx_ref.at[yy, xx, 1 - k], twin_dx.at[yy, xx], dst=sibling)
    dst_copies = [links.push(ddst_ref.at[t], dst_all.at[z], src=t) for t in others]
    twin_weights.wait_recv()

    def add_cells(wanted):
        for dy, dx in cells:
            if rank((dy, dx)) != wanted:
                continue
            yy, xx = lax.rem(y + dy, 4), lax.rem(x + dx, 4)
            twin_copies[dy, dx].wait_recv()
            total[yy, xx, 0:128] = dx_ref[yy, xx, k, 0:128] + twin_dx[yy, xx, 0:128]
            total[yy, xx, 128:152] = w_ref[yy, xx, k, 0:24] + twin_w[yy, xx, 0:24]
            total[yy, xx, 152:280] = dx_ref[yy, xx, k, 128:256] + twin_dx[yy, xx, 128:256]
            total[yy, xx, 280:304] = w_ref[yy, xx, k, 24:48] + twin_w[yy, xx, 24:48]

    def ring(region, plus, minus, far_buf, near_buf):
        c0 = links.push(region(2, 0), far_buf(0, 0), dst=plus)
        c1 = links.push(region(2, 1), far_buf(1, 1), dst=minus)
        yield
        c2 = links.push(region(1, 1), near_buf(0, 1), dst=plus)
        c3 = links.push(region(-1, 0), near_buf(1, 0), dst=minus)
        yield
        c0.wait_recv()
        part = region(1, 0)
        part[...] += far_buf(0, 0)[...]
        c4 = links.push(part, near_buf(2, 0), dst=plus)
        yield
        c1.wait_recv()
        part = region(-1, 1)
        part[...] += far_buf(1, 1)[...]
        c5 = links.push(part, near_buf(3, 1), dst=minus)
        yield
        for copy, index, piece in ((c2, 0, 1), (c3, 1, 0), (c4, 2, 0), (c5, 3, 1)):
            yield
            copy.wait_recv()
            part = region(0, piece)
            part[...] += near_buf(index, piece)[...]

    def grads(half):
        rows = pl.ds(152 * half, 152)

        def wide(v, piece):
            if half == 0:
                return total.at[lax.rem(y + v + 4, 4), pl.ds(2 * piece, 2), rows]
            return total.at[pl.ds(2 * piece, 2), lax.rem(x + v + 4, 4), rows]

        def narrow(u, piece):
            span = pl.ds(152 * half + 80 * piece, 80 - 8 * piece)
            if half == 0:
                return total.at[y, lax.rem(x + u + 4, 4), span]
            return total.at[lax.rem(y + u + 4, 4), x, span]

        def short(buffer):
            return lambda index, piece: buffer.at[half, index, pl.ds(0, 80 - 8 * piece)]

        along_y = (node(y + 1, x, k), node(y - 1, x, k))
        along_x = (node(y, x + 1, k), node(y, x - 1, k))
        first, then = (along_y, along_x) if half == 0 else (along_x, along_y)
        yield from ring(wide, *first, lambda i, p: far.at[half, i], lambda i, p: near.at[half, i])
        yield from ring(narrow, *then, short(far2), short(near2))

    chains = [grads(0), grads(1)]
    for wanted in range(3):
        add_cells(wanted)
        if wanted < 2:
            for chain in chains:
                next(chain)
    run_chains(chains)

    joined[0:24] = total[y, x, 128:152]
    joined[24:40] = total[y, x, 280:296]
    tower[z] = joined[...]
    coming = [links.push(joined, tower.at[z], src=t) for t in others]
    dx_out[0:128] = total[y, x, 0:128]
    dx_out[128:256] = total[y, x, 152:280]
    for copy in dst_copies:
        copy.wait_recv()
    dst_all[z] = ddst_ref[z]
    dst_total = dst_all[0]
    for t in range(1, 8):
        dst_total = dst_total + dst_all[t]
    dst_out[...] = dst_total
    for copy in coming:
        copy.wait_recv()
    value = tower[0]
    for i in range(1, 8):
        value = value + tower[i]
    dp_out[chip, k] = value
    coming = [
        links.push(dp_out.at[chip, k], dp_out.at[chip, k], dst=node(y + dy, x + dx, k)) for dy, dx in offsets
    ]
    for copy in coming:
        copy.wait_recv()
    over = links.push(dp_out.at[:, k], dp_out.at[:, k], dst=sibling)
    over.wait_recv()
    links.drain()


def reduce_grads(dx, w, ddst):
    count = 1 + 16 + 7 + 24 + 7 + 15 + 1
    return pl.pallas_call(
        reduce_body,
        out_shape=(
            jax.ShapeDtypeStruct((256, 128), F32),
            jax.ShapeDtypeStruct((16, 2, 40, 128), F32),
            jax.ShapeDtypeStruct((8, 128), F32),
        ),
        in_specs=[VMEM] * 3,
        out_specs=(VMEM,) * 3,
        scratch_shapes=[
            pltpu.SemaphoreType.DMA((count,)),
            pltpu.SemaphoreType.DMA((count,)),
            pltpu.VMEM((4, 4, 256, 128), F32),
            pltpu.VMEM((4, 4, 48, 128), F32),
            pltpu.VMEM((4, 4, 304, 128), F32),
            pltpu.VMEM((2, 2, 2, 152, 128), F32),
            pltpu.VMEM((2, 4, 2, 152, 128), F32),
            pltpu.VMEM((2, 2, 80, 128), F32),
            pltpu.VMEM((2, 4, 80, 128), F32),
            pltpu.VMEM((8, 8, 128), F32),
            pltpu.VMEM((40, 128), F32),
            pltpu.VMEM((8, 40, 128), F32),
        ],
        compiler_params=pltpu.CompilerParams(
            collective_id=2, has_side_effects=True, vmem_limit_bytes=BIG_VMEM
        ),
    )(dx.reshape(4, 4, 2, 256, 128), w.reshape(4, 4, 2, 48, 128), ddst)


def finish_body(dx_ref, w_ref, dst_ref, p_ref, dst_att_ref, in_ref, proj_ref, src_ref, dst_out):
    proj = p_ref[...]
    a_rows = per_head_rows(dst_att_ref[...])
    score = dot(a_rows, proj, NT, HIGHEST)
    pad = jnp.zeros((120, 256), F32)
    score_t = jnp.concatenate([score, pad], axis=0).T
    dst_wide = jnp.concatenate([dst_ref[...], jnp.zeros((120, 128), F32)], axis=0)
    in_ref[...] = (dx_ref[...] + dot(score_t, dst_wide, NN, HIGHEST)).T

    def row(i):
        return jnp.concatenate([w_ref[i, 32:33], w_ref[i + 16, 32:33]], axis=1)

    u = jnp.concatenate([row(h) for h in range(8)], axis=0)
    v = jnp.concatenate([row(8 + h) for h in range(8)], axis=0)
    wide_u = jnp.concatenate([u, jnp.zeros((120, 256), F32)], axis=0)
    att = jnp.concatenate([a_rows, jnp.zeros((120, 512), F32)], axis=0)
    grad_t = jnp.concatenate(
        [jnp.concatenate([w_ref[i, 0:16], w_ref[i, 16:32]], axis=1) for i in range(32)], axis=0
    )
    proj_ref[...] = (grad_t + dot(att.T, wide_u, NN, HIGHEST)).T
    both = dot(jnp.concatenate([u, v], axis=0), proj, NN, HIGHEST)
    dst_out[...] = jnp.concatenate([both[h : h + 1, 64 * h : 64 * h + 64] for h in range(8)], axis=0)
    src_ref[...] = jnp.concatenate([both[8 + h : 9 + h, 64 * h : 64 * h + 64] for h in range(8)], axis=0)


def finish(dx, weights, dst_total, proj, att_dst):
    return pl.pallas_call(
        finish_body,
        out_shape=(
            jax.ShapeDtypeStruct((128, 256), F32),
            jax.ShapeDtypeStruct((256, 512), F32),
            jax.ShapeDtypeStruct((8, 64), F32),
            jax.ShapeDtypeStruct((8, 64), F32),
        ),
        in_specs=[VMEM] * 5,
        out_specs=(VMEM,) * 4,
    )(dx, weights.reshape(32, 40, 128), dst_total, proj, att_dst)


def shards(inputs, projection, att_src, att_dst, blocks, counts, tile_masks, cotangent):
    coords = blocks.reshape(64)
    live = counts.reshape(1)
    masks = tile_masks[0, 0]
    spot = jnp.stack([lax.axis_index("dst"), lax.axis_index("src")]).astype(jnp.int32)
    panel, group, own = gather_inputs(inputs, projection, att_src, att_dst)
    acc = forward_local(coords, live, panel, projection, group, masks)
    output, pays, dh_self, d_self = exchange(acc, inputs, projection, own, cotangent)
    dx, w, ddst = backward_local(
        coords, live, spot, panel, projection, att_src, group, masks, pays, dh_self, d_self
    )
    dx_own, weights, dst_total = reduce_grads(dx, w, ddst)
    in_grad, proj_grad, src_grad, dst_grad = finish(dx_own, weights, dst_total, projection, att_dst)
    return (output, in_grad, proj_grad, src_grad, dst_grad)


def solution(mesh):
    in_specs = (
        P(("dst", "src"), None),
        P(),
        P(),
        P(),
        P("dst", "src", None, None),
        P("dst", "src"),
        P("dst", "src", None, None, None),
        P(("dst", "src"), None),
    )
    out_specs = (P(("dst", "src"), None), P(("dst", "src"), None), P(), P(), P())
    return jax.shard_map(shards, mesh=mesh, in_specs=in_specs, out_specs=out_specs, check_vma=False)
```

```python
import functools

import jax
import jax.numpy as jnp
from jax import lax
from jax.experimental import pallas as pl
from jax.experimental.pallas import tpu as pltpu
from jax.sharding import PartitionSpec as P

HIGHEST = lax.Precision.HIGHEST
F32 = jnp.float32
BF16 = jnp.bfloat16
LOG2E = 1.4426950408889634
NEG = -1e30
MESH = pl.DeviceIdType.MESH
VMEM = pl.BlockSpec(memory_space=pltpu.VMEM)
SMEM = pl.BlockSpec(memory_space=pltpu.SMEM)
ANY = pl.BlockSpec(memory_space=pl.ANY)
NN = (((1,), (0,)), ((), ()))
NT = (((1,), (1,)), ((), ()))
BIG_VMEM = 60 * 1024 * 1024


def dot(a, b, dims=NN, precision=None):
    return lax.dot_general(a, b, dims, precision=precision, preferred_element_type=F32)


def split(value):
    high = value.astype(BF16)
    return high, (value - high.astype(F32)).astype(BF16)


def leaky(raw):
    return jnp.maximum(raw, 0.2 * raw)


def per_head_rows(att):
    wide = jnp.concatenate([att] * 8, axis=1)
    head = lax.broadcasted_iota(jnp.int32, wide.shape, 0)
    column = lax.broadcasted_iota(jnp.int32, wide.shape, 1)
    return jnp.where(column // 64 == head, wide, 0.0)


def score_rows(att, proj):
    return dot(per_head_rows(att), proj, NT, HIGHEST)


def lanes(shape):
    return lax.broadcasted_iota(jnp.int32, shape, len(shape) - 1)


def place():
    d = lax.axis_index("dst")
    z = lax.axis_index("src")
    return d, d // 8, lax.rem(d // 2, 4), lax.rem(d, 2), z


def node(y, x, k):
    return lax.rem(y + 8, 4) * 8 + lax.rem(x + 8, 4) * 2 + k


class Links:
    def __init__(self, send, recv):
        self.send, self.recv, self.used, self.open = send, recv, 0, []

    def push(self, source, landing, **target):
        copy = pltpu.make_async_remote_copy(
            src_ref=source,
            dst_ref=landing,
            send_sem=self.send.at[self.used],
            recv_sem=self.recv.at[self.used],
            device_id=target,
            device_id_type=MESH,
        )
        self.used += 1
        copy.start()
        self.open.append(copy)
        return copy

    def drain(self):
        for copy in self.open:
            copy.wait_send()


def greet(dsts, srcs):
    barrier = pltpu.get_barrier_semaphore()
    for other in dsts:
        pl.semaphore_signal(barrier, inc=1, device_id={"dst": other}, device_id_type=MESH)
    for other in srcs:
        pl.semaphore_signal(barrier, inc=1, device_id={"src": other}, device_id_type=MESH)
    return lambda: pl.semaphore_wait(barrier, len(dsts) + len(srcs))


def run_chains(chains):
    chains = list(chains)
    while chains:
        for chain in list(chains):
            try:
                next(chain)
            except StopIteration:
                chains.remove(chain)


def around(links, own_ref, all_ref, z):
    spans = (pl.ds(0, 64), pl.ds(64, 72))
    right, left = lax.rem(z + 1, 8), lax.rem(z + 7, 8)

    def push(step, way, sub):
        block = lax.rem(z + 8 - step, 8) if way == 0 else lax.rem(z + step, 8)
        part = all_ref.at[block, spans[sub]]
        source = own_ref.at[spans[sub]] if step == 0 else part
        return links.push(source, part, src=right if way == 0 else left)

    order = [(way, sub) for sub in range(2) for way in range(2)]
    coming = {item: push(0, *item) for item in order}
    for step in range(1, 4):
        for item in order:
            yield
            coming[item].wait_recv()
            if step < 3 or item[0] == item[1]:
                coming[item] = push(step, *item)
            else:
                del coming[item]
    for copy in list(coming.values()):
        yield
        copy.wait_recv()


def gather_body(x_ref, p_ref, src_ref, dst_ref, panel_ref, group_ref, own_ref, pay, send, recv, own_sem):
    d, y, x, k, z = place()
    sibling = node(y, x, 1 - k)
    wait_all = greet(
        [sibling, node(y + 1, x, k), node(y - 1, x, k), node(y, x + 1, k), node(y, x - 1, k)],
        [lax.rem(z + 1, 8), lax.rem(z + 7, 8)],
    )
    rows = jnp.concatenate([score_rows(r[...], p_ref[...]) for r in (src_ref, dst_ref)], axis=0) * LOG2E
    scores = dot(rows, x_ref[...], NT, HIGHEST)
    pay[0:128] = x_ref[...]
    pay[128:136, 0:128] = scores[0:8]
    pay[128:136, 128:256] = scores[8:16]
    own_ref[...] = scores
    own_copies = [
        pltpu.make_async_copy(pay, panel_ref.at[d], own_sem.at[0]),
        pltpu.make_async_copy(pay, group_ref.at[z], own_sem.at[1]),
    ]
    for copy in own_copies:
        copy.start()
    wait_all()
    links = Links(send, recv)

    def chain(half):
        def at(u, v):
            return node(y + v, x + u, k) if half == 0 else node(y + u, x + v, k)

        def region(u, v, quarter=None):
            start, size = 64 * half, 64 + 8 * half
            if quarter is not None:
                start, size = start + 32 * quarter, 32 + 8 * half * quarter
            return panel_ref.at[at(u, v), pl.ds(start, size)]

        def to(part, du, dv, src=None):
            return links.push(part if src is None else src, part, dst=at(du, dv))

        def twin(u, v, src=None):
            part = region(u, v)
            return links.push(part if src is None else src, part, dst=sibling)

        own = pay.at[pl.ds(64 * half, 64 + 8 * half)]
        first = [to(region(0, 0), 1, 0, own), to(region(0, 0), -1, 0, own)]
        second = {0: [to(region(0, 0), 0, 1, own), to(region(0, 0), 0, -1, own)]}
        twins = [twin(0, 0, own)]
        last = {}

        def spread(u):
            second[u] = [to(region(u, 0), 0, 1), to(region(u, 0), 0, -1)]
            twins.append(twin(u, 0))

        def relay(u):
            pair = []
            for index, v in ((0, -1), (1, 1)):
                yield
                second[u][index].wait_recv()
                pair.append(to(region(u, v, index), 0, -v))
                twins.append(twin(u, v))
            last[u] = pair

        def finish(u):
            yield
            for copy in last[u]:
                copy.wait_recv()
            twins.append(twin(u, 2))

        far = []
        for index, u in ((0, -1), (1, 1)):
            yield
            first[index].wait_recv()
            far.append(to(region(u, 0, index), -u, 0))
            spread(u)
        yield from relay(0)
        yield
        for copy in far:
            copy.wait_recv()
        spread(2)
        yield from relay(-1)
        yield from relay(1)
        yield from finish(0)
        yield from relay(2)
        yield from finish(-1)
        yield from finish(1)
        yield from finish(2)
        yield
        for copy in twins:
            copy.wait_recv()

    run_chains([chain(0), chain(1), around(links, pay, group_ref, z)])
    for copy in own_copies:
        copy.wait()
    links.drain()


def gather_inputs(x, proj, att_src, att_dst):
    count = 72 + 14
    return pl.pallas_call(
        gather_body,
        out_shape=(
            jax.ShapeDtypeStruct((32, 136, 256), F32),
            jax.ShapeDtypeStruct((8, 136, 256), F32),
            jax.ShapeDtypeStruct((16, 128), F32),
        ),
        in_specs=[VMEM] * 4,
        out_specs=(ANY, ANY, VMEM),
        scratch_shapes=[
            pltpu.VMEM((136, 256), F32),
            pltpu.SemaphoreType.DMA((count,)),
            pltpu.SemaphoreType.DMA((count,)),
            pltpu.SemaphoreType.DMA((2,)),
        ],
        compiler_params=pltpu.CompilerParams(collective_id=0, has_side_effects=True),
    )(x, proj, att_src, att_dst)


def split_weights(p_ref, p_cat):
    high, low = split(p_ref[...])
    p_cat[0:256] = high
    p_cat[256:512] = low
    p_cat[512:768] = high


def stream_in(panel, x_ref, masks, mask_ref, group, a_ref, sems):
    def part(i):
        span = pl.ds(4 * i, 4)
        return pltpu.make_async_copy(panel.at[span], x_ref.at[span], sems.at[i])

    for i in range(8):
        part(i).start()
    pltpu.make_async_copy(masks, mask_ref, sems.at[8]).start()
    pltpu.make_async_copy(group.at[:, pl.ds(128, 8), pl.ds(128, 128)], a_ref, sems.at[9]).start()
    return part


def prepare_features(x_ref, p_cat, hb, arrive, leave):
    n = 4

    def step(group, carry):
        arrive(group).wait()
        x_high, x_low = split(jnp.concatenate([x_ref[group * n + s, 0:128] for s in range(n)], axis=0))
        left = jnp.concatenate([x_high, x_high, x_low], axis=1)
        for wide in range(2):
            h_high, h_low = split(dot(left, p_cat[:, 256 * wide : 256 * wide + 256]))
            for s in range(n):
                for side in range(2):
                    part = (slice(128 * s, 128 * s + 128), slice(128 * side, 128 * side + 128))
                    pair = 2 * wide + side
                    hb[group * n + s, pair, 0:128] = h_high[part]
                    hb[group * n + s, pair, 128:256] = h_low[part]
        leave(group).start()
        return carry

    lax.fori_loop(0, 32 // n, step, 0)


def columns_of(rows):
    pad = jnp.zeros((128 - rows.shape[0], 128), F32)
    return jnp.concatenate([rows, pad], axis=0).T


def spread_rows(rows_of, put):
    parts = []
    for b in range(8):
        kinds = rows_of(b)
        pieces = []
        for rows in kinds:
            high = rows.astype(BF16).astype(F32)
            middle = (rows - high).astype(BF16).astype(F32)
            pieces += [high, middle, rows - high - middle]
        parts.append(columns_of(jnp.concatenate(pieces, axis=0)).astype(BF16))
    left = jnp.concatenate(parts, axis=0)
    count = len(kinds)
    row = lax.broadcasted_iota(jnp.int32, (128, 128 * count), 0)
    kind = lax.broadcasted_iota(jnp.int32, (128, 128 * count), 1) // 128
    for h in range(8):
        pick = jnp.logical_and(row // 24 == kind, lax.rem(row, 8) == h)
        out = dot(left, jnp.where(pick, 1.0, 0.0).astype(BF16))
        for k in range(count):
            for b in range(8):
                put(k, b, h, out[128 * b : 128 * b + 128, 128 * k : 128 * k + 128])


SPAN = 40.0


def peaks(scores):
    high, low = scores[0], scores[0]
    for c in range(1, 32):
        high, low = jnp.maximum(high, scores[c]), jnp.minimum(low, scores[c])
    high, low = jnp.max(high, axis=1, keepdims=True), jnp.min(low, axis=1, keepdims=True)
    return high, jnp.max(high - low)


def source_factors(scores, high, factors):
    for c in range(32):
        below = scores[c] - high
        factors[c, 0:8] = jnp.exp2(below)
        factors[c, 8:16] = jnp.exp2(0.2 * below)


def target_factors(a, high, shift):
    best = a + high
    return [jnp.exp2(jnp.minimum(part - shift, 100.0)) for part in (best, 0.2 * best)]


def forward_body(
    blocks, counts, panel, p_ref, group, masks, acc_out, hb_out, b_out,
    p_cat, hb, top, abc, sums, acc, top_rows, factors, hb_sems, a_ref, x_ref, mask_ref, sems
):
    arrive = stream_in(panel, x_ref, masks, mask_ref, group, a_ref, sems)

    def leave(i):
        span = pl.ds(4 * i, 4)
        return pltpu.make_async_copy(hb.at[span], hb_out.at[span], hb_sems.at[i])

    split_weights(p_ref, p_cat)
    prepare_features(x_ref, p_cat, hb, arrive, leave)
    pltpu.make_async_copy(masks, mask_ref, sems.at[8]).wait()
    pltpu.make_async_copy(group.at[:, pl.ds(128, 8), pl.ds(128, 128)], a_ref, sems.at[9]).wait()
    b_out[...] = x_ref[:, 128:136, 0:128]
    sums[...] = jnp.zeros(sums.shape, F32)
    acc[...] = jnp.zeros(acc.shape, F32)
    live = counts[0]
    high, reach = peaks(b_out)
    close = reach < SPAN

    def put(kind, b, h, tile):
        (abc, top)[kind][b * 8 + h] = tile

    def accumulate(weight):
        lane = lanes((128, 128))

        def step(k, carry):
            b, c = blocks[2 * k], blocks[2 * k + 1]
            keep = mask_ref[k] > 0
            for pair in range(4):
                sides = []
                for h in (2 * pair, 2 * pair + 1):
                    w = weight(b, c, h, keep)
                    sums[b * 8 + h] += w
                    w_high, w_low = split(w)
                    sides.append(jnp.concatenate([w_high, w_high, w_low], axis=1))
                right = jnp.concatenate([hb[c, pair], hb[c, pair, 0:128]], axis=0)
                both = dot(jnp.concatenate(sides, axis=0), right)
                acc[b * 4 + pair] += jnp.where(lane < 64, both[0:128], both[128:256])
            return carry

        lax.fori_loop(0, live, step, 0)

    @pl.when(close)
    def _():
        source_factors(b_out, high, factors)
        for b in range(8):
            top_rows[b] = leaky(a_ref[b] + high)
        spread_rows(lambda b: target_factors(a_ref[b], high, top_rows[b]), put)

        def weight(b, c, h, keep):
            one = abc[b * 8 + h] * factors[c, pl.ds(h, 1)]
            two = top[b * 8 + h] * factors[c, pl.ds(8 + h, 1)]
            return jnp.where(keep, jnp.maximum(one, two), 0.0)

        accumulate(weight)

    @pl.when(jnp.logical_not(close))
    def _():
        top[...] = jnp.full(top.shape, NEG, F32)

        def find_top(k, carry):
            b, c = blocks[2 * k], blocks[2 * k + 1]
            keep = mask_ref[k] > 0
            for h in range(8):
                top[b * 8 + h] = jnp.maximum(top[b * 8 + h], jnp.where(keep, b_out[c, pl.ds(h, 1)], NEG))
            return carry

        lax.fori_loop(0, live, find_top, 0)

        def find_rows(b, carry):
            best = jnp.concatenate([jnp.max(top[b * 8 + h].T, axis=0, keepdims=True) for h in range(8)], axis=0)
            top_rows[b] = leaky(a_ref[b] + best)
            return carry

        lax.fori_loop(0, 8, find_rows, 0)
        spread_rows(lambda b: [a_ref[b], top_rows[b]], put)

        def weight(b, c, h, keep):
            raw = abc[b * 8 + h] + jnp.where(keep, b_out[c, pl.ds(h, 1)], NEG)
            return jnp.exp2(leaky(raw) - top[b * 8 + h])

        accumulate(weight)

    def pack(b, carry):
        totals = [jnp.sum(sums[b * 8 + h].T, axis=0, keepdims=True) for h in range(8)]
        tops = [
            jnp.where(totals[h] > 0, top_rows[b, h : h + 1], 0.2 * NEG) for h in range(8)
        ]
        for way in range(2):
            for inner in range(2):
                h = 4 * way + 2 * inner
                packed = jnp.concatenate(
                    tops[h : h + 2] + totals[h : h + 2] + [jnp.zeros((4, 128), F32)], axis=0
                )
                for half in range(2):
                    sub = 2 * inner + half
                    acc_out[b, way, sub, 0:64] = acc[b * 4 + 2 * way + inner][64 * half : 64 * half + 64]
                    acc_out[b, way, sub, 64:72] = packed
        return carry

    lax.fori_loop(0, 8, pack, 0)
    for i in range(8):
        leave(i).wait()


def forward_local(blocks, counts, panel, proj, group, masks):
    return pl.pallas_call(
        forward_body,
        out_shape=(
            jax.ShapeDtypeStruct((8, 2, 4, 72, 128), F32),
            jax.ShapeDtypeStruct((32, 4, 256, 128), BF16),
            jax.ShapeDtypeStruct((32, 8, 128), F32),
        ),
        in_specs=[SMEM, SMEM, ANY, VMEM, ANY, ANY],
        out_specs=(VMEM, ANY, VMEM),
        scratch_shapes=[
            pltpu.VMEM((768, 512), BF16),
            pltpu.VMEM((32, 4, 256, 128), BF16),
            pltpu.VMEM((64, 128, 128), F32),
            pltpu.VMEM((64, 128, 128), F32),
            pltpu.VMEM((64, 128, 128), F32),
            pltpu.VMEM((32, 128, 128), F32),
            pltpu.VMEM((8, 8, 128), F32),
            pltpu.VMEM((32, 16, 128), F32),
            pltpu.SemaphoreType.DMA((8,)),
            pltpu.VMEM((8, 8, 128), F32),
            pltpu.VMEM((32, 136, 256), F32),
            pltpu.VMEM((32, 128, 128), jnp.int32),
            pltpu.SemaphoreType.DMA((10,)),
        ],
        compiler_params=pltpu.CompilerParams(vmem_limit_bytes=BIG_VMEM),
    )(blocks, counts, panel, proj, group, masks)


def merge(arrived, mine, half):
    one, two = arrived[64:72], mine[64:72]
    best = jnp.maximum(one[0:2], two[0:2])
    f_one, f_two = jnp.exp2(one[0:2] - best), jnp.exp2(two[0:2] - best)
    total = one[2:4] * f_one + two[2:4] * f_two
    cols = columns_of(jnp.concatenate([f_one, f_two, best, total], axis=0))[64 * half : 64 * half + 64]
    lane = lanes((64, 128))
    factor = [jnp.where(lane < 64, cols[:, s : s + 1], cols[:, s + 1 : s + 2]) for s in (0, 2)]
    values = arrived[0:64] * factor[0] + mine[0:64] * factor[1]
    return values, jnp.concatenate([best, total, one[4:8]], axis=0)


def exchange_body(
    acc_ref, x_ref, p_ref, own_ref, cot_ref, out_ref, all_ref, self_ref, dself_ref,
    slots, total, pay, h_own, send, recv, grad_send, grad_recv, own_sem,
):
    z = lax.axis_index("src")
    right, left = lax.rem(z + 1, 8), lax.rem(z + 7, 8)
    wait_all = greet([], [right, left])
    wait_all()

    def copy(step, way, sub):
        if isinstance(step, int) and step == 0:
            src = acc_ref.at[left if way == 0 else right, way, sub]
        else:
            src = slots.at[step - 1, way, sub]
        return pltpu.make_async_remote_copy(
            src_ref=src,
            dst_ref=slots.at[step, way, sub],
            send_sem=send.at[step, way, sub],
            recv_sem=recv.at[step, way, sub],
            device_id={"src": right if way == 0 else left},
            device_id_type=MESH,
        )

    order = [(way, sub) for sub in range(4) for way in range(2)]
    for way, sub in order:
        copy(0, way, sub).start()
    h_own[...] = dot(x_ref[...], p_ref[...], NN, HIGHEST)

    def block_of(step, way):
        return lax.rem(z + 15 - step, 8) if way == 0 else lax.rem(z + 1 + step, 8)

    def hop(step, carry):
        for way, sub in order:
            pltpu.make_async_remote_copy(
                src_ref=slots.at[step - 1, way, sub],
                dst_ref=slots.at[step - 1, way, sub],
                send_sem=send.at[step - 1, way, sub],
                recv_sem=recv.at[step - 1, way, sub],
                device_id={"src": right if way == 0 else left},
                device_id_type=MESH,
            ).wait_recv()
            values, stats = merge(slots[step - 1, way, sub], acc_ref[block_of(step, way), way, sub], sub % 2)
            slots[step - 1, way, sub, 0:64] = values
            slots[step - 1, way, sub, 64:72] = stats
            copy(step, way, sub).start()
        return carry

    lax.fori_loop(1, 7, hop, 0)
    for way, sub in order:
        last = copy(6, way, sub)
        last.wait_recv()
        values, stats = merge(slots[6, way, sub], acc_ref[z, way, sub], sub % 2)
        total[way, sub, 0:64] = values
        total[way, sub, 64:72] = stats
    owner_rows(total, own_ref, h_own, cot_ref, out_ref, pay, self_ref, dself_ref)
    own_copy = pltpu.make_async_copy(pay, all_ref.at[z], own_sem)
    own_copy.start()
    links = Links(grad_send, grad_recv)
    run_chains([around(links, pay, all_ref, z)])
    for step in range(7):
        for way, sub in order:
            copy(step, way, sub).wait_send()
    own_copy.wait()
    links.drain()


def exchange(acc, x, proj, own, cotangent):
    return pl.pallas_call(
        exchange_body,
        out_shape=(
            jax.ShapeDtypeStruct((128, 512), F32),
            jax.ShapeDtypeStruct((8, 136, 512), F32),
            jax.ShapeDtypeStruct((512, 128), F32),
            jax.ShapeDtypeStruct((8, 128), F32),
        ),
        in_specs=[VMEM] * 5,
        out_specs=(VMEM, ANY, VMEM, VMEM),
        scratch_shapes=[
            pltpu.VMEM((7, 2, 4, 72, 128), F32),
            pltpu.VMEM((2, 4, 72, 128), F32),
            pltpu.VMEM((136, 512), F32),
            pltpu.VMEM((128, 512), F32),
            pltpu.SemaphoreType.DMA((7, 2, 4)),
            pltpu.SemaphoreType.DMA((7, 2, 4)),
            pltpu.SemaphoreType.DMA((14,)),
            pltpu.SemaphoreType.DMA((14,)),
            pltpu.SemaphoreType.DMA,
        ],
        compiler_params=pltpu.CompilerParams(collective_id=1, has_side_effects=True),
    )(acc, x, proj, own, cotangent)


def minus_one(power):
    series = power * (1 + power * (1 / 2 + power * (1 / 6 + power * (1 / 24 + power * (1 / 120)))))
    return jnp.where(power > -0.1, series, jnp.exp(power) - 1)


def owner_rows(total_ref, own_ref, h_own, cot_ref, out_ref, pay_ref, self_ref, dself_ref):
    raw = own_ref[0:8] + own_ref[8:16]
    own = leaky(raw)
    parts = [total_ref[pair // 2, 2 * (pair % 2), 64:72] for pair in range(4)]
    tops = jnp.concatenate([part[0:2] for part in parts], axis=0)
    sums = jnp.concatenate([part[2:4] for part in parts], axis=0)
    best = jnp.maximum(tops, own)
    f_tot, f_own = jnp.exp2(tops - best), jnp.exp2(own - best)
    inverse = 1.0 / (sums * f_tot + f_own)
    slope = jnp.where(raw > 0, 1.0, 0.2)
    cols = columns_of(jnp.concatenate([f_tot * inverse, f_own * inverse, inverse, slope], axis=0))
    lane = lanes((128, 128))
    stats = jnp.zeros((128, 128), F32)
    for pair in range(4):
        way, inner = pair // 2, pair % 2
        span = slice(128 * pair, 128 * pair + 128)
        acc = jnp.concatenate([total_ref[way, 2 * inner + half, 0:64] for half in range(2)], axis=0)

        def wide(kind):
            s = 8 * kind + 2 * pair
            return jnp.where(lane < 64, cols[:, s : s + 1], cols[:, s + 1 : s + 2])

        alpha, h_pair = wide(1), h_own[:, span]
        agg = acc * wide(0) + h_pair * alpha
        low = jnp.minimum(agg, 0.0)
        out_ref[:, span] = jnp.where(agg > 0, agg, minus_one(low))
        grad = cot_ref[:, span] * jnp.where(agg > 0, 1.0, jnp.exp(low))
        pay_ref[0:128, span] = grad * wide(2)
        self_ref[span] = (grad * alpha).T
        for odd in range(2):
            h = 2 * pair + odd
            mine = lane >= 64 if odd else lane < 64
            row_dot = jnp.sum(jnp.where(mine, grad * agg, 0.0), axis=1, keepdims=True)
            d_alpha = jnp.sum(jnp.where(mine, grad * h_pair, 0.0), axis=1, keepdims=True)
            d_self = cols[:, 8 + h : 9 + h] * (d_alpha - row_dot) * cols[:, 24 + h : 25 + h]
            stats = jnp.where(lane == h, row_dot * cols[:, 16 + h : 17 + h], stats)
            stats = jnp.where(lane == 8 + h, d_self, stats)
    turned = stats.T
    pay_ref[128:136, 0:128] = best
    pay_ref[128:136, 128:256] = turned[0:8]
    pay_ref[128:136, 256:512] = jnp.zeros((8, 256), F32)
    dself_ref[...] = turned[8:16]


def backward_body(
    blocks, counts, spot, panel, p_ref, att_ref, group, masks, pay_ref, self_ref, dself_ref, hb_in, b_ref,
    dx_out, w_out, ddst_out, hb, gn, gt, top, abc, minus, ddst, dsrc, dh, p_wide, att_wide,
    dx_slots, dx_sems, dp_out, group_sems, hb_sem, factors, a_ref, x_ref, mask_ref, sems,
):
    features = pltpu.make_async_copy(hb_in, hb, hb_sem)
    features.start()
    arrive = stream_in(panel, x_ref, masks, mask_ref, group, a_ref, sems)
    lane = lanes((128, 128))
    minus[...] = jnp.full(minus.shape, -1.0, BF16)

    def setup(b, carry):
        row_dot = pay_ref[b, 128:136, 128:256]
        high = row_dot.astype(BF16).astype(F32)
        middle = (row_dot - high).astype(BF16).astype(F32)
        dots = columns_of(jnp.concatenate([high, middle, row_dot - high - middle], axis=0))
        for pair in range(4):
            grad = pay_ref[b, 0:128, 128 * pair : 128 * pair + 128]
            for side in range(2):
                rows = slice(128 * side, 128 * side + 128)
                mine = lane >= 64 if side else lane < 64
                g_high, g_low = split(jnp.where(mine, grad, 0.0))
                gn[b, pair, rows, 0:128] = g_high
                gn[b, pair, rows, 128:256] = g_low
                own_dot = jnp.logical_and(lane < 24, lax.rem(lane, 8) == 2 * pair + side)
                gn[b, pair, rows, 256:384] = jnp.where(own_dot, dots, 0.0).astype(BF16)
            t_high, t_low = split(grad.T)
            gt[b, pair, :, 0:128] = t_high
            gt[b, pair, :, 128:256] = t_low
        return carry

    lax.fori_loop(0, 8, setup, 0)

    ddst[...] = jnp.zeros(ddst.shape, F32)
    dsrc[...] = jnp.zeros(dsrc.shape, F32)
    dh[...] = jnp.zeros(dh.shape, F32)
    dh[spot[0]] = self_ref[...]
    high, reach = peaks(b_ref)
    close = reach < SPAN
    pltpu.make_async_copy(masks, mask_ref, sems.at[8]).wait()
    pltpu.make_async_copy(group.at[:, pl.ds(128, 8), pl.ds(128, 128)], a_ref, sems.at[9]).wait()

    def put(kind, b, h, tile):
        (abc, top)[kind][b * 8 + h] = tile

    def accumulate(weight):
        def step(k, carry):
            b, c = blocks[2 * k], blocks[2 * k + 1]
            keep = mask_ref[k] > 0
            for pair in range(4):
                g_high, h_high = gn[b, pair, :, 0:128], hb[c, pair, 0:128]
                d_alpha = dot(
                    jnp.concatenate([g_high, g_high, gn[b, pair, :, 128:384]], axis=1),
                    jnp.concatenate([h_high, hb[c, pair, 128:256], h_high, minus[...]], axis=1),
                    NT,
                )
                highs, lows = [], []
                for side in range(2):
                    h = 2 * pair + side
                    w, positive = weight(b, c, h, keep)
                    d_raw = w * d_alpha[128 * side : 128 * side + 128]
                    d_raw = jnp.where(positive, d_raw, 0.2 * d_raw)
                    ddst[b * 8 + h] += d_raw
                    dsrc[c * 8 + h] += jnp.sum(d_raw.reshape(16, 8, 128), axis=0)
                    w_high, w_low = split(w)
                    highs.append(w_high)
                    lows.append(w_low)
                w_high, w_low = jnp.concatenate(highs, axis=1), jnp.concatenate(lows, axis=1)
                both = dot(
                    jnp.concatenate([gt[b, pair], gt[b, pair, :, 0:128]], axis=1),
                    jnp.concatenate([w_high, w_high, w_low], axis=0),
                )
                dh[c, 128 * pair : 128 * pair + 64] += both[0:64, 0:128]
                dh[c, 128 * pair + 64 : 128 * pair + 128] += both[64:128, 128:256]
            return carry

        lax.fori_loop(0, counts[0], step, 0)

    @pl.when(close)
    def _():
        source_factors(b_ref, high, factors)
        spread_rows(lambda b: target_factors(a_ref[b], high, pay_ref[b, 128:136, 0:128]), put)
        features.wait()

        def weight(b, c, h, keep):
            one = abc[b * 8 + h] * factors[c, pl.ds(h, 1)]
            two = top[b * 8 + h] * factors[c, pl.ds(8 + h, 1)]
            return jnp.where(keep, jnp.maximum(one, two), 0.0), one > two

        accumulate(weight)

    @pl.when(jnp.logical_not(close))
    def _():
        spread_rows(lambda b: [a_ref[b], pay_ref[b, 128:136, 0:128]], put)
        features.wait()

        def weight(b, c, h, keep):
            raw = abc[b * 8 + h] + jnp.where(keep, b_ref[c, pl.ds(h, 1)], NEG)
            return jnp.exp2(leaky(raw) - top[b * 8 + h]), raw > 0

        accumulate(weight)

    for i in range(8):
        arrive(i).wait()

    def group_half(b, side):
        part = group.at[b, pl.ds(0, 128), pl.ds(128 * side, 128)]
        return pltpu.make_async_copy(part, abc.at[2 * b + side], group_sems.at[2 * b + side])

    for b in range(8):
        for side in range(2):
            group_half(b, side).start()

    def pack_dst(b, carry):
        ddst_out[b] = jnp.concatenate(
            [jnp.sum(ddst[b * 8 + h].T, axis=0, keepdims=True) for h in range(8)], axis=0
        )
        return carry

    lax.fori_loop(0, 8, pack_dst, 0)
    ddst_out[spot[1]] += dself_ref[...]

    high, low = split(p_ref[...])
    p_wide[:, 0:512] = high
    p_wide[:, 512:1024] = low
    p_wide[:, 1024:1536] = high
    att_cols = columns_of(jnp.concatenate([att_ref[...], jnp.zeros((8, 64), F32)], axis=1))
    for h in range(8):
        att_wide[64 * h : 64 * h + 64] = jnp.broadcast_to(att_cols[0:64, h : h + 1], (64, 128))
    dp_out[...] = jnp.zeros(dp_out.shape, F32)
    own = spot[0]

    def leave(four, slot):
        return pltpu.make_async_copy(dx_slots.at[slot], dx_out.at[pl.ds(4 * four, 4)], dx_sems.at[slot])

    def project(four, carry):
        wide_dh, wide_src = [], []
        for s in range(4):
            c = 4 * four + s
            d_src = jnp.concatenate(
                [jnp.sum(dsrc[c * 8 + h], axis=0, keepdims=True) for h in range(8)], axis=0
            )
            d_src = d_src + jnp.where(c == own, dself_ref[...], 0.0)
            spread = jnp.concatenate(
                [att_wide[64 * h : 64 * h + 64] * d_src[h : h + 1] for h in range(8)], axis=0
            )
            wide_dh.append(dh[c] + spread)
            wide_src.append(jnp.concatenate([d_src, jnp.zeros((8, 128), F32)], axis=0))
        high, low = split(jnp.concatenate(wide_dh, axis=1))
        s_high, s_low = split(jnp.concatenate(wide_src, axis=1))
        x_high, x_low = split(jnp.concatenate([x_ref[4 * four + s, 0:128] for s in range(4)], axis=0))
        dx = dot(p_wide[...], jnp.concatenate([high, high, low], axis=0))
        slot = lax.rem(four, 2)

        @pl.when(four >= 2)
        def _():
            leave(four - 2, slot).wait()

        for s in range(4):
            dx_slots[slot, s] = dx[:, 128 * s : 128 * s + 128]
        leave(four, slot).start()
        tall_high = jnp.concatenate([high, s_high], axis=0)
        tall_low = jnp.concatenate([low, s_low], axis=0)
        dp_out[...] += dot(
            jnp.concatenate([tall_high, tall_high, tall_low], axis=1),
            jnp.concatenate([x_high, x_low, x_high], axis=0),
        )
        return carry

    lax.fori_loop(0, 8, project, 0)
    u = jnp.zeros((8, 256), F32)
    for b in range(8):
        for side in range(2):
            group_half(b, side).wait()
        u += dot(ddst_out[b], jnp.concatenate([abc[2 * b], abc[2 * b + 1]], axis=1), NN, HIGHEST)
    for i in range(32):
        w_out[i, 0:16] = dp_out[16 * i : 16 * i + 16, 0:128]
        w_out[i, 16:32] = dp_out[16 * i : 16 * i + 16, 128:256]
        w_out[i, 32:48] = jnp.zeros((16, 128), F32)
    for h in range(8):
        for side in range(2):
            span = slice(128 * side, 128 * side + 128)
            w_out[h + 16 * side, 32:33] = u[h : h + 1, span]
            w_out[8 + h + 16 * side, 32:33] = dp_out[512 + h : 513 + h, span]
    leave(6, 0).wait()
    leave(7, 1).wait()


def backward_local(blocks, counts, spot, panel, proj, att_src, group, masks, pays, dh_self, d_self, hb, b):
    return pl.pallas_call(
        backward_body,
        out_shape=(
            jax.ShapeDtypeStruct((32, 256, 128), F32),
            jax.ShapeDtypeStruct((32, 48, 128), F32),
            jax.ShapeDtypeStruct((8, 8, 128), F32),
        ),
        in_specs=[SMEM] * 3 + [ANY, VMEM, VMEM, ANY, ANY, VMEM, VMEM, VMEM, ANY, VMEM],
        out_specs=(ANY, VMEM, VMEM),
        scratch_shapes=[
            pltpu.VMEM((32, 4, 256, 128), BF16),
            pltpu.VMEM((8, 4, 256, 384), BF16),
            pltpu.VMEM((8, 4, 128, 256), BF16),
            pltpu.VMEM((64, 128, 128), F32),
            pltpu.VMEM((64, 128, 128), F32),
            pltpu.VMEM((128, 128), BF16),
            pltpu.VMEM((64, 128, 128), F32),
            pltpu.VMEM((256, 8, 128), F32),
            pltpu.VMEM((32, 512, 128), F32),
            pltpu.VMEM((256, 1536), BF16),
            pltpu.VMEM((512, 128), F32),
            pltpu.VMEM((2, 4, 256, 128), F32),
            pltpu.SemaphoreType.DMA((2,)),
            pltpu.VMEM((528, 256), F32),
            pltpu.SemaphoreType.DMA((16,)),
            pltpu.SemaphoreType.DMA,
            pltpu.VMEM((32, 16, 128), F32),
            pltpu.VMEM((8, 8, 128), F32),
            pltpu.VMEM((32, 136, 256), F32),
            pltpu.VMEM((32, 128, 128), jnp.int32),
            pltpu.SemaphoreType.DMA((10,)),
        ],
        compiler_params=pltpu.CompilerParams(vmem_limit_bytes=BIG_VMEM),
    )(blocks, counts, spot, panel, proj, att_src, group, masks, pays, dh_self, d_self, hb, b)


def reduce_body(
    dx_ref, w_ref, ddst_ref, dx_out, dp_out, dst_out,
    send, recv, twin_dx, twin_w, total, far, near, far2, near2, dst_all, joined, tower,
):
    d, y, x, k, z = place()
    sibling = node(y, x, 1 - k)
    chip = y * 4 + x
    offsets = [(dy, dx) for dy in range(4) for dx in range(4) if (dy, dx) != (0, 0)]
    others = [lax.rem(z + s, 8) for s in range(1, 8)]
    wait_all = greet([sibling] + [node(y + dy, x + dx, k) for dy, dx in offsets], others)
    links = Links(send, recv)
    wait_all()

    def rank(offset):
        return 0 if 2 in offset else (2 if offset == (0, 0) else 1)

    cells = sorted([(0, 0)] + offsets, key=rank)
    twin_weights = links.push(w_ref.at[:, :, 1 - k], twin_w, dst=sibling)
    twin_copies = {}
    for dy, dx in cells:
        yy, xx = lax.rem(y + dy, 4), lax.rem(x + dx, 4)
        twin_copies[dy, dx] = links.push(dx_ref.at[yy, xx, 1 - k], twin_dx.at[yy, xx], dst=sibling)
    dst_copies = [links.push(ddst_ref.at[t], dst_all.at[z], src=t) for t in others]
    twin_weights.wait_recv()

    def add_cells(wanted):
        for dy, dx in cells:
            if rank((dy, dx)) != wanted:
                continue
            yy, xx = lax.rem(y + dy, 4), lax.rem(x + dx, 4)
            twin_copies[dy, dx].wait_recv()
            total[yy, xx, 0:128] = dx_ref[yy, xx, k, 0:128] + twin_dx[yy, xx, 0:128]
            total[yy, xx, 128:152] = w_ref[yy, xx, k, 0:24] + twin_w[yy, xx, 0:24]
            total[yy, xx, 152:280] = dx_ref[yy, xx, k, 128:256] + twin_dx[yy, xx, 128:256]
            total[yy, xx, 280:304] = w_ref[yy, xx, k, 24:48] + twin_w[yy, xx, 24:48]

    def ring(region, plus, minus, far_buf, near_buf):
        c0 = links.push(region(2, 0), far_buf(0, 0), dst=plus)
        c1 = links.push(region(2, 1), far_buf(1, 1), dst=minus)
        yield
        c2 = links.push(region(1, 1), near_buf(0, 1), dst=plus)
        c3 = links.push(region(-1, 0), near_buf(1, 0), dst=minus)
        yield
        c0.wait_recv()
        part = region(1, 0)
        part[...] += far_buf(0, 0)[...]
        c4 = links.push(part, near_buf(2, 0), dst=plus)
        yield
        c1.wait_recv()
        part = region(-1, 1)
        part[...] += far_buf(1, 1)[...]
        c5 = links.push(part, near_buf(3, 1), dst=minus)
        yield
        for copy, index, piece in ((c2, 0, 1), (c3, 1, 0), (c4, 2, 0), (c5, 3, 1)):
            yield
            copy.wait_recv()
            part = region(0, piece)
            part[...] += near_buf(index, piece)[...]

    def grads(half):
        rows = pl.ds(152 * half, 152)

        def wide(v, piece):
            if half == 0:
                return total.at[lax.rem(y + v + 4, 4), pl.ds(2 * piece, 2), rows]
            return total.at[pl.ds(2 * piece, 2), lax.rem(x + v + 4, 4), rows]

        def narrow(u, piece):
            span = pl.ds(152 * half + 80 * piece, 80 - 8 * piece)
            if half == 0:
                return total.at[y, lax.rem(x + u + 4, 4), span]
            return total.at[lax.rem(y + u + 4, 4), x, span]

        def short(buffer):
            return lambda index, piece: buffer.at[half, index, pl.ds(0, 80 - 8 * piece)]

        along_y = (node(y + 1, x, k), node(y - 1, x, k))
        along_x = (node(y, x + 1, k), node(y, x - 1, k))
        first, then = (along_y, along_x) if half == 0 else (along_x, along_y)
        yield from ring(wide, *first, lambda i, p: far.at[half, i], lambda i, p: near.at[half, i])
        yield from ring(narrow, *then, short(far2), short(near2))

    chains = [grads(0), grads(1)]
    for wanted in range(3):
        add_cells(wanted)
        if wanted < 2:
            for chain in chains:
                next(chain)
    run_chains(chains)

    joined[0:24] = total[y, x, 128:152]
    joined[24:40] = total[y, x, 280:296]
    tower[z] = joined[...]
    coming = [links.push(joined, tower.at[z], src=t) for t in others]
    dx_out[0:128] = total[y, x, 0:128]
    dx_out[128:256] = total[y, x, 152:280]
    for copy in dst_copies:
        copy.wait_recv()
    dst_all[z] = ddst_ref[z]
    dst_total = dst_all[0]
    for t in range(1, 8):
        dst_total = dst_total + dst_all[t]
    dst_out[...] = dst_total
    for copy in coming:
        copy.wait_recv()
    value = tower[0]
    for i in range(1, 8):
        value = value + tower[i]
    dp_out[chip, k] = value
    coming = [
        links.push(dp_out.at[chip, k], dp_out.at[chip, k], dst=node(y + dy, x + dx, k)) for dy, dx in offsets
    ]
    for copy in coming:
        copy.wait_recv()
    over = links.push(dp_out.at[:, k], dp_out.at[:, k], dst=sibling)
    over.wait_recv()
    links.drain()


def reduce_grads(dx, w, ddst):
    count = 1 + 16 + 7 + 24 + 7 + 15 + 1
    return pl.pallas_call(
        reduce_body,
        out_shape=(
            jax.ShapeDtypeStruct((256, 128), F32),
            jax.ShapeDtypeStruct((16, 2, 40, 128), F32),
            jax.ShapeDtypeStruct((8, 128), F32),
        ),
        in_specs=[VMEM] * 3,
        out_specs=(VMEM,) * 3,
        scratch_shapes=[
            pltpu.SemaphoreType.DMA((count,)),
            pltpu.SemaphoreType.DMA((count,)),
            pltpu.VMEM((4, 4, 256, 128), F32),
            pltpu.VMEM((4, 4, 48, 128), F32),
            pltpu.VMEM((4, 4, 304, 128), F32),
            pltpu.VMEM((2, 2, 2, 152, 128), F32),
            pltpu.VMEM((2, 4, 2, 152, 128), F32),
            pltpu.VMEM((2, 2, 80, 128), F32),
            pltpu.VMEM((2, 4, 80, 128), F32),
            pltpu.VMEM((8, 8, 128), F32),
            pltpu.VMEM((40, 128), F32),
            pltpu.VMEM((8, 40, 128), F32),
        ],
        compiler_params=pltpu.CompilerParams(
            collective_id=2, has_side_effects=True, vmem_limit_bytes=BIG_VMEM
        ),
    )(dx.reshape(4, 4, 2, 256, 128), w.reshape(4, 4, 2, 48, 128), ddst)


def finish_body(dx_ref, w_ref, dst_ref, p_ref, dst_att_ref, in_ref, proj_ref, src_ref, dst_out):
    proj = p_ref[...]
    a_rows = per_head_rows(dst_att_ref[...])
    score = dot(a_rows, proj, NT, HIGHEST)
    pad = jnp.zeros((120, 256), F32)
    score_t = jnp.concatenate([score, pad], axis=0).T
    dst_wide = jnp.concatenate([dst_ref[...], jnp.zeros((120, 128), F32)], axis=0)
    in_ref[...] = (dx_ref[...] + dot(score_t, dst_wide, NN, HIGHEST)).T

    def row(i):
        return jnp.concatenate([w_ref[i, 32:33], w_ref[i + 16, 32:33]], axis=1)

    u = jnp.concatenate([row(h) for h in range(8)], axis=0)
    v = jnp.concatenate([row(8 + h) for h in range(8)], axis=0)
    wide_u = jnp.concatenate([u, jnp.zeros((120, 256), F32)], axis=0)
    att = jnp.concatenate([a_rows, jnp.zeros((120, 512), F32)], axis=0)
    grad_t = jnp.concatenate(
        [jnp.concatenate([w_ref[i, 0:16], w_ref[i, 16:32]], axis=1) for i in range(32)], axis=0
    )
    proj_ref[...] = (grad_t + dot(att.T, wide_u, NN, HIGHEST)).T
    both = dot(jnp.concatenate([u, v], axis=0), proj, NN, HIGHEST)
    dst_out[...] = jnp.concatenate([both[h : h + 1, 64 * h : 64 * h + 64] for h in range(8)], axis=0)
    src_ref[...] = jnp.concatenate([both[8 + h : 9 + h, 64 * h : 64 * h + 64] for h in range(8)], axis=0)


def finish(dx, weights, dst_total, proj, att_dst):
    return pl.pallas_call(
        finish_body,
        out_shape=(
            jax.ShapeDtypeStruct((128, 256), F32),
            jax.ShapeDtypeStruct((256, 512), F32),
            jax.ShapeDtypeStruct((8, 64), F32),
            jax.ShapeDtypeStruct((8, 64), F32),
        ),
        in_specs=[VMEM] * 5,
        out_specs=(VMEM,) * 4,
    )(dx, weights.reshape(32, 40, 128), dst_total, proj, att_dst)


def shards(inputs, projection, att_src, att_dst, blocks, counts, tile_masks, cotangent):
    coords = blocks.reshape(64)
    live = counts.reshape(1)
    masks = tile_masks[0, 0]
    spot = jnp.stack([lax.axis_index("dst"), lax.axis_index("src")]).astype(jnp.int32)
    panel, group, own = gather_inputs(inputs, projection, att_src, att_dst)
    acc, hb, b = forward_local(coords, live, panel, projection, group, masks)
    output, pays, dh_self, d_self = exchange(acc, inputs, projection, own, cotangent)
    dx, w, ddst = backward_local(
        coords, live, spot, panel, projection, att_src, group, masks, pays, dh_self, d_self, hb, b
    )
    dx_own, weights, dst_total = reduce_grads(dx, w, ddst)
    in_grad, proj_grad, src_grad, dst_grad = finish(dx_own, weights, dst_total, projection, att_dst)
    return (output, in_grad, proj_grad, src_grad, dst_grad)


def solution(mesh):
    in_specs = (
        P(("dst", "src"), None),
        P(),
        P(),
        P(),
        P("dst", "src", None, None),
        P("dst", "src"),
        P("dst", "src", None, None, None),
        P(("dst", "src"), None),
    )
    out_specs = (P(("dst", "src"), None), P(("dst", "src"), None), P(), P(), P())
    return jax.shard_map(shards, mesh=mesh, in_specs=in_specs, out_specs=out_specs, check_vma=False)
```

```python
import functools

import jax
import jax.numpy as jnp
from jax import lax
from jax.experimental import pallas as pl
from jax.experimental.pallas import tpu as pltpu
from jax.sharding import PartitionSpec as P

HIGHEST = lax.Precision.HIGHEST
F32 = jnp.float32
BF16 = jnp.bfloat16
LOG2E = 1.4426950408889634
NEG = -1e30
MESH = pl.DeviceIdType.MESH
VMEM = pl.BlockSpec(memory_space=pltpu.VMEM)
SMEM = pl.BlockSpec(memory_space=pltpu.SMEM)
ANY = pl.BlockSpec(memory_space=pl.ANY)
NN = (((1,), (0,)), ((), ()))
NT = (((1,), (1,)), ((), ()))
BIG_VMEM = 60 * 1024 * 1024


def dot(a, b, dims=NN, precision=None):
    return lax.dot_general(a, b, dims, precision=precision, preferred_element_type=F32)


def split(value):
    high = value.astype(BF16)
    return high, (value - high.astype(F32)).astype(BF16)


def leaky(raw):
    return jnp.maximum(raw, 0.2 * raw)


def per_head_rows(att):
    wide = jnp.concatenate([att] * 8, axis=1)
    head = lax.broadcasted_iota(jnp.int32, wide.shape, 0)
    column = lax.broadcasted_iota(jnp.int32, wide.shape, 1)
    return jnp.where(column // 64 == head, wide, 0.0)


def score_rows(att, proj):
    return dot(per_head_rows(att), proj, NT, HIGHEST)


def lanes(shape):
    return lax.broadcasted_iota(jnp.int32, shape, len(shape) - 1)


def place():
    d = lax.axis_index("dst")
    z = lax.axis_index("src")
    return d, d // 8, lax.rem(d // 2, 4), lax.rem(d, 2), z


def node(y, x, k):
    return lax.rem(y + 8, 4) * 8 + lax.rem(x + 8, 4) * 2 + k


class Links:
    def __init__(self, send, recv):
        self.send, self.recv, self.used, self.open = send, recv, 0, []

    def push(self, source, landing, **target):
        copy = pltpu.make_async_remote_copy(
            src_ref=source,
            dst_ref=landing,
            send_sem=self.send.at[self.used],
            recv_sem=self.recv.at[self.used],
            device_id=target,
            device_id_type=MESH,
        )
        self.used += 1
        copy.start()
        self.open.append(copy)
        return copy

    def drain(self):
        for copy in self.open:
            copy.wait_send()


def greet(dsts, srcs):
    barrier = pltpu.get_barrier_semaphore()
    for other in dsts:
        pl.semaphore_signal(barrier, inc=1, device_id={"dst": other}, device_id_type=MESH)
    for other in srcs:
        pl.semaphore_signal(barrier, inc=1, device_id={"src": other}, device_id_type=MESH)
    return lambda: pl.semaphore_wait(barrier, len(dsts) + len(srcs))


def run_chains(chains):
    chains = list(chains)
    while chains:
        for chain in list(chains):
            try:
                next(chain)
            except StopIteration:
                chains.remove(chain)


def around(links, own_ref, all_ref, z):
    spans = (pl.ds(0, 64), pl.ds(64, 72))
    right, left = lax.rem(z + 1, 8), lax.rem(z + 7, 8)

    def push(step, way, sub):
        block = lax.rem(z + 8 - step, 8) if way == 0 else lax.rem(z + step, 8)
        part = all_ref.at[block, spans[sub]]
        source = own_ref.at[spans[sub]] if step == 0 else part
        return links.push(source, part, src=right if way == 0 else left)

    order = [(way, sub) for sub in range(2) for way in range(2)]
    coming = {item: push(0, *item) for item in order}
    for step in range(1, 4):
        for item in order:
            yield
            coming[item].wait_recv()
            if step < 3 or item[0] == item[1]:
                coming[item] = push(step, *item)
            else:
                del coming[item]
    for copy in list(coming.values()):
        yield
        copy.wait_recv()


def gather_body(x_ref, p_ref, src_ref, dst_ref, panel_ref, group_ref, own_ref, pay, send, recv, own_sem):
    d, y, x, k, z = place()
    sibling = node(y, x, 1 - k)
    wait_all = greet(
        [sibling, node(y + 1, x, k), node(y - 1, x, k), node(y, x + 1, k), node(y, x - 1, k)],
        [lax.rem(z + 1, 8), lax.rem(z + 7, 8)],
    )
    rows = jnp.concatenate([score_rows(r[...], p_ref[...]) for r in (src_ref, dst_ref)], axis=0) * LOG2E
    scores = dot(rows, x_ref[...], NT, HIGHEST)
    pay[0:128] = x_ref[...]
    pay[128:136, 0:128] = scores[0:8]
    pay[128:136, 128:256] = scores[8:16]
    own_ref[...] = scores
    own_copies = [
        pltpu.make_async_copy(pay, panel_ref.at[d], own_sem.at[0]),
        pltpu.make_async_copy(pay, group_ref.at[z], own_sem.at[1]),
    ]
    for copy in own_copies:
        copy.start()
    wait_all()
    links = Links(send, recv)

    def chain(half):
        def at(u, v):
            return node(y + v, x + u, k) if half == 0 else node(y + u, x + v, k)

        def region(u, v, quarter=None):
            start, size = 64 * half, 64 + 8 * half
            if quarter is not None:
                start, size = start + 32 * quarter, 32 + 8 * half * quarter
            return panel_ref.at[at(u, v), pl.ds(start, size)]

        def to(part, du, dv, src=None):
            return links.push(part if src is None else src, part, dst=at(du, dv))

        def twin(u, v, src=None):
            part = region(u, v)
            return links.push(part if src is None else src, part, dst=sibling)

        own = pay.at[pl.ds(64 * half, 64 + 8 * half)]
        first = [to(region(0, 0), 1, 0, own), to(region(0, 0), -1, 0, own)]
        second = {0: [to(region(0, 0), 0, 1, own), to(region(0, 0), 0, -1, own)]}
        twins = [twin(0, 0, own)]
        last = {}

        def spread(u):
            second[u] = [to(region(u, 0), 0, 1), to(region(u, 0), 0, -1)]
            twins.append(twin(u, 0))

        def relay(u):
            pair = []
            for index, v in ((0, -1), (1, 1)):
                yield
                second[u][index].wait_recv()
                pair.append(to(region(u, v, index), 0, -v))
                twins.append(twin(u, v))
            last[u] = pair

        def finish(u):
            yield
            for copy in last[u]:
                copy.wait_recv()
            twins.append(twin(u, 2))

        far = []
        for index, u in ((0, -1), (1, 1)):
            yield
            first[index].wait_recv()
            far.append(to(region(u, 0, index), -u, 0))
            spread(u)
        yield from relay(0)
        yield
        for copy in far:
            copy.wait_recv()
        spread(2)
        yield from relay(-1)
        yield from relay(1)
        yield from finish(0)
        yield from relay(2)
        yield from finish(-1)
        yield from finish(1)
        yield from finish(2)
        yield
        for copy in twins:
            copy.wait_recv()

    run_chains([chain(0), chain(1), around(links, pay, group_ref, z)])
    for copy in own_copies:
        copy.wait()
    links.drain()


def gather_inputs(x, proj, att_src, att_dst):
    count = 72 + 14
    return pl.pallas_call(
        gather_body,
        out_shape=(
            jax.ShapeDtypeStruct((32, 136, 256), F32),
            jax.ShapeDtypeStruct((8, 136, 256), F32),
            jax.ShapeDtypeStruct((16, 128), F32),
        ),
        in_specs=[VMEM] * 4,
        out_specs=(ANY, ANY, VMEM),
        scratch_shapes=[
            pltpu.VMEM((136, 256), F32),
            pltpu.SemaphoreType.DMA((count,)),
            pltpu.SemaphoreType.DMA((count,)),
            pltpu.SemaphoreType.DMA((2,)),
        ],
        compiler_params=pltpu.CompilerParams(collective_id=0, has_side_effects=True),
    )(x, proj, att_src, att_dst)


def split_weights(p_ref, p_cat):
    high, low = split(p_ref[...])
    p_cat[0:256] = high
    p_cat[256:512] = low
    p_cat[512:768] = high


def stream_in(panel, x_ref, masks, mask_ref, group, a_ref, sems):
    def part(i):
        span = pl.ds(4 * i, 4)
        return pltpu.make_async_copy(panel.at[span], x_ref.at[span], sems.at[i])

    for i in range(8):
        part(i).start()
    pltpu.make_async_copy(masks, mask_ref, sems.at[8]).start()
    pltpu.make_async_copy(group.at[:, pl.ds(128, 8), pl.ds(128, 128)], a_ref, sems.at[9]).start()
    return part


def prepare_features(x_ref, p_cat, hb, arrive, leave):
    n = 4

    def step(group, carry):
        arrive(group).wait()
        x_high, x_low = split(jnp.concatenate([x_ref[group * n + s, 0:128] for s in range(n)], axis=0))
        left = jnp.concatenate([x_high, x_high, x_low], axis=1)
        for wide in range(2):
            h_high, h_low = split(dot(left, p_cat[:, 256 * wide : 256 * wide + 256]))
            for s in range(n):
                for side in range(2):
                    part = (slice(128 * s, 128 * s + 128), slice(128 * side, 128 * side + 128))
                    pair = 2 * wide + side
                    hb[group * n + s, pair, 0:128] = h_high[part]
                    hb[group * n + s, pair, 128:256] = h_low[part]
        leave(group).start()
        return carry

    lax.fori_loop(0, 32 // n, step, 0)


def columns_of(rows):
    pad = jnp.zeros((128 - rows.shape[0], 128), F32)
    return jnp.concatenate([rows, pad], axis=0).T


def spread_rows(rows_of, put):
    parts = []
    for b in range(8):
        kinds = rows_of(b)
        pieces = []
        for rows in kinds:
            high = rows.astype(BF16).astype(F32)
            middle = (rows - high).astype(BF16).astype(F32)
            pieces += [high, middle, rows - high - middle]
        parts.append(columns_of(jnp.concatenate(pieces, axis=0)).astype(BF16))
    left = jnp.concatenate(parts, axis=0)
    count = len(kinds)
    row = lax.broadcasted_iota(jnp.int32, (128, 128 * count), 0)
    kind = lax.broadcasted_iota(jnp.int32, (128, 128 * count), 1) // 128
    for h in range(8):
        pick = jnp.logical_and(row // 24 == kind, lax.rem(row, 8) == h)
        out = dot(left, jnp.where(pick, 1.0, 0.0).astype(BF16))
        for k in range(count):
            for b in range(8):
                put(k, b, h, out[128 * b : 128 * b + 128, 128 * k : 128 * k + 128])


SPAN = 40.0


def peaks(scores):
    high, low = scores[0], scores[0]
    for c in range(1, 32):
        high, low = jnp.maximum(high, scores[c]), jnp.minimum(low, scores[c])
    high, low = jnp.max(high, axis=1, keepdims=True), jnp.min(low, axis=1, keepdims=True)
    return high, jnp.max(high - low)


def source_factors(scores, high, factors):
    for c in range(32):
        below = scores[c] - high
        factors[c, 0:8] = jnp.exp2(below)
        factors[c, 8:16] = jnp.exp2(0.2 * below)


def target_factors(a, high, shift):
    best = a + high
    return [jnp.exp2(jnp.minimum(part - shift, 100.0)) for part in (best, 0.2 * best)]


def forward_body(
    blocks, counts, panel, p_ref, group, masks, acc_out, hb_out, b_out,
    p_cat, hb, top, abc, sums, acc, top_rows, factors, hb_sems, a_ref, x_ref, mask_ref, sems
):
    arrive = stream_in(panel, x_ref, masks, mask_ref, group, a_ref, sems)

    def leave(i):
        span = pl.ds(4 * i, 4)
        return pltpu.make_async_copy(hb.at[span], hb_out.at[span], hb_sems.at[i])

    split_weights(p_ref, p_cat)
    prepare_features(x_ref, p_cat, hb, arrive, leave)
    pltpu.make_async_copy(masks, mask_ref, sems.at[8]).wait()
    pltpu.make_async_copy(group.at[:, pl.ds(128, 8), pl.ds(128, 128)], a_ref, sems.at[9]).wait()
    b_out[...] = x_ref[:, 128:136, 0:128]
    sums[...] = jnp.zeros(sums.shape, F32)
    acc[...] = jnp.zeros(acc.shape, F32)
    live = counts[0]
    high, reach = peaks(b_out)
    close = reach < SPAN

    def put(kind, b, h, tile):
        (abc, top)[kind][b * 8 + h] = tile

    def accumulate(weight):
        lane = lanes((128, 128))

        def step(k, carry):
            b, c = blocks[2 * k], blocks[2 * k + 1]
            keep = mask_ref[k] > 0
            for pair in range(4):
                sides = []
                for h in (2 * pair, 2 * pair + 1):
                    w = weight(b, c, h, keep)
                    sums[b * 8 + h] += w
                    w_high, w_low = split(w)
                    sides.append(jnp.concatenate([w_high, w_high, w_low], axis=1))
                right = jnp.concatenate([hb[c, pair], hb[c, pair, 0:128]], axis=0)
                both = dot(jnp.concatenate(sides, axis=0), right)
                acc[b * 4 + pair] += jnp.where(lane < 64, both[0:128], both[128:256])
            return carry

        lax.fori_loop(0, live, step, 0)

    @pl.when(close)
    def _():
        source_factors(b_out, high, factors)
        for b in range(8):
            top_rows[b] = leaky(a_ref[b] + high)
        spread_rows(lambda b: target_factors(a_ref[b], high, top_rows[b]), put)

        def weight(b, c, h, keep):
            one = abc[b * 8 + h] * factors[c, pl.ds(h, 1)]
            two = top[b * 8 + h] * factors[c, pl.ds(8 + h, 1)]
            return jnp.where(keep, jnp.maximum(one, two), 0.0)

        accumulate(weight)

    @pl.when(jnp.logical_not(close))
    def _():
        top[...] = jnp.full(top.shape, NEG, F32)

        def find_top(k, carry):
            b, c = blocks[2 * k], blocks[2 * k + 1]
            keep = mask_ref[k] > 0
            for h in range(8):
                top[b * 8 + h] = jnp.maximum(top[b * 8 + h], jnp.where(keep, b_out[c, pl.ds(h, 1)], NEG))
            return carry

        lax.fori_loop(0, live, find_top, 0)

        def find_rows(b, carry):
            best = jnp.concatenate([jnp.max(top[b * 8 + h].T, axis=0, keepdims=True) for h in range(8)], axis=0)
            top_rows[b] = leaky(a_ref[b] + best)
            return carry

        lax.fori_loop(0, 8, find_rows, 0)
        spread_rows(lambda b: [a_ref[b], top_rows[b]], put)

        def weight(b, c, h, keep):
            raw = abc[b * 8 + h] + jnp.where(keep, b_out[c, pl.ds(h, 1)], NEG)
            return jnp.exp2(leaky(raw) - top[b * 8 + h])

        accumulate(weight)

    def pack(b, carry):
        totals = [jnp.sum(sums[b * 8 + h].T, axis=0, keepdims=True) for h in range(8)]
        tops = [
            jnp.where(totals[h] > 0, top_rows[b, h : h + 1], 0.2 * NEG) for h in range(8)
        ]
        for way in range(2):
            for inner in range(2):
                h = 4 * way + 2 * inner
                packed = jnp.concatenate(
                    tops[h : h + 2] + totals[h : h + 2] + [jnp.zeros((4, 128), F32)], axis=0
                )
                for half in range(2):
                    sub = 2 * inner + half
                    acc_out[b, way, sub, 0:64] = acc[b * 4 + 2 * way + inner][64 * half : 64 * half + 64]
                    acc_out[b, way, sub, 64:72] = packed
        return carry

    lax.fori_loop(0, 8, pack, 0)
    for i in range(8):
        leave(i).wait()


def forward_local(blocks, counts, panel, proj, group, masks):
    return pl.pallas_call(
        forward_body,
        out_shape=(
            jax.ShapeDtypeStruct((8, 2, 4, 72, 128), F32),
            jax.ShapeDtypeStruct((32, 4, 256, 128), BF16),
            jax.ShapeDtypeStruct((32, 8, 128), F32),
        ),
        in_specs=[SMEM, SMEM, ANY, VMEM, ANY, ANY],
        out_specs=(VMEM, ANY, VMEM),
        scratch_shapes=[
            pltpu.VMEM((768, 512), BF16),
            pltpu.VMEM((32, 4, 256, 128), BF16),
            pltpu.VMEM((64, 128, 128), F32),
            pltpu.VMEM((64, 128, 128), F32),
            pltpu.VMEM((64, 128, 128), F32),
            pltpu.VMEM((32, 128, 128), F32),
            pltpu.VMEM((8, 8, 128), F32),
            pltpu.VMEM((32, 16, 128), F32),
            pltpu.SemaphoreType.DMA((8,)),
            pltpu.VMEM((8, 8, 128), F32),
            pltpu.VMEM((32, 136, 256), F32),
            pltpu.VMEM((32, 128, 128), jnp.int32),
            pltpu.SemaphoreType.DMA((10,)),
        ],
        compiler_params=pltpu.CompilerParams(vmem_limit_bytes=BIG_VMEM),
    )(blocks, counts, panel, proj, group, masks)


def merge(arrived, mine, half):
    one, two = arrived[64:72], mine[64:72]
    best = jnp.maximum(one[0:2], two[0:2])
    f_one, f_two = jnp.exp2(one[0:2] - best), jnp.exp2(two[0:2] - best)
    total = one[2:4] * f_one + two[2:4] * f_two
    cols = columns_of(jnp.concatenate([f_one, f_two, best, total], axis=0))[64 * half : 64 * half + 64]
    lane = lanes((64, 128))
    factor = [jnp.where(lane < 64, cols[:, s : s + 1], cols[:, s + 1 : s + 2]) for s in (0, 2)]
    values = arrived[0:64] * factor[0] + mine[0:64] * factor[1]
    return values, jnp.concatenate([best, total, one[4:8]], axis=0)


def exchange_body(
    acc_ref, x_ref, p_ref, own_ref, cot_ref, out_ref, all_ref, self_ref, dself_ref,
    slots, total, pay, h_own, send, recv, grad_send, grad_recv, own_sem,
):
    z = lax.axis_index("src")
    right, left = lax.rem(z + 1, 8), lax.rem(z + 7, 8)
    wait_all = greet([], [right, left])
    wait_all()

    def copy(step, way, sub):
        if isinstance(step, int) and step == 0:
            src = acc_ref.at[left if way == 0 else right, way, sub]
        else:
            src = slots.at[step - 1, way, sub]
        return pltpu.make_async_remote_copy(
            src_ref=src,
            dst_ref=slots.at[step, way, sub],
            send_sem=send.at[step, way, sub],
            recv_sem=recv.at[step, way, sub],
            device_id={"src": right if way == 0 else left},
            device_id_type=MESH,
        )

    order = [(way, sub) for sub in range(4) for way in range(2)]
    for way, sub in order:
        copy(0, way, sub).start()
    h_own[...] = dot(x_ref[...], p_ref[...], NN, HIGHEST)

    def block_of(step, way):
        return lax.rem(z + 15 - step, 8) if way == 0 else lax.rem(z + 1 + step, 8)

    def hop(step, carry):
        for way, sub in order:
            pltpu.make_async_remote_copy(
                src_ref=slots.at[step - 1, way, sub],
                dst_ref=slots.at[step - 1, way, sub],
                send_sem=send.at[step - 1, way, sub],
                recv_sem=recv.at[step - 1, way, sub],
                device_id={"src": right if way == 0 else left},
                device_id_type=MESH,
            ).wait_recv()
            values, stats = merge(slots[step - 1, way, sub], acc_ref[block_of(step, way), way, sub], sub % 2)
            slots[step - 1, way, sub, 0:64] = values
            slots[step - 1, way, sub, 64:72] = stats
            copy(step, way, sub).start()
        return carry

    lax.fori_loop(1, 7, hop, 0)
    for way, sub in order:
        last = copy(6, way, sub)
        last.wait_recv()
        values, stats = merge(slots[6, way, sub], acc_ref[z, way, sub], sub % 2)
        total[way, sub, 0:64] = values
        total[way, sub, 64:72] = stats
    owner_rows(total, own_ref, h_own, cot_ref, out_ref, pay, self_ref, dself_ref)
    own_copy = pltpu.make_async_copy(pay, all_ref.at[z], own_sem)
    own_copy.start()
    links = Links(grad_send, grad_recv)
    run_chains([around(links, pay, all_ref, z)])
    for step in range(7):
        for way, sub in order:
            copy(step, way, sub).wait_send()
    own_copy.wait()
    links.drain()


def exchange(acc, x, proj, own, cotangent):
    return pl.pallas_call(
        exchange_body,
        out_shape=(
            jax.ShapeDtypeStruct((128, 512), F32),
            jax.ShapeDtypeStruct((8, 136, 512), F32),
            jax.ShapeDtypeStruct((512, 128), F32),
            jax.ShapeDtypeStruct((8, 128), F32),
        ),
        in_specs=[VMEM] * 5,
        out_specs=(VMEM, ANY, VMEM, VMEM),
        scratch_shapes=[
            pltpu.VMEM((7, 2, 4, 72, 128), F32),
            pltpu.VMEM((2, 4, 72, 128), F32),
            pltpu.VMEM((136, 512), F32),
            pltpu.VMEM((128, 512), F32),
            pltpu.SemaphoreType.DMA((7, 2, 4)),
            pltpu.SemaphoreType.DMA((7, 2, 4)),
            pltpu.SemaphoreType.DMA((14,)),
            pltpu.SemaphoreType.DMA((14,)),
            pltpu.SemaphoreType.DMA,
        ],
        compiler_params=pltpu.CompilerParams(collective_id=1, has_side_effects=True),
    )(acc, x, proj, own, cotangent)


def minus_one(power):
    series = power * (1 + power * (1 / 2 + power * (1 / 6 + power * (1 / 24 + power * (1 / 120)))))
    return jnp.where(power > -0.1, series, jnp.exp(power) - 1)


def owner_rows(total_ref, own_ref, h_own, cot_ref, out_ref, pay_ref, self_ref, dself_ref):
    raw = own_ref[0:8] + own_ref[8:16]
    own = leaky(raw)
    parts = [total_ref[pair // 2, 2 * (pair % 2), 64:72] for pair in range(4)]
    tops = jnp.concatenate([part[0:2] for part in parts], axis=0)
    sums = jnp.concatenate([part[2:4] for part in parts], axis=0)
    best = jnp.maximum(tops, own)
    f_tot, f_own = jnp.exp2(tops - best), jnp.exp2(own - best)
    inverse = 1.0 / (sums * f_tot + f_own)
    slope = jnp.where(raw > 0, 1.0, 0.2)
    cols = columns_of(jnp.concatenate([f_tot * inverse, f_own * inverse, inverse, slope], axis=0))
    lane = lanes((128, 128))
    stats = jnp.zeros((128, 128), F32)
    for pair in range(4):
        way, inner = pair // 2, pair % 2
        span = slice(128 * pair, 128 * pair + 128)
        acc = jnp.concatenate([total_ref[way, 2 * inner + half, 0:64] for half in range(2)], axis=0)

        def wide(kind):
            s = 8 * kind + 2 * pair
            return jnp.where(lane < 64, cols[:, s : s + 1], cols[:, s + 1 : s + 2])

        alpha, h_pair = wide(1), h_own[:, span]
        agg = acc * wide(0) + h_pair * alpha
        low = jnp.minimum(agg, 0.0)
        out_ref[:, span] = jnp.where(agg > 0, agg, minus_one(low))
        grad = cot_ref[:, span] * jnp.where(agg > 0, 1.0, jnp.exp(low))
        pay_ref[0:128, span] = grad * wide(2)
        self_ref[span] = (grad * alpha).T
        for odd in range(2):
            h = 2 * pair + odd
            mine = lane >= 64 if odd else lane < 64
            row_dot = jnp.sum(jnp.where(mine, grad * agg, 0.0), axis=1, keepdims=True)
            d_alpha = jnp.sum(jnp.where(mine, grad * h_pair, 0.0), axis=1, keepdims=True)
            d_self = cols[:, 8 + h : 9 + h] * (d_alpha - row_dot) * cols[:, 24 + h : 25 + h]
            stats = jnp.where(lane == h, row_dot * cols[:, 16 + h : 17 + h], stats)
            stats = jnp.where(lane == 8 + h, d_self, stats)
    turned = stats.T
    pay_ref[128:136, 0:128] = best
    pay_ref[128:136, 128:256] = turned[0:8]
    pay_ref[128:136, 256:512] = jnp.zeros((8, 256), F32)
    dself_ref[...] = turned[8:16]


def backward_body(
    blocks, counts, spot, panel, p_ref, att_ref, group, masks, pay_ref, self_ref, dself_ref, hb_in, b_ref,
    dx_out, w_out, ddst_out, hb, gn, gt, top, abc, minus, ddst, dsrc, dh, p_wide, att_wide,
    dx_slots, dx_sems, dp_out, group_sems, hb_sem, factors, a_ref, x_ref, mask_ref, sems,
):
    features = pltpu.make_async_copy(hb_in, hb, hb_sem)
    features.start()
    arrive = stream_in(panel, x_ref, masks, mask_ref, group, a_ref, sems)
    lane = lanes((128, 128))
    minus[...] = jnp.full(minus.shape, -1.0, BF16)

    def setup(b, carry):
        row_dot = pay_ref[b, 128:136, 128:256]
        high = row_dot.astype(BF16).astype(F32)
        middle = (row_dot - high).astype(BF16).astype(F32)
        dots = columns_of(jnp.concatenate([high, middle, row_dot - high - middle], axis=0))
        for pair in range(4):
            grad = pay_ref[b, 0:128, 128 * pair : 128 * pair + 128]
            for side in range(2):
                rows = slice(128 * side, 128 * side + 128)
                mine = lane >= 64 if side else lane < 64
                g_high, g_low = split(jnp.where(mine, grad, 0.0))
                gn[b, pair, rows, 0:128] = g_high
                gn[b, pair, rows, 128:256] = g_low
                own_dot = jnp.logical_and(lane < 24, lax.rem(lane, 8) == 2 * pair + side)
                gn[b, pair, rows, 256:384] = jnp.where(own_dot, dots, 0.0).astype(BF16)
            t_high, t_low = split(grad.T)
            gt[b, pair, :, 0:128] = t_high
            gt[b, pair, :, 128:256] = t_low
        return carry

    lax.fori_loop(0, 8, setup, 0)

    ddst[...] = jnp.zeros(ddst.shape, F32)
    dsrc[...] = jnp.zeros(dsrc.shape, F32)
    dh[...] = jnp.zeros(dh.shape, F32)
    dh[spot[0]] = self_ref[...]
    high, reach = peaks(b_ref)
    close = reach < SPAN
    pltpu.make_async_copy(masks, mask_ref, sems.at[8]).wait()
    pltpu.make_async_copy(group.at[:, pl.ds(128, 8), pl.ds(128, 128)], a_ref, sems.at[9]).wait()

    def put(kind, b, h, tile):
        (abc, top)[kind][b * 8 + h] = tile

    def accumulate(weight):
        def step(k, carry):
            b, c = blocks[2 * k], blocks[2 * k + 1]
            keep = mask_ref[k] > 0
            for pair in range(4):
                g_high, h_high = gn[b, pair, :, 0:128], hb[c, pair, 0:128]
                d_alpha = dot(
                    jnp.concatenate([g_high, g_high, gn[b, pair, :, 128:384]], axis=1),
                    jnp.concatenate([h_high, hb[c, pair, 128:256], h_high, minus[...]], axis=1),
                    NT,
                )
                highs, lows = [], []
                for side in range(2):
                    h = 2 * pair + side
                    w, positive = weight(b, c, h, keep)
                    d_raw = w * d_alpha[128 * side : 128 * side + 128]
                    d_raw = jnp.where(positive, d_raw, 0.2 * d_raw)
                    ddst[b * 8 + h] += d_raw
                    dsrc[c * 8 + h] += jnp.sum(d_raw.reshape(16, 8, 128), axis=0)
                    w_high, w_low = split(w)
                    highs.append(w_high)
                    lows.append(w_low)
                w_high, w_low = jnp.concatenate(highs, axis=1), jnp.concatenate(lows, axis=1)
                both = dot(
                    jnp.concatenate([gt[b, pair], gt[b, pair, :, 0:128]], axis=1),
                    jnp.concatenate([w_high, w_high, w_low], axis=0),
                )
                dh[c, 128 * pair : 128 * pair + 64] += both[0:64, 0:128]
                dh[c, 128 * pair + 64 : 128 * pair + 128] += both[64:128, 128:256]
            return carry

        lax.fori_loop(0, counts[0], step, 0)

    @pl.when(close)
    def _():
        source_factors(b_ref, high, factors)
        spread_rows(lambda b: target_factors(a_ref[b], high, pay_ref[b, 128:136, 0:128]), put)
        features.wait()

        def weight(b, c, h, keep):
            one = abc[b * 8 + h] * factors[c, pl.ds(h, 1)]
            two = top[b * 8 + h] * factors[c, pl.ds(8 + h, 1)]
            return jnp.where(keep, jnp.maximum(one, two), 0.0), one > two

        accumulate(weight)

    @pl.when(jnp.logical_not(close))
    def _():
        spread_rows(lambda b: [a_ref[b], pay_ref[b, 128:136, 0:128]], put)
        features.wait()

        def weight(b, c, h, keep):
            raw = abc[b * 8 + h] + jnp.where(keep, b_ref[c, pl.ds(h, 1)], NEG)
            return jnp.exp2(leaky(raw) - top[b * 8 + h]), raw > 0

        accumulate(weight)

    for i in range(8):
        arrive(i).wait()

    def group_half(b, side):
        part = group.at[b, pl.ds(0, 128), pl.ds(128 * side, 128)]
        return pltpu.make_async_copy(part, abc.at[2 * b + side], group_sems.at[2 * b + side])

    for b in range(8):
        for side in range(2):
            group_half(b, side).start()

    def pack_dst(b, carry):
        ddst_out[b] = jnp.concatenate(
            [jnp.sum(ddst[b * 8 + h].T, axis=0, keepdims=True) for h in range(8)], axis=0
        )
        return carry

    lax.fori_loop(0, 8, pack_dst, 0)
    ddst_out[spot[1]] += dself_ref[...]

    high, low = split(p_ref[...])
    p_wide[:, 0:512] = high
    p_wide[:, 512:1024] = low
    p_wide[:, 1024:1536] = high
    att_cols = columns_of(jnp.concatenate([att_ref[...], jnp.zeros((8, 64), F32)], axis=1))
    for h in range(8):
        att_wide[64 * h : 64 * h + 64] = jnp.broadcast_to(att_cols[0:64, h : h + 1], (64, 128))
    dp_out[...] = jnp.zeros(dp_out.shape, F32)
    own = spot[0]

    def leave(four, slot):
        return pltpu.make_async_copy(dx_slots.at[slot], dx_out.at[pl.ds(4 * four, 4)], dx_sems.at[slot])

    def project(four, carry):
        wide_dh, wide_src = [], []
        for s in range(4):
            c = 4 * four + s
            d_src = jnp.concatenate(
                [jnp.sum(dsrc[c * 8 + h], axis=0, keepdims=True) for h in range(8)], axis=0
            )
            d_src = d_src + jnp.where(c == own, dself_ref[...], 0.0)
            spread = jnp.concatenate(
                [att_wide[64 * h : 64 * h + 64] * d_src[h : h + 1] for h in range(8)], axis=0
            )
            wide_dh.append(dh[c] + spread)
            wide_src.append(jnp.concatenate([d_src, jnp.zeros((8, 128), F32)], axis=0))
        high, low = split(jnp.concatenate(wide_dh, axis=1))
        s_high, s_low = split(jnp.concatenate(wide_src, axis=1))
        x_high, x_low = split(jnp.concatenate([x_ref[4 * four + s, 0:128] for s in range(4)], axis=0))
        dx = dot(p_wide[...], jnp.concatenate([high, high, low], axis=0))
        slot = lax.rem(four, 2)

        @pl.when(four >= 2)
        def _():
            leave(four - 2, slot).wait()

        for s in range(4):
            dx_slots[slot, s] = dx[:, 128 * s : 128 * s + 128]
        leave(four, slot).start()
        tall_high = jnp.concatenate([high, s_high], axis=0)
        tall_low = jnp.concatenate([low, s_low], axis=0)
        dp_out[...] += dot(
            jnp.concatenate([tall_high, tall_high, tall_low], axis=1),
            jnp.concatenate([x_high, x_low, x_high], axis=0),
        )
        return carry

    lax.fori_loop(0, 8, project, 0)
    u = jnp.zeros((8, 256), F32)
    for b in range(8):
        for side in range(2):
            group_half(b, side).wait()
        u += dot(ddst_out[b], jnp.concatenate([abc[2 * b], abc[2 * b + 1]], axis=1), NN, HIGHEST)
    for i in range(32):
        w_out[i, 0:16] = dp_out[16 * i : 16 * i + 16, 0:128]
        w_out[i, 16:32] = dp_out[16 * i : 16 * i + 16, 128:256]
        w_out[i, 32:40] = jnp.zeros((8, 128), F32)
    for h in range(8):
        for side in range(2):
            span = slice(128 * side, 128 * side + 128)
            w_out[h + 16 * side, 32:33] = u[h : h + 1, span]
            w_out[8 + h + 16 * side, 32:33] = dp_out[512 + h : 513 + h, span]
    leave(6, 0).wait()
    leave(7, 1).wait()


def backward_local(blocks, counts, spot, panel, proj, att_src, group, masks, pays, dh_self, d_self, hb, b):
    return pl.pallas_call(
        backward_body,
        out_shape=(
            jax.ShapeDtypeStruct((32, 256, 128), F32),
            jax.ShapeDtypeStruct((32, 40, 128), F32),
            jax.ShapeDtypeStruct((8, 8, 128), F32),
        ),
        in_specs=[SMEM] * 3 + [ANY, VMEM, VMEM, ANY, ANY, VMEM, VMEM, VMEM, ANY, VMEM],
        out_specs=(ANY, VMEM, VMEM),
        scratch_shapes=[
            pltpu.VMEM((32, 4, 256, 128), BF16),
            pltpu.VMEM((8, 4, 256, 384), BF16),
            pltpu.VMEM((8, 4, 128, 256), BF16),
            pltpu.VMEM((64, 128, 128), F32),
            pltpu.VMEM((64, 128, 128), F32),
            pltpu.VMEM((128, 128), BF16),
            pltpu.VMEM((64, 128, 128), F32),
            pltpu.VMEM((256, 8, 128), F32),
            pltpu.VMEM((32, 512, 128), F32),
            pltpu.VMEM((256, 1536), BF16),
            pltpu.VMEM((512, 128), F32),
            pltpu.VMEM((2, 4, 256, 128), F32),
            pltpu.SemaphoreType.DMA((2,)),
            pltpu.VMEM((528, 256), F32),
            pltpu.SemaphoreType.DMA((16,)),
            pltpu.SemaphoreType.DMA,
            pltpu.VMEM((32, 16, 128), F32),
            pltpu.VMEM((8, 8, 128), F32),
            pltpu.VMEM((32, 136, 256), F32),
            pltpu.VMEM((32, 128, 128), jnp.int32),
            pltpu.SemaphoreType.DMA((10,)),
        ],
        compiler_params=pltpu.CompilerParams(vmem_limit_bytes=BIG_VMEM),
    )(blocks, counts, spot, panel, proj, att_src, group, masks, pays, dh_self, d_self, hb, b)


def reduce_body(
    dx_ref, w_ref, ddst_ref, dx_out, dp_out, dst_out,
    send, recv, twin_dx, twin_w, total, far, near, far2, near2, dst_all, merged, plane, joined, tower,
):
    d, y, x, k, z = place()
    sibling = node(y, x, 1 - k)
    chip = y * 4 + x
    offsets = [(dy, dx) for dy in range(4) for dx in range(4) if (dy, dx) != (0, 0)]
    others = [lax.rem(z + s, 8) for s in range(1, 8)]
    wait_all = greet([sibling] + [node(y + dy, x + dx, k) for dy, dx in offsets], others)
    links = Links(send, recv)
    wait_all()

    def rank(offset):
        return 0 if 2 in offset else (2 if offset == (0, 0) else 1)

    cells = sorted([(0, 0)] + offsets, key=rank)
    twin_weights = links.push(w_ref.at[:, 1 - k], twin_w, dst=sibling)
    twin_copies = {}
    for dy, dx in cells:
        yy, xx = lax.rem(y + dy, 4), lax.rem(x + dx, 4)
        twin_copies[dy, dx] = links.push(dx_ref.at[yy, xx, 1 - k], twin_dx.at[yy, xx], dst=sibling)
    twin_weights.wait_recv()
    merged[...] = w_ref[:, k] + twin_w[...]
    plane_copies = []
    for dy, dx in offsets:
        target = lax.rem(y + dy, 4) * 4 + lax.rem(x + dx, 4)
        plane_copies.append(links.push(merged.at[target], plane.at[chip], dst=node(y + dy, x + dx, k)))
    dst_copies = [links.push(ddst_ref.at[t], dst_all.at[z], src=t) for t in others]

    def add_cells(wanted):
        for dy, dx in cells:
            if rank((dy, dx)) == wanted:
                yy, xx = lax.rem(y + dy, 4), lax.rem(x + dx, 4)
                twin_copies[dy, dx].wait_recv()
                total[yy, xx] = dx_ref[yy, xx, k] + twin_dx[yy, xx]

    def ring(region, plus, minus, far_buf, near_buf):
        c0 = links.push(region(2, 0), far_buf.at[0], dst=plus)
        c1 = links.push(region(2, 1), far_buf.at[1], dst=minus)
        yield
        c2 = links.push(region(1, 1), near_buf.at[0], dst=plus)
        c3 = links.push(region(-1, 0), near_buf.at[1], dst=minus)
        yield
        c0.wait_recv()
        part = region(1, 0)
        part[...] += far_buf[0]
        c4 = links.push(part, near_buf.at[2], dst=plus)
        yield
        c1.wait_recv()
        part = region(-1, 1)
        part[...] += far_buf[1]
        c5 = links.push(part, near_buf.at[3], dst=minus)
        for copy, index, piece in ((c2, 0, 1), (c3, 1, 0), (c4, 2, 0), (c5, 3, 1)):
            yield
            copy.wait_recv()
            part = region(0, piece)
            part[...] += near_buf[index]

    def grads(half):
        rows = pl.ds(128 * half, 128)

        def wide(v, piece):
            if half == 0:
                return total.at[lax.rem(y + v + 4, 4), pl.ds(2 * piece, 2), rows]
            return total.at[pl.ds(2 * piece, 2), lax.rem(x + v + 4, 4), rows]

        def narrow(u, piece):
            span = pl.ds(128 * half + 64 * piece, 64)
            if half == 0:
                return total.at[y, lax.rem(x + u + 4, 4), span]
            return total.at[lax.rem(y + u + 4, 4), x, span]

        along_y = (node(y + 1, x, k), node(y - 1, x, k))
        along_x = (node(y, x + 1, k), node(y, x - 1, k))
        first, then = (along_y, along_x) if half == 0 else (along_x, along_y)
        yield from ring(wide, *first, far.at[half], near.at[half])
        yield from ring(narrow, *then, far2.at[half], near2.at[half])

    chains = [grads(0), grads(1)]

    def advance(count):
        for _ in range(count):
            for chain in chains:
                next(chain)

    add_cells(0)
    advance(1)
    add_cells(1)
    advance(1)
    add_cells(2)
    plane[chip] = merged[chip]
    for copy in plane_copies:
        copy.wait_recv()
    value = plane[0]
    for i in range(1, 16):
        value = value + plane[i]
    joined[...] = value
    tower[z] = value
    tower_copies = [links.push(joined, tower.at[z], src=t) for t in others]
    advance(2)
    for copy in tower_copies:
        copy.wait_recv()
    value = tower[0]
    for i in range(1, 8):
        value = value + tower[i]
    dp_out[chip, k] = value
    spread_copies = [
        links.push(dp_out.at[chip, k], dp_out.at[chip, k], dst=node(y + dy, x + dx, k)) for dy, dx in offsets
    ]
    advance(7)
    for copy in spread_copies:
        copy.wait_recv()
    over = links.push(dp_out.at[:, k], dp_out.at[:, k], dst=sibling)
    run_chains(chains)
    dx_out[...] = total[y, x]
    for copy in dst_copies:
        copy.wait_recv()
    dst_all[z] = ddst_ref[z]
    dst_total = dst_all[0]
    for t in range(1, 8):
        dst_total = dst_total + dst_all[t]
    dst_out[...] = dst_total
    over.wait_recv()
    links.drain()


def reduce_grads(dx, w, ddst):
    count = 1 + 16 + 15 + 7 + 24 + 7 + 15 + 1
    return pl.pallas_call(
        reduce_body,
        out_shape=(
            jax.ShapeDtypeStruct((256, 128), F32),
            jax.ShapeDtypeStruct((16, 2, 40, 128), F32),
            jax.ShapeDtypeStruct((8, 128), F32),
        ),
        in_specs=[VMEM] * 3,
        out_specs=(VMEM,) * 3,
        scratch_shapes=[
            pltpu.SemaphoreType.DMA((count,)),
            pltpu.SemaphoreType.DMA((count,)),
            pltpu.VMEM((4, 4, 256, 128), F32),
            pltpu.VMEM((16, 40, 128), F32),
            pltpu.VMEM((4, 4, 256, 128), F32),
            pltpu.VMEM((2, 2, 2, 128, 128), F32),
            pltpu.VMEM((2, 4, 2, 128, 128), F32),
            pltpu.VMEM((2, 2, 64, 128), F32),
            pltpu.VMEM((2, 4, 64, 128), F32),
            pltpu.VMEM((8, 8, 128), F32),
            pltpu.VMEM((16, 40, 128), F32),
            pltpu.VMEM((16, 40, 128), F32),
            pltpu.VMEM((40, 128), F32),
            pltpu.VMEM((8, 40, 128), F32),
        ],
        compiler_params=pltpu.CompilerParams(
            collective_id=2, has_side_effects=True, vmem_limit_bytes=BIG_VMEM
        ),
    )(dx.reshape(4, 4, 2, 256, 128), w.reshape(16, 2, 40, 128), ddst)


def finish_body(dx_ref, w_ref, dst_ref, p_ref, dst_att_ref, in_ref, proj_ref, src_ref, dst_out):
    proj = p_ref[...]
    a_rows = per_head_rows(dst_att_ref[...])
    score = dot(a_rows, proj, NT, HIGHEST)
    pad = jnp.zeros((120, 256), F32)
    score_t = jnp.concatenate([score, pad], axis=0).T
    dst_wide = jnp.concatenate([dst_ref[...], jnp.zeros((120, 128), F32)], axis=0)
    in_ref[...] = (dx_ref[...] + dot(score_t, dst_wide, NN, HIGHEST)).T

    def row(i):
        return jnp.concatenate([w_ref[i, 32:33], w_ref[i + 16, 32:33]], axis=1)

    u = jnp.concatenate([row(h) for h in range(8)], axis=0)
    v = jnp.concatenate([row(8 + h) for h in range(8)], axis=0)
    wide_u = jnp.concatenate([u, jnp.zeros((120, 256), F32)], axis=0)
    att = jnp.concatenate([a_rows, jnp.zeros((120, 512), F32)], axis=0)
    grad_t = jnp.concatenate(
        [jnp.concatenate([w_ref[i, 0:16], w_ref[i, 16:32]], axis=1) for i in range(32)], axis=0
    )
    proj_ref[...] = (grad_t + dot(att.T, wide_u, NN, HIGHEST)).T
    both = dot(jnp.concatenate([u, v], axis=0), proj, NN, HIGHEST)
    dst_out[...] = jnp.concatenate([both[h : h + 1, 64 * h : 64 * h + 64] for h in range(8)], axis=0)
    src_ref[...] = jnp.concatenate([both[8 + h : 9 + h, 64 * h : 64 * h + 64] for h in range(8)], axis=0)


def finish(dx, weights, dst_total, proj, att_dst):
    return pl.pallas_call(
        finish_body,
        out_shape=(
            jax.ShapeDtypeStruct((128, 256), F32),
            jax.ShapeDtypeStruct((256, 512), F32),
            jax.ShapeDtypeStruct((8, 64), F32),
            jax.ShapeDtypeStruct((8, 64), F32),
        ),
        in_specs=[VMEM] * 5,
        out_specs=(VMEM,) * 4,
    )(dx, weights.reshape(32, 40, 128), dst_total, proj, att_dst)


def shards(inputs, projection, att_src, att_dst, blocks, counts, tile_masks, cotangent):
    coords = blocks.reshape(64)
    live = counts.reshape(1)
    masks = tile_masks[0, 0]
    spot = jnp.stack([lax.axis_index("dst"), lax.axis_index("src")]).astype(jnp.int32)
    panel, group, own = gather_inputs(inputs, projection, att_src, att_dst)
    acc, hb, b = forward_local(coords, live, panel, projection, group, masks)
    output, pays, dh_self, d_self = exchange(acc, inputs, projection, own, cotangent)
    dx, w, ddst = backward_local(
        coords, live, spot, panel, projection, att_src, group, masks, pays, dh_self, d_self, hb, b
    )
    dx_own, weights, dst_total = reduce_grads(dx, w, ddst)
    in_grad, proj_grad, src_grad, dst_grad = finish(dx_own, weights, dst_total, projection, att_dst)
    return (output, in_grad, proj_grad, src_grad, dst_grad)


def solution(mesh):
    in_specs = (
        P(("dst", "src"), None),
        P(),
        P(),
        P(),
        P("dst", "src", None, None),
        P("dst", "src"),
        P("dst", "src", None, None, None),
        P(("dst", "src"), None),
    )
    out_specs = (P(("dst", "src"), None), P(("dst", "src"), None), P(), P(), P())
    return jax.shard_map(shards, mesh=mesh, in_specs=in_specs, out_specs=out_specs, check_vma=False)
```

```python
import functools

import jax
import jax.numpy as jnp
from jax import lax
from jax.experimental import pallas as pl
from jax.experimental.pallas import tpu as pltpu
from jax.sharding import PartitionSpec as P

HIGHEST = lax.Precision.HIGHEST
F32 = jnp.float32
BF16 = jnp.bfloat16
LOG2E = 1.4426950408889634
NEG = -1e30
MESH = pl.DeviceIdType.MESH
VMEM = pl.BlockSpec(memory_space=pltpu.VMEM)
SMEM = pl.BlockSpec(memory_space=pltpu.SMEM)
ANY = pl.BlockSpec(memory_space=pl.ANY)
NN = (((1,), (0,)), ((), ()))
NT = (((1,), (1,)), ((), ()))
BIG_VMEM = 60 * 1024 * 1024


def dot(a, b, dims=NN, precision=None):
    return lax.dot_general(a, b, dims, precision=precision, preferred_element_type=F32)


def split(value):
    high = value.astype(BF16)
    return high, (value - high.astype(F32)).astype(BF16)


def leaky(raw):
    return jnp.maximum(raw, 0.2 * raw)


def per_head_rows(att):
    wide = jnp.concatenate([att] * 8, axis=1)
    head = lax.broadcasted_iota(jnp.int32, wide.shape, 0)
    column = lax.broadcasted_iota(jnp.int32, wide.shape, 1)
    return jnp.where(column // 64 == head, wide, 0.0)


def score_rows(att, proj):
    return dot(per_head_rows(att), proj, NT, HIGHEST)


def lanes(shape):
    return lax.broadcasted_iota(jnp.int32, shape, len(shape) - 1)


def place():
    d = lax.axis_index("dst")
    z = lax.axis_index("src")
    return d, d // 8, lax.rem(d // 2, 4), lax.rem(d, 2), z


def node(y, x, k):
    return lax.rem(y + 8, 4) * 8 + lax.rem(x + 8, 4) * 2 + k


class Links:
    def __init__(self, send, recv):
        self.send, self.recv, self.used, self.open = send, recv, 0, []

    def push(self, source, landing, **target):
        copy = pltpu.make_async_remote_copy(
            src_ref=source,
            dst_ref=landing,
            send_sem=self.send.at[self.used],
            recv_sem=self.recv.at[self.used],
            device_id=target,
            device_id_type=MESH,
        )
        self.used += 1
        copy.start()
        self.open.append(copy)
        return copy

    def drain(self):
        for copy in self.open:
            copy.wait_send()


def greet(dsts, srcs):
    barrier = pltpu.get_barrier_semaphore()
    for other in dsts:
        pl.semaphore_signal(barrier, inc=1, device_id={"dst": other}, device_id_type=MESH)
    for other in srcs:
        pl.semaphore_signal(barrier, inc=1, device_id={"src": other}, device_id_type=MESH)
    return lambda: pl.semaphore_wait(barrier, len(dsts) + len(srcs))


def run_chains(chains):
    chains = list(chains)
    while chains:
        for chain in list(chains):
            try:
                next(chain)
            except StopIteration:
                chains.remove(chain)


def around(links, own_ref, all_ref, z):
    spans = (pl.ds(0, 64), pl.ds(64, 72))
    right, left = lax.rem(z + 1, 8), lax.rem(z + 7, 8)

    def push(step, way, sub):
        block = lax.rem(z + 8 - step, 8) if way == 0 else lax.rem(z + step, 8)
        part = all_ref.at[block, spans[sub]]
        source = own_ref.at[spans[sub]] if step == 0 else part
        return links.push(source, part, src=right if way == 0 else left)

    order = [(way, sub) for sub in range(2) for way in range(2)]
    coming = {item: push(0, *item) for item in order}
    for step in range(1, 4):
        for item in order:
            yield
            coming[item].wait_recv()
            if step < 3 or item[0] == item[1]:
                coming[item] = push(step, *item)
            else:
                del coming[item]
    for copy in list(coming.values()):
        yield
        copy.wait_recv()


def gather_body(x_ref, p_ref, src_ref, dst_ref, panel_ref, group_ref, own_ref, pay, send, recv, own_sem):
    d, y, x, k, z = place()
    sibling = node(y, x, 1 - k)
    wait_all = greet(
        [sibling, node(y + 1, x, k), node(y - 1, x, k), node(y, x + 1, k), node(y, x - 1, k)],
        [lax.rem(z + 1, 8), lax.rem(z + 7, 8)],
    )
    rows = jnp.concatenate([score_rows(r[...], p_ref[...]) for r in (src_ref, dst_ref)], axis=0) * LOG2E
    scores = dot(rows, x_ref[...], NT, HIGHEST)
    pay[0:128] = x_ref[...]
    pay[128:136, 0:128] = scores[0:8]
    pay[128:136, 128:256] = scores[8:16]
    own_ref[...] = scores
    own_copies = [
        pltpu.make_async_copy(pay, panel_ref.at[d], own_sem.at[0]),
        pltpu.make_async_copy(pay, group_ref.at[z], own_sem.at[1]),
    ]
    for copy in own_copies:
        copy.start()
    wait_all()
    links = Links(send, recv)

    def chain(half):
        def at(u, v):
            return node(y + v, x + u, k) if half == 0 else node(y + u, x + v, k)

        def region(u, v, quarter=None):
            start, size = 64 * half, 64 + 8 * half
            if quarter is not None:
                start, size = start + 32 * quarter, 32 + 8 * half * quarter
            return panel_ref.at[at(u, v), pl.ds(start, size)]

        def to(part, du, dv, src=None):
            return links.push(part if src is None else src, part, dst=at(du, dv))

        def twin(u, v, src=None):
            part = region(u, v)
            return links.push(part if src is None else src, part, dst=sibling)

        own = pay.at[pl.ds(64 * half, 64 + 8 * half)]
        first = [to(region(0, 0), 1, 0, own), to(region(0, 0), -1, 0, own)]
        second = {0: [to(region(0, 0), 0, 1, own), to(region(0, 0), 0, -1, own)]}
        twins = [twin(0, 0, own)]
        last = {}

        def spread(u):
            second[u] = [to(region(u, 0), 0, 1), to(region(u, 0), 0, -1)]
            twins.append(twin(u, 0))

        def relay(u):
            pair = []
            for index, v in ((0, -1), (1, 1)):
                yield
                second[u][index].wait_recv()
                pair.append(to(region(u, v, index), 0, -v))
                twins.append(twin(u, v))
            last[u] = pair

        def finish(u):
            yield
            for copy in last[u]:
                copy.wait_recv()
            twins.append(twin(u, 2))

        far = []
        for index, u in ((0, -1), (1, 1)):
            yield
            first[index].wait_recv()
            far.append(to(region(u, 0, index), -u, 0))
            spread(u)
        yield from relay(0)
        yield
        for copy in far:
            copy.wait_recv()
        spread(2)
        yield from relay(-1)
        yield from relay(1)
        yield from finish(0)
        yield from relay(2)
        yield from finish(-1)
        yield from finish(1)
        yield from finish(2)
        yield
        for copy in twins:
            copy.wait_recv()

    run_chains([chain(0), chain(1), around(links, pay, group_ref, z)])
    for copy in own_copies:
        copy.wait()
    links.drain()


def gather_inputs(x, proj, att_src, att_dst):
    count = 72 + 14
    return pl.pallas_call(
        gather_body,
        out_shape=(
            jax.ShapeDtypeStruct((32, 136, 256), F32),
            jax.ShapeDtypeStruct((8, 136, 256), F32),
            jax.ShapeDtypeStruct((16, 128), F32),
        ),
        in_specs=[VMEM] * 4,
        out_specs=(ANY, ANY, VMEM),
        scratch_shapes=[
            pltpu.VMEM((136, 256), F32),
            pltpu.SemaphoreType.DMA((count,)),
            pltpu.SemaphoreType.DMA((count,)),
            pltpu.SemaphoreType.DMA((2,)),
        ],
        compiler_params=pltpu.CompilerParams(collective_id=0, has_side_effects=True),
    )(x, proj, att_src, att_dst)


def split_weights(p_ref, p_cat):
    high, low = split(p_ref[...])
    p_cat[0:256] = high
    p_cat[256:512] = low
    p_cat[512:768] = high


def stream_in(panel, x_ref, masks, mask_ref, group, a_ref, sems):
    def part(i):
        span = pl.ds(4 * i, 4)
        return pltpu.make_async_copy(panel.at[span], x_ref.at[span], sems.at[i])

    for i in range(8):
        part(i).start()
    pltpu.make_async_copy(masks, mask_ref, sems.at[8]).start()
    pltpu.make_async_copy(group.at[:, pl.ds(128, 8), pl.ds(128, 128)], a_ref, sems.at[9]).start()
    return part


def prepare_features(x_ref, p_cat, hb, arrive, leave):
    n = 4

    def step(group, carry):
        arrive(group).wait()
        x_high, x_low = split(jnp.concatenate([x_ref[group * n + s, 0:128] for s in range(n)], axis=0))
        left = jnp.concatenate([x_high, x_high, x_low], axis=1)
        for wide in range(2):
            h_high, h_low = split(dot(left, p_cat[:, 256 * wide : 256 * wide + 256]))
            for s in range(n):
                for side in range(2):
                    part = (slice(128 * s, 128 * s + 128), slice(128 * side, 128 * side + 128))
                    pair = 2 * wide + side
                    hb[group * n + s, pair, 0:128] = h_high[part]
                    hb[group * n + s, pair, 128:256] = h_low[part]
        leave(group).start()
        return carry

    lax.fori_loop(0, 32 // n, step, 0)


def columns_of(rows):
    pad = jnp.zeros((128 - rows.shape[0], 128), F32)
    return jnp.concatenate([rows, pad], axis=0).T


def spread_rows(rows_of, put):
    parts = []
    for b in range(8):
        kinds = rows_of(b)
        pieces = []
        for rows in kinds:
            high = rows.astype(BF16).astype(F32)
            middle = (rows - high).astype(BF16).astype(F32)
            pieces += [high, middle, rows - high - middle]
        parts.append(columns_of(jnp.concatenate(pieces, axis=0)).astype(BF16))
    left = jnp.concatenate(parts, axis=0)
    count = len(kinds)
    row = lax.broadcasted_iota(jnp.int32, (128, 128 * count), 0)
    kind = lax.broadcasted_iota(jnp.int32, (128, 128 * count), 1) // 128
    for h in range(8):
        pick = jnp.logical_and(row // 24 == kind, lax.rem(row, 8) == h)
        out = dot(left, jnp.where(pick, 1.0, 0.0).astype(BF16))
        for k in range(count):
            for b in range(8):
                put(k, b, h, out[128 * b : 128 * b + 128, 128 * k : 128 * k + 128])


SPAN = 40.0


def peaks(scores):
    high, low = scores[0], scores[0]
    for c in range(1, 32):
        high, low = jnp.maximum(high, scores[c]), jnp.minimum(low, scores[c])
    high, low = jnp.max(high, axis=1, keepdims=True), jnp.min(low, axis=1, keepdims=True)
    return high, jnp.max(high - low)


def source_factors(scores, high, factors):
    for c in range(32):
        below = scores[c] - high
        factors[c, 0:8] = jnp.exp2(below)
        factors[c, 8:16] = jnp.exp2(0.2 * below)


def target_factors(a, high, shift):
    best = a + high
    return [jnp.exp2(jnp.minimum(part - shift, 100.0)) for part in (best, 0.2 * best)]


def forward_body(
    blocks, counts, panel, p_ref, group, masks, acc_out, hb_out, b_out,
    p_cat, hb, top, abc, sums, acc, top_rows, factors, hb_sems, a_ref, x_ref, mask_ref, sems
):
    arrive = stream_in(panel, x_ref, masks, mask_ref, group, a_ref, sems)

    def leave(i):
        span = pl.ds(4 * i, 4)
        return pltpu.make_async_copy(hb.at[span], hb_out.at[span], hb_sems.at[i])

    split_weights(p_ref, p_cat)
    prepare_features(x_ref, p_cat, hb, arrive, leave)
    pltpu.make_async_copy(masks, mask_ref, sems.at[8]).wait()
    pltpu.make_async_copy(group.at[:, pl.ds(128, 8), pl.ds(128, 128)], a_ref, sems.at[9]).wait()
    b_out[...] = x_ref[:, 128:136, 0:128]
    sums[...] = jnp.zeros(sums.shape, F32)
    acc[...] = jnp.zeros(acc.shape, F32)
    live = counts[0]
    high, reach = peaks(b_out)
    close = reach < SPAN

    def put(kind, b, h, tile):
        (abc, top)[kind][b * 8 + h] = tile

    def accumulate(weight):
        lane = lanes((128, 128))

        def slot(k, keep):
            b, c = blocks[2 * k], blocks[2 * k + 1]
            for pair in range(4):
                sides = []
                for h in (2 * pair, 2 * pair + 1):
                    w = weight(b, c, h, keep)
                    sums[b * 8 + h] += w
                    w_high, w_low = split(w)
                    sides.append(jnp.concatenate([w_high, w_high, w_low], axis=1))
                right = jnp.concatenate([hb[c, pair], hb[c, pair, 0:128]], axis=0)
                both = dot(jnp.concatenate(sides, axis=0), right)
                acc[b * 4 + pair] += jnp.where(lane < 64, both[0:128], both[128:256])

        def step(two, carry):
            slot(2 * two, mask_ref[2 * two] > 0)
            slot(2 * two + 1, mask_ref[2 * two + 1] * jnp.where(2 * two + 1 < live, 1, 0) > 0)
            return carry

        lax.fori_loop(0, (live + 1) // 2, step, 0)

    @pl.when(close)
    def _():
        source_factors(b_out, high, factors)
        for b in range(8):
            top_rows[b] = leaky(a_ref[b] + high)
        spread_rows(lambda b: target_factors(a_ref[b], high, top_rows[b]), put)

        def weight(b, c, h, keep):
            one = abc[b * 8 + h] * factors[c, pl.ds(h, 1)]
            two = top[b * 8 + h] * factors[c, pl.ds(8 + h, 1)]
            return jnp.where(keep, jnp.maximum(one, two), 0.0)

        accumulate(weight)

    @pl.when(jnp.logical_not(close))
    def _():
        top[...] = jnp.full(top.shape, NEG, F32)

        def find_top(k, carry):
            b, c = blocks[2 * k], blocks[2 * k + 1]
            keep = mask_ref[k] > 0
            for h in range(8):
                top[b * 8 + h] = jnp.maximum(top[b * 8 + h], jnp.where(keep, b_out[c, pl.ds(h, 1)], NEG))
            return carry

        lax.fori_loop(0, live, find_top, 0)

        def find_rows(b, carry):
            best = jnp.concatenate([jnp.max(top[b * 8 + h].T, axis=0, keepdims=True) for h in range(8)], axis=0)
            top_rows[b] = leaky(a_ref[b] + best)
            return carry

        lax.fori_loop(0, 8, find_rows, 0)
        spread_rows(lambda b: [a_ref[b], top_rows[b]], put)

        def weight(b, c, h, keep):
            raw = abc[b * 8 + h] + jnp.where(keep, b_out[c, pl.ds(h, 1)], NEG)
            return jnp.exp2(leaky(raw) - top[b * 8 + h])

        accumulate(weight)

    def pack(b, carry):
        totals = [jnp.sum(sums[b * 8 + h].T, axis=0, keepdims=True) for h in range(8)]
        tops = [
            jnp.where(totals[h] > 0, top_rows[b, h : h + 1], 0.2 * NEG) for h in range(8)
        ]
        for way in range(2):
            for inner in range(2):
                h = 4 * way + 2 * inner
                packed = jnp.concatenate(
                    tops[h : h + 2] + totals[h : h + 2] + [jnp.zeros((4, 128), F32)], axis=0
                )
                for half in range(2):
                    sub = 2 * inner + half
                    acc_out[b, way, sub, 0:64] = acc[b * 4 + 2 * way + inner][64 * half : 64 * half + 64]
                    acc_out[b, way, sub, 64:72] = packed
        return carry

    lax.fori_loop(0, 8, pack, 0)
    for i in range(8):
        leave(i).wait()


def forward_local(blocks, counts, panel, proj, group, masks):
    return pl.pallas_call(
        forward_body,
        out_shape=(
            jax.ShapeDtypeStruct((8, 2, 4, 72, 128), F32),
            jax.ShapeDtypeStruct((32, 4, 256, 128), BF16),
            jax.ShapeDtypeStruct((32, 8, 128), F32),
        ),
        in_specs=[SMEM, SMEM, ANY, VMEM, ANY, ANY],
        out_specs=(VMEM, ANY, VMEM),
        scratch_shapes=[
            pltpu.VMEM((768, 512), BF16),
            pltpu.VMEM((32, 4, 256, 128), BF16),
            pltpu.VMEM((64, 128, 128), F32),
            pltpu.VMEM((64, 128, 128), F32),
            pltpu.VMEM((64, 128, 128), F32),
            pltpu.VMEM((32, 128, 128), F32),
            pltpu.VMEM((8, 8, 128), F32),
            pltpu.VMEM((32, 16, 128), F32),
            pltpu.SemaphoreType.DMA((8,)),
            pltpu.VMEM((8, 8, 128), F32),
            pltpu.VMEM((32, 136, 256), F32),
            pltpu.VMEM((32, 128, 128), jnp.int32),
            pltpu.SemaphoreType.DMA((10,)),
        ],
        compiler_params=pltpu.CompilerParams(vmem_limit_bytes=BIG_VMEM),
    )(blocks, counts, panel, proj, group, masks)


def merge(arrived, mine, half):
    one, two = arrived[64:72], mine[64:72]
    best = jnp.maximum(one[0:2], two[0:2])
    f_one, f_two = jnp.exp2(one[0:2] - best), jnp.exp2(two[0:2] - best)
    total = one[2:4] * f_one + two[2:4] * f_two
    cols = columns_of(jnp.concatenate([f_one, f_two, best, total], axis=0))[64 * half : 64 * half + 64]
    lane = lanes((64, 128))
    factor = [jnp.where(lane < 64, cols[:, s : s + 1], cols[:, s + 1 : s + 2]) for s in (0, 2)]
    values = arrived[0:64] * factor[0] + mine[0:64] * factor[1]
    return values, jnp.concatenate([best, total, one[4:8]], axis=0)


def exchange_body(
    acc_ref, x_ref, p_ref, own_ref, cot_ref, out_ref, all_ref, self_ref, dself_ref,
    slots, total, pay, h_own, send, recv, grad_send, grad_recv, own_sem,
):
    z = lax.axis_index("src")
    right, left = lax.rem(z + 1, 8), lax.rem(z + 7, 8)
    wait_all = greet([], [right, left])
    wait_all()

    def copy(step, way, sub):
        if isinstance(step, int) and step == 0:
            src = acc_ref.at[left if way == 0 else right, way, sub]
        else:
            src = slots.at[step - 1, way, sub]
        return pltpu.make_async_remote_copy(
            src_ref=src,
            dst_ref=slots.at[step, way, sub],
            send_sem=send.at[step, way, sub],
            recv_sem=recv.at[step, way, sub],
            device_id={"src": right if way == 0 else left},
            device_id_type=MESH,
        )

    order = [(way, sub) for sub in range(4) for way in range(2)]
    for way, sub in order:
        copy(0, way, sub).start()
    h_own[...] = dot(x_ref[...], p_ref[...], NN, HIGHEST)

    def block_of(step, way):
        return lax.rem(z + 15 - step, 8) if way == 0 else lax.rem(z + 1 + step, 8)

    def hop(step, carry):
        for way, sub in order:
            pltpu.make_async_remote_copy(
                src_ref=slots.at[step - 1, way, sub],
                dst_ref=slots.at[step - 1, way, sub],
                send_sem=send.at[step - 1, way, sub],
                recv_sem=recv.at[step - 1, way, sub],
                device_id={"src": right if way == 0 else left},
                device_id_type=MESH,
            ).wait_recv()
            values, stats = merge(slots[step - 1, way, sub], acc_ref[block_of(step, way), way, sub], sub % 2)
            slots[step - 1, way, sub, 0:64] = values
            slots[step - 1, way, sub, 64:72] = stats
            copy(step, way, sub).start()
        return carry

    lax.fori_loop(1, 7, hop, 0)
    for way, sub in order:
        last = copy(6, way, sub)
        last.wait_recv()
        values, stats = merge(slots[6, way, sub], acc_ref[z, way, sub], sub % 2)
        total[way, sub, 0:64] = values
        total[way, sub, 64:72] = stats
    owner_rows(total, own_ref, h_own, cot_ref, out_ref, pay, self_ref, dself_ref)
    own_copy = pltpu.make_async_copy(pay, all_ref.at[z], own_sem)
    own_copy.start()
    links = Links(grad_send, grad_recv)
    run_chains([around(links, pay, all_ref, z)])
    for step in range(7):
        for way, sub in order:
            copy(step, way, sub).wait_send()
    own_copy.wait()
    links.drain()


def exchange(acc, x, proj, own, cotangent):
    return pl.pallas_call(
        exchange_body,
        out_shape=(
            jax.ShapeDtypeStruct((128, 512), F32),
            jax.ShapeDtypeStruct((8, 136, 512), F32),
            jax.ShapeDtypeStruct((512, 128), F32),
            jax.ShapeDtypeStruct((8, 128), F32),
        ),
        in_specs=[VMEM] * 5,
        out_specs=(VMEM, ANY, VMEM, VMEM),
        scratch_shapes=[
            pltpu.VMEM((7, 2, 4, 72, 128), F32),
            pltpu.VMEM((2, 4, 72, 128), F32),
            pltpu.VMEM((136, 512), F32),
            pltpu.VMEM((128, 512), F32),
            pltpu.SemaphoreType.DMA((7, 2, 4)),
            pltpu.SemaphoreType.DMA((7, 2, 4)),
            pltpu.SemaphoreType.DMA((14,)),
            pltpu.SemaphoreType.DMA((14,)),
            pltpu.SemaphoreType.DMA,
        ],
        compiler_params=pltpu.CompilerParams(collective_id=1, has_side_effects=True),
    )(acc, x, proj, own, cotangent)


def minus_one(power):
    series = power * (1 + power * (1 / 2 + power * (1 / 6 + power * (1 / 24 + power * (1 / 120)))))
    return jnp.where(power > -0.1, series, jnp.exp(power) - 1)


def owner_rows(total_ref, own_ref, h_own, cot_ref, out_ref, pay_ref, self_ref, dself_ref):
    raw = own_ref[0:8] + own_ref[8:16]
    own = leaky(raw)
    parts = [total_ref[pair // 2, 2 * (pair % 2), 64:72] for pair in range(4)]
    tops = jnp.concatenate([part[0:2] for part in parts], axis=0)
    sums = jnp.concatenate([part[2:4] for part in parts], axis=0)
    best = jnp.maximum(tops, own)
    f_tot, f_own = jnp.exp2(tops - best), jnp.exp2(own - best)
    inverse = 1.0 / (sums * f_tot + f_own)
    slope = jnp.where(raw > 0, 1.0, 0.2)
    cols = columns_of(jnp.concatenate([f_tot * inverse, f_own * inverse, inverse, slope], axis=0))
    lane = lanes((128, 128))
    stats = jnp.zeros((128, 128), F32)
    for pair in range(4):
        way, inner = pair // 2, pair % 2
        span = slice(128 * pair, 128 * pair + 128)
        acc = jnp.concatenate([total_ref[way, 2 * inner + half, 0:64] for half in range(2)], axis=0)

        def wide(kind):
            s = 8 * kind + 2 * pair
            return jnp.where(lane < 64, cols[:, s : s + 1], cols[:, s + 1 : s + 2])

        alpha, h_pair = wide(1), h_own[:, span]
        agg = acc * wide(0) + h_pair * alpha
        low = jnp.minimum(agg, 0.0)
        out_ref[:, span] = jnp.where(agg > 0, agg, minus_one(low))
        grad = cot_ref[:, span] * jnp.where(agg > 0, 1.0, jnp.exp(low))
        pay_ref[0:128, span] = grad * wide(2)
        self_ref[span] = (grad * alpha).T
        for odd in range(2):
            h = 2 * pair + odd
            mine = lane >= 64 if odd else lane < 64
            row_dot = jnp.sum(jnp.where(mine, grad * agg, 0.0), axis=1, keepdims=True)
            d_alpha = jnp.sum(jnp.where(mine, grad * h_pair, 0.0), axis=1, keepdims=True)
            d_self = cols[:, 8 + h : 9 + h] * (d_alpha - row_dot) * cols[:, 24 + h : 25 + h]
            stats = jnp.where(lane == h, row_dot * cols[:, 16 + h : 17 + h], stats)
            stats = jnp.where(lane == 8 + h, d_self, stats)
    turned = stats.T
    pay_ref[128:136, 0:128] = best
    pay_ref[128:136, 128:256] = turned[0:8]
    pay_ref[128:136, 256:512] = jnp.zeros((8, 256), F32)
    dself_ref[...] = turned[8:16]


def backward_body(
    blocks, counts, spot, panel, p_ref, att_ref, group, masks, pay_ref, self_ref, dself_ref, hb_in, b_ref,
    dx_out, w_out, ddst_out, hb, gn, gt, top, abc, minus, ddst, dsrc, dh, p_wide, att_wide,
    dx_slots, dx_sems, dp_out, group_sems, hb_sem, factors, a_ref, x_ref, mask_ref, sems,
):
    features = pltpu.make_async_copy(hb_in, hb, hb_sem)
    features.start()
    arrive = stream_in(panel, x_ref, masks, mask_ref, group, a_ref, sems)
    lane = lanes((128, 128))
    minus[...] = jnp.full(minus.shape, -1.0, BF16)

    def setup(b, carry):
        row_dot = pay_ref[b, 128:136, 128:256]
        high = row_dot.astype(BF16).astype(F32)
        middle = (row_dot - high).astype(BF16).astype(F32)
        dots = columns_of(jnp.concatenate([high, middle, row_dot - high - middle], axis=0))
        for pair in range(4):
            grad = pay_ref[b, 0:128, 128 * pair : 128 * pair + 128]
            for side in range(2):
                rows = slice(128 * side, 128 * side + 128)
                mine = lane >= 64 if side else lane < 64
                g_high, g_low = split(jnp.where(mine, grad, 0.0))
                gn[b, pair, rows, 0:128] = g_high
                gn[b, pair, rows, 128:256] = g_low
                own_dot = jnp.logical_and(lane < 24, lax.rem(lane, 8) == 2 * pair + side)
                gn[b, pair, rows, 256:384] = jnp.where(own_dot, dots, 0.0).astype(BF16)
            t_high, t_low = split(grad.T)
            gt[b, pair, :, 0:128] = t_high
            gt[b, pair, :, 128:256] = t_low
        return carry

    lax.fori_loop(0, 8, setup, 0)

    ddst[...] = jnp.zeros(ddst.shape, F32)
    dsrc[...] = jnp.zeros(dsrc.shape, F32)
    dh[...] = jnp.zeros(dh.shape, F32)
    dh[spot[0]] = self_ref[...]
    high, reach = peaks(b_ref)
    close = reach < SPAN
    pltpu.make_async_copy(masks, mask_ref, sems.at[8]).wait()
    pltpu.make_async_copy(group.at[:, pl.ds(128, 8), pl.ds(128, 128)], a_ref, sems.at[9]).wait()

    def put(kind, b, h, tile):
        (abc, top)[kind][b * 8 + h] = tile

    def accumulate(weight):
        def slot(k, keep):
            b, c = blocks[2 * k], blocks[2 * k + 1]
            for pair in range(4):
                g_high, h_high = gn[b, pair, :, 0:128], hb[c, pair, 0:128]
                d_alpha = dot(
                    jnp.concatenate([g_high, g_high, gn[b, pair, :, 128:384]], axis=1),
                    jnp.concatenate([h_high, hb[c, pair, 128:256], h_high, minus[...]], axis=1),
                    NT,
                )
                highs, lows = [], []
                for side in range(2):
                    h = 2 * pair + side
                    w, positive = weight(b, c, h, keep)
                    d_raw = w * d_alpha[128 * side : 128 * side + 128]
                    d_raw = jnp.where(positive, d_raw, 0.2 * d_raw)
                    ddst[b * 8 + h] += d_raw
                    dsrc[c * 8 + h] += jnp.sum(d_raw.reshape(16, 8, 128), axis=0)
                    w_high, w_low = split(w)
                    highs.append(w_high)
                    lows.append(w_low)
                w_high, w_low = jnp.concatenate(highs, axis=1), jnp.concatenate(lows, axis=1)
                both = dot(
                    jnp.concatenate([gt[b, pair], gt[b, pair, :, 0:128]], axis=1),
                    jnp.concatenate([w_high, w_high, w_low], axis=0),
                )
                dh[c, 128 * pair : 128 * pair + 64] += both[0:64, 0:128]
                dh[c, 128 * pair + 64 : 128 * pair + 128] += both[64:128, 128:256]

        def step(two, carry):
            slot(2 * two, mask_ref[2 * two] > 0)
            slot(2 * two + 1, mask_ref[2 * two + 1] * jnp.where(2 * two + 1 < counts[0], 1, 0) > 0)
            return carry

        lax.fori_loop(0, (counts[0] + 1) // 2, step, 0)

    @pl.when(close)
    def _():
        source_factors(b_ref, high, factors)
        spread_rows(lambda b: target_factors(a_ref[b], high, pay_ref[b, 128:136, 0:128]), put)
        features.wait()

        def weight(b, c, h, keep):
            one = abc[b * 8 + h] * factors[c, pl.ds(h, 1)]
            two = top[b * 8 + h] * factors[c, pl.ds(8 + h, 1)]
            return jnp.where(keep, jnp.maximum(one, two), 0.0), one > two

        accumulate(weight)

    @pl.when(jnp.logical_not(close))
    def _():
        spread_rows(lambda b: [a_ref[b], pay_ref[b, 128:136, 0:128]], put)
        features.wait()

        def weight(b, c, h, keep):
            raw = abc[b * 8 + h] + jnp.where(keep, b_ref[c, pl.ds(h, 1)], NEG)
            return jnp.exp2(leaky(raw) - top[b * 8 + h]), raw > 0

        accumulate(weight)

    for i in range(8):
        arrive(i).wait()

    def group_half(b, side):
        part = group.at[b, pl.ds(0, 128), pl.ds(128 * side, 128)]
        return pltpu.make_async_copy(part, abc.at[2 * b + side], group_sems.at[2 * b + side])

    for b in range(8):
        for side in range(2):
            group_half(b, side).start()

    def pack_dst(b, carry):
        ddst_out[b] = jnp.concatenate(
            [jnp.sum(ddst[b * 8 + h].T, axis=0, keepdims=True) for h in range(8)], axis=0
        )
        return carry

    lax.fori_loop(0, 8, pack_dst, 0)
    ddst_out[spot[1]] += dself_ref[...]

    high, low = split(p_ref[...])
    p_wide[:, 0:512] = high
    p_wide[:, 512:1024] = low
    p_wide[:, 1024:1536] = high
    att_cols = columns_of(jnp.concatenate([att_ref[...], jnp.zeros((8, 64), F32)], axis=1))
    for h in range(8):
        att_wide[64 * h : 64 * h + 64] = jnp.broadcast_to(att_cols[0:64, h : h + 1], (64, 128))
    dp_out[...] = jnp.zeros(dp_out.shape, F32)
    own = spot[0]

    def leave(four, slot):
        return pltpu.make_async_copy(dx_slots.at[slot], dx_out.at[pl.ds(4 * four, 4)], dx_sems.at[slot])

    def project(four, carry):
        wide_dh, wide_src = [], []
        for s in range(4):
            c = 4 * four + s
            d_src = jnp.concatenate(
                [jnp.sum(dsrc[c * 8 + h], axis=0, keepdims=True) for h in range(8)], axis=0
            )
            d_src = d_src + jnp.where(c == own, dself_ref[...], 0.0)
            spread = jnp.concatenate(
                [att_wide[64 * h : 64 * h + 64] * d_src[h : h + 1] for h in range(8)], axis=0
            )
            wide_dh.append(dh[c] + spread)
            wide_src.append(jnp.concatenate([d_src, jnp.zeros((8, 128), F32)], axis=0))
        high, low = split(jnp.concatenate(wide_dh, axis=1))
        s_high, s_low = split(jnp.concatenate(wide_src, axis=1))
        x_high, x_low = split(jnp.concatenate([x_ref[4 * four + s, 0:128] for s in range(4)], axis=0))
        dx = dot(p_wide[...], jnp.concatenate([high, high, low], axis=0))
        slot = lax.rem(four, 2)

        @pl.when(four >= 2)
        def _():
            leave(four - 2, slot).wait()

        for s in range(4):
            dx_slots[slot, s] = dx[:, 128 * s : 128 * s + 128]
        leave(four, slot).start()
        tall_high = jnp.concatenate([high, s_high], axis=0)
        tall_low = jnp.concatenate([low, s_low], axis=0)
        dp_out[...] += dot(
            jnp.concatenate([tall_high, tall_high, tall_low], axis=1),
            jnp.concatenate([x_high, x_low, x_high], axis=0),
        )
        return carry

    lax.fori_loop(0, 8, project, 0)
    u = jnp.zeros((8, 256), F32)
    for b in range(8):
        for side in range(2):
            group_half(b, side).wait()
        u += dot(ddst_out[b], jnp.concatenate([abc[2 * b], abc[2 * b + 1]], axis=1), NN, lax.Precision.HIGH)
    for i in range(32):
        w_out[i, 0:16] = dp_out[16 * i : 16 * i + 16, 0:128]
        w_out[i, 16:32] = dp_out[16 * i : 16 * i + 16, 128:256]
        w_out[i, 32:40] = jnp.zeros((8, 128), F32)
    for h in range(8):
        for side in range(2):
            span = slice(128 * side, 128 * side + 128)
            w_out[h + 16 * side, 32:33] = u[h : h + 1, span]
            w_out[8 + h + 16 * side, 32:33] = dp_out[512 + h : 513 + h, span]
    leave(6, 0).wait()
    leave(7, 1).wait()


def backward_local(blocks, counts, spot, panel, proj, att_src, group, masks, pays, dh_self, d_self, hb, b):
    return pl.pallas_call(
        backward_body,
        out_shape=(
            jax.ShapeDtypeStruct((32, 256, 128), F32),
            jax.ShapeDtypeStruct((32, 40, 128), F32),
            jax.ShapeDtypeStruct((8, 8, 128), F32),
        ),
        in_specs=[SMEM] * 3 + [ANY, VMEM, VMEM, ANY, ANY, VMEM, VMEM, VMEM, ANY, VMEM],
        out_specs=(ANY, VMEM, VMEM),
        scratch_shapes=[
            pltpu.VMEM((32, 4, 256, 128), BF16),
            pltpu.VMEM((8, 4, 256, 384), BF16),
            pltpu.VMEM((8, 4, 128, 256), BF16),
            pltpu.VMEM((64, 128, 128), F32),
            pltpu.VMEM((64, 128, 128), F32),
            pltpu.VMEM((128, 128), BF16),
            pltpu.VMEM((64, 128, 128), F32),
            pltpu.VMEM((256, 8, 128), F32),
            pltpu.VMEM((32, 512, 128), F32),
            pltpu.VMEM((256, 1536), BF16),
            pltpu.VMEM((512, 128), F32),
            pltpu.VMEM((2, 4, 256, 128), F32),
            pltpu.SemaphoreType.DMA((2,)),
            pltpu.VMEM((528, 256), F32),
            pltpu.SemaphoreType.DMA((16,)),
            pltpu.SemaphoreType.DMA,
            pltpu.VMEM((32, 16, 128), F32),
            pltpu.VMEM((8, 8, 128), F32),
            pltpu.VMEM((32, 136, 256), F32),
            pltpu.VMEM((32, 128, 128), jnp.int32),
            pltpu.SemaphoreType.DMA((10,)),
        ],
        compiler_params=pltpu.CompilerParams(vmem_limit_bytes=BIG_VMEM),
    )(blocks, counts, spot, panel, proj, att_src, group, masks, pays, dh_self, d_self, hb, b)


def reduce_body(
    dx_ref, w_ref, ddst_ref, dx_out, dp_out, dst_out,
    send, recv, twin_dx, twin_w, total, far, near, far2, near2, dst_all, merged, plane, joined, tower,
):
    d, y, x, k, z = place()
    sibling = node(y, x, 1 - k)
    chip = y * 4 + x
    offsets = [(dy, dx) for dy in range(4) for dx in range(4) if (dy, dx) != (0, 0)]
    others = [lax.rem(z + s, 8) for s in range(1, 8)]
    wait_all = greet([sibling] + [node(y + dy, x + dx, k) for dy, dx in offsets], others)
    links = Links(send, recv)
    wait_all()

    def rank(offset):
        return 0 if 2 in offset else (2 if offset == (0, 0) else 1)

    cells = sorted([(0, 0)] + offsets, key=rank)
    twin_weights = links.push(w_ref.at[:, 1 - k], twin_w, dst=sibling)
    twin_copies = {}
    for dy, dx in cells:
        yy, xx = lax.rem(y + dy, 4), lax.rem(x + dx, 4)
        twin_copies[dy, dx] = links.push(dx_ref.at[yy, xx, 1 - k], twin_dx.at[yy, xx], dst=sibling)
    twin_weights.wait_recv()
    merged[...] = w_ref[:, k] + twin_w[...]
    plane_copies = []
    for dy, dx in offsets:
        target = lax.rem(y + dy, 4) * 4 + lax.rem(x + dx, 4)
        plane_copies.append(links.push(merged.at[target], plane.at[chip], dst=node(y + dy, x + dx, k)))
    dst_copies = [links.push(ddst_ref.at[t], dst_all.at[z], src=t) for t in others]

    def add_cells(wanted):
        for dy, dx in cells:
            if rank((dy, dx)) == wanted:
                yy, xx = lax.rem(y + dy, 4), lax.rem(x + dx, 4)
                twin_copies[dy, dx].wait_recv()
                total[yy, xx] = dx_ref[yy, xx, k] + twin_dx[yy, xx]

    def ring(region, plus, minus, far_buf, near_buf):
        c0 = links.push(region(2, 0), far_buf.at[0], dst=plus)
        c1 = links.push(region(2, 1), far_buf.at[1], dst=minus)
        yield
        c2 = links.push(region(1, 1), near_buf.at[0], dst=plus)
        c3 = links.push(region(-1, 0), near_buf.at[1], dst=minus)
        yield
        c0.wait_recv()
        part = region(1, 0)
        part[...] += far_buf[0]
        c4 = links.push(part, near_buf.at[2], dst=plus)
        yield
        c1.wait_recv()
        part = region(-1, 1)
        part[...] += far_buf[1]
        c5 = links.push(part, near_buf.at[3], dst=minus)
        for copy, index, piece in ((c2, 0, 1), (c3, 1, 0), (c4, 2, 0), (c5, 3, 1)):
            yield
            copy.wait_recv()
            part = region(0, piece)
            part[...] += near_buf[index]

    def grads(half):
        rows = pl.ds(128 * half, 128)

        def wide(v, piece):
            if half == 0:
                return total.at[lax.rem(y + v + 4, 4), pl.ds(2 * piece, 2), rows]
            return total.at[pl.ds(2 * piece, 2), lax.rem(x + v + 4, 4), rows]

        def narrow(u, piece):
            span = pl.ds(128 * half + 64 * piece, 64)
            if half == 0:
                return total.at[y, lax.rem(x + u + 4, 4), span]
            return total.at[lax.rem(y + u + 4, 4), x, span]

        along_y = (node(y + 1, x, k), node(y - 1, x, k))
        along_x = (node(y, x + 1, k), node(y, x - 1, k))
        first, then = (along_y, along_x) if half == 0 else (along_x, along_y)
        yield from ring(wide, *first, far.at[half], near.at[half])
        yield from ring(narrow, *then, far2.at[half], near2.at[half])

    chains = [grads(0), grads(1)]

    def advance(count):
        for _ in range(count):
            for chain in chains:
                next(chain)

    add_cells(0)
    advance(1)
    add_cells(1)
    advance(1)
    add_cells(2)
    plane[chip] = merged[chip]
    for copy in plane_copies:
        copy.wait_recv()
    value = plane[0]
    for i in range(1, 16):
        value = value + plane[i]
    joined[...] = value
    tower[z] = value
    tower_copies = [links.push(joined, tower.at[z], src=t) for t in others]
    advance(2)
    for copy in tower_copies:
        copy.wait_recv()
    value = tower[0]
    for i in range(1, 8):
        value = value + tower[i]
    dp_out[chip, k] = value
    spread_copies = [
        links.push(dp_out.at[chip, k], dp_out.at[chip, k], dst=node(y + dy, x + dx, k)) for dy, dx in offsets
    ]
    advance(7)
    for copy in spread_copies:
        copy.wait_recv()
    over = links.push(dp_out.at[:, k], dp_out.at[:, k], dst=sibling)
    run_chains(chains)
    dx_out[...] = total[y, x]
    for copy in dst_copies:
        copy.wait_recv()
    dst_all[z] = ddst_ref[z]
    dst_total = dst_all[0]
    for t in range(1, 8):
        dst_total = dst_total + dst_all[t]
    dst_out[...] = dst_total
    over.wait_recv()
    links.drain()


def reduce_grads(dx, w, ddst):
    count = 1 + 16 + 15 + 7 + 24 + 7 + 15 + 1
    return pl.pallas_call(
        reduce_body,
        out_shape=(
            jax.ShapeDtypeStruct((256, 128), F32),
            jax.ShapeDtypeStruct((16, 2, 40, 128), F32),
            jax.ShapeDtypeStruct((8, 128), F32),
        ),
        in_specs=[VMEM] * 3,
        out_specs=(VMEM,) * 3,
        scratch_shapes=[
            pltpu.SemaphoreType.DMA((count,)),
            pltpu.SemaphoreType.DMA((count,)),
            pltpu.VMEM((4, 4, 256, 128), F32),
            pltpu.VMEM((16, 40, 128), F32),
            pltpu.VMEM((4, 4, 256, 128), F32),
            pltpu.VMEM((2, 2, 2, 128, 128), F32),
            pltpu.VMEM((2, 4, 2, 128, 128), F32),
            pltpu.VMEM((2, 2, 64, 128), F32),
            pltpu.VMEM((2, 4, 64, 128), F32),
            pltpu.VMEM((8, 8, 128), F32),
            pltpu.VMEM((16, 40, 128), F32),
            pltpu.VMEM((16, 40, 128), F32),
            pltpu.VMEM((40, 128), F32),
            pltpu.VMEM((8, 40, 128), F32),
        ],
        compiler_params=pltpu.CompilerParams(
            collective_id=2, has_side_effects=True, vmem_limit_bytes=BIG_VMEM
        ),
    )(dx.reshape(4, 4, 2, 256, 128), w.reshape(16, 2, 40, 128), ddst)


def finish_body(dx_ref, w_ref, dst_ref, p_ref, dst_att_ref, in_ref, proj_ref, src_ref, dst_out):
    proj = p_ref[...]
    a_rows = per_head_rows(dst_att_ref[...])
    score = dot(a_rows, proj, NT, HIGHEST)
    pad = jnp.zeros((120, 256), F32)
    score_t = jnp.concatenate([score, pad], axis=0).T
    dst_wide = jnp.concatenate([dst_ref[...], jnp.zeros((120, 128), F32)], axis=0)
    in_ref[...] = (dx_ref[...] + dot(score_t, dst_wide, NN, lax.Precision.HIGH)).T

    def row(i):
        return jnp.concatenate([w_ref[i, 32:33], w_ref[i + 16, 32:33]], axis=1)

    u = jnp.concatenate([row(h) for h in range(8)], axis=0)
    v = jnp.concatenate([row(8 + h) for h in range(8)], axis=0)
    wide_u = jnp.concatenate([u, jnp.zeros((120, 256), F32)], axis=0)
    att = jnp.concatenate([a_rows, jnp.zeros((120, 512), F32)], axis=0)
    grad_t = jnp.concatenate(
        [jnp.concatenate([w_ref[i, 0:16], w_ref[i, 16:32]], axis=1) for i in range(32)], axis=0
    )
    proj_ref[...] = (grad_t + dot(att.T, wide_u, NN, lax.Precision.HIGH)).T
    both = dot(jnp.concatenate([u, v], axis=0), proj, NN, lax.Precision.HIGH)
    dst_out[...] = jnp.concatenate([both[h : h + 1, 64 * h : 64 * h + 64] for h in range(8)], axis=0)
    src_ref[...] = jnp.concatenate([both[8 + h : 9 + h, 64 * h : 64 * h + 64] for h in range(8)], axis=0)


def finish(dx, weights, dst_total, proj, att_dst):
    return pl.pallas_call(
        finish_body,
        out_shape=(
            jax.ShapeDtypeStruct((128, 256), F32),
            jax.ShapeDtypeStruct((256, 512), F32),
            jax.ShapeDtypeStruct((8, 64), F32),
            jax.ShapeDtypeStruct((8, 64), F32),
        ),
        in_specs=[VMEM] * 5,
        out_specs=(VMEM,) * 4,
    )(dx, weights.reshape(32, 40, 128), dst_total, proj, att_dst)


def shards(inputs, projection, att_src, att_dst, blocks, counts, tile_masks, cotangent):
    coords = blocks.reshape(64)
    live = counts.reshape(1)
    masks = tile_masks[0, 0]
    spot = jnp.stack([lax.axis_index("dst"), lax.axis_index("src")]).astype(jnp.int32)
    panel, group, own = gather_inputs(inputs, projection, att_src, att_dst)
    acc, hb, b = forward_local(coords, live, panel, projection, group, masks)
    output, pays, dh_self, d_self = exchange(acc, inputs, projection, own, cotangent)
    dx, w, ddst = backward_local(
        coords, live, spot, panel, projection, att_src, group, masks, pays, dh_self, d_self, hb, b
    )
    dx_own, weights, dst_total = reduce_grads(dx, w, ddst)
    in_grad, proj_grad, src_grad, dst_grad = finish(dx_own, weights, dst_total, projection, att_dst)
    return (output, in_grad, proj_grad, src_grad, dst_grad)


def solution(mesh):
    in_specs = (
        P(("dst", "src"), None),
        P(),
        P(),
        P(),
        P("dst", "src", None, None),
        P("dst", "src"),
        P("dst", "src", None, None, None),
        P(("dst", "src"), None),
    )
    out_specs = (P(("dst", "src"), None), P(("dst", "src"), None), P(), P(), P())
    return jax.shard_map(shards, mesh=mesh, in_specs=in_specs, out_specs=out_specs, check_vma=False)
```
